128 devices in a mesh: cplx: 4 (over y), frag: 32 (over z, x, core).
Axes of the slice: x: 4, y: 4, z: 4, core: 2. Of those that a mesh axis runs over, the one named last changes fastest.
Arguments:
- coeffs: float32 [2048, 256], P(('cplx', 'frag')), parts along dimension 0, may hold values from -0.3 to 0.3
- centres: float32 [2048, 4, 256], P(('cplx', 'frag')), parts along dimension 0, may hold values from -3 to 3, as said below
- frag_sizes: int32 [2048], P(('cplx', 'frag')), parts along dimension 0, may hold values from 64 to 256
- pairs: int32 [131072, 2], P(('cplx', 'frag')), parts along dimension 0, may hold values from 0 to 511, as said below
Outputs:
- potential: float32 [2048, 256], P(('cplx', 'frag')), parts along dimension 0
The draws below stay inside these ranges and needn't reach their ends.
There are 4 independent parts, one for each index of `cplx`. The reference program is written for one: setup_inputs(seed, part) draws one part's arguments, and reference() takes and returns one part's arrays. A program takes and returns all parts, laid end to end along the dimension named above; each array names one. Nothing has to cross between parts.
Inputs may be any that keep to these rules, and one draw needn't show every extreme that they name: `pairs`: slots 1024 * d to 1024 * (d + 1) - 1 belong to device d of frag; their first fragment is one of fragments 16 * d to 16 * (d + 1) - 1. Slot r of that block (counted from the block's start) either has its second fragment equal to its first (an empty slot) or names a second fragment owned by device r // 32, that is one of fragments 16 * (r // 32) on. Slots toward the device itself are never empty and never name the same fragment twice. `centres`: widths are positive.
All inputs are finite; a program needn't handle non-finite values.
Results may differ from the reference program's by a relative error of at most 0.0003.
Values sent between devices are 32-bit elements; how exact they have to be, the bound alone decides.
No kernel may reach another device: no remote copies, remote signals or barrier semaphores. Data moves between devices by JAX's collectives and lax.ppermute only.
A program may use at most 128 MiB of HBM per device.

```python
import jax
import jax.numpy as jnp
from jax import lax

FRAG_DEV = 16
AUX = 256
DIM_DEV = 1024
FRAGS = 512
DIMERS = 32768
N_FRAG = 32


def draw_centres(key, part):
    key = jax.random.fold_in(key, 11)
    key_pos, key_width = jax.random.split(key)
    places = jax.random.uniform(key_pos, (FRAGS, 3, AUX), jnp.float32, -3.0, 3.0)
    logs = jax.random.uniform(key_width, (FRAGS, 1, AUX), jnp.float32, jnp.log(0.05), jnp.log(1.0))
    return jnp.concatenate([places, jnp.exp(logs)], axis=1)


def draw_frag_sizes(key, part):
    key = jax.random.fold_in(key, 12)
    key_size, key_pick = jax.random.split(key)
    sizes = jax.random.randint(key_size, (FRAGS,), AUX // 4, AUX + 1)
    pick = jax.random.randint(key_pick, (), 0, FRAGS)
    return jnp.where(jnp.arange(FRAGS) == pick, AUX, sizes).astype(jnp.int32)


def draw_pairs(key, part):
    key = jax.random.fold_in(key, 13)
    key_live, key_first, key_other, key_self = jax.random.split(key, 4)
    slots = jnp.arange(DIMERS, dtype=jnp.int32)
    device = slots // DIM_DEV
    peer = slots % DIM_DEV // (DIM_DEV // N_FRAG)
    apart = jnp.abs(device - peer)
    apart = jnp.minimum(apart, N_FRAG - apart)
    chance = jnp.where(apart == 0, 100, jnp.maximum(20, 100 - 160 * apart // N_FRAG))
    live = jax.random.randint(key_live, (DIMERS,), 0, 100) < chance
    first_local = jax.random.randint(key_first, (DIMERS,), 0, FRAG_DEV)
    first = device * FRAG_DEV + first_local
    other = peer * FRAG_DEV + jax.random.randint(key_other, (DIMERS,), 0, FRAG_DEV)
    step_self = 1 + jax.random.randint(key_self, (DIMERS,), 0, FRAG_DEV - 1)
    same = device * FRAG_DEV + (first_local + step_self) % FRAG_DEV
    second = jnp.where(apart == 0, same, other)
    second = jnp.where(live, second, first)
    return jnp.stack([first, second], axis=1).astype(jnp.int32)


def levels(stream_key, extent, pieces, low, largest):
    factor_of, own = 1.0, jax.random.fold_in(stream_key, 6)
    for axis_at, shards_of in pieces:
        draws = jnp.exp(jax.random.uniform(jax.random.fold_in(own, axis_at), (shards_of,), jnp.float32, low / len(pieces), largest / len(pieces)))
        factor_of = factor_of * jnp.repeat(draws, extent[axis_at] // shards_of).reshape([-1 if axis == axis_at else 1 for axis in range(len(extent))])
    return factor_of


def bell_draw(key, extent, scale, bound, shards=(), kind=jnp.bfloat16):
    result = scale * jax.random.normal(key, extent, jnp.float32)
    if shards:
        result = result * levels(key, extent, shards, -0.22, 0.18)
    return jnp.clip(result, -bound, bound).astype(kind)


def setup_inputs(seed: int = 0, part: int = 0) -> dict:
    key_of = jax.random.split(jax.random.key(seed), 5)
    part_splits = jax.random.split(jax.random.fold_in(key_of[4], part), 5)
    return {
        "coeffs": bell_draw(part_splits[0], (FRAGS, AUX), 0.05, 0.3, ((0, 32),), jnp.float32),
        "centres": draw_centres(jax.random.fold_in(jax.random.fold_in(key_of[4], part), 71), part),
        "frag_sizes": draw_frag_sizes(jax.random.fold_in(jax.random.fold_in(key_of[4], part), 71), part),
        "pairs": draw_pairs(jax.random.fold_in(jax.random.fold_in(key_of[4], part), 71), part),
    }


def pair_terms(mine, partner):
    delta = (mine[:, 1, :, None] - partner[:, 1, None, :]) ** 2
    delta = delta + (mine[:, 2, :, None] - partner[:, 2, None, :]) ** 2
    delta = delta + (mine[:, 3, :, None] - partner[:, 3, None, :]) ** 2
    kernel = lax.rsqrt(delta + mine[:, 4, :, None] + partner[:, 4, None, :])
    to_first = jnp.einsum('rab,rb->ra', kernel, partner[:, 0], precision=lax.Precision.HIGHEST)
    to_second = jnp.einsum('rab,ra->rb', kernel, mine[:, 0], precision=lax.Precision.HIGHEST)
    return (to_first, to_second)

def reference(coeffs, centres, frag_sizes, pairs):
    mask = (jnp.arange(AUX, dtype=jnp.int32)[None, :] < frag_sizes[:, None]).astype(jnp.float32)
    packed = jnp.concatenate([(coeffs * mask)[:, None, :], centres], axis=1)
    blocks = pairs.reshape(-1, 16, 2)

    def step(total, rows):
        first = rows[:, 0]
        second = rows[:, 1]
        live = (first != second).astype(jnp.float32)[:, None]
        to_first, to_second = pair_terms(packed[first], packed[second])
        total = total.at[first].add(to_first * live)
        total = total.at[second].add(to_second * live)
        return (total, None)
    total, unused = lax.scan(step, jnp.zeros((FRAGS, AUX), jnp.float32), blocks)
    return total * mask
```

```python
import functools

import jax
import jax.numpy as jnp
from jax import lax
from jax.experimental import pallas as pl
from jax.experimental.pallas import tpu as pltpu
from jax.sharding import PartitionSpec as P

FRAG_DEV = 16
AUX = 256
ROWS = 96
NF = 64
NG = 128
CHUNK = 32
CPF = AUX // CHUNK
PER_TILE = 8
DUMMY = NF * AUX
DEPTH = 48
UNROLL = 8
WIDTH_FLOOR = 1.0 / 32.0


def pieces(value):
    first = value.astype(jnp.bfloat16).astype(jnp.float32)
    rest = value - first
    second = rest.astype(jnp.bfloat16).astype(jnp.float32)
    return first, second, rest - second


def pair_kernel(meta, *refs):
    packets = refs[:11]
    out_sib, out_far, out_near, out_own, outf_far, outf_near, outf_own = refs[11:18]
    (lhs, cfb, acc, acc_left, acc_right, rhs, cg, build, slots, counts, chunks, at_v, at_f, table_v, table, sem) = refs[18:]
    f_blocks = [packets[0], packets[1], packets[2], packets[3]]
    g_blocks = [packets[0]] + list(packets[4:])
    plane = meta[0]
    column = meta[1]

    def put_rows(r, value):
        for h in range(2):
            build[h, pl.ds(r * 16, 16), :] = value[:, 128 * h:128 * h + 128]

    def take_rows(h, at, count):
        return build.at[h][pl.ds(at, count, stride=16), :]

    lowest = None
    for i, blk in enumerate(f_blocks):
        x, y, z, w, c = (blk[pl.ds(16 * k, 16), :] for k in range(5))
        lowest = w if lowest is None else jnp.minimum(lowest, w)
        s = x * x + y * y + z * z + w
        one = jnp.ones_like(x)
        zero = jnp.zeros_like(x)
        px, py, pz = pieces(-2.0 * x), pieces(-2.0 * y), pieces(-2.0 * z)
        ps, pw, pc = pieces(s), pieces(w), pieces(c)
        for k in range(3):
            delta = one if k == 0 else zero
            extra = pc if k == 0 else (pw if k == 1 else (zero, zero, zero))
            rows = [px[k], py[k], pz[k], delta, ps[k], *extra,
                    px[k], py[k], pz[k], delta, px[k], py[k], pz[k], delta]
            for r, value in enumerate(rows):
                put_rows(16 * k + r, value)

        def one_row(lf, _, i=i):
            for h in range(2):
                start = pl.multiple_of((i * 16 + lf) * AUX + 128 * h, 128)
                lhs[pl.ds(start, 128), :] = take_rows(h, lf, DEPTH).T.astype(jnp.bfloat16)
            return 0

        lax.fori_loop(0, 16, one_row, 0, unroll=4)
    spare_lane = lax.broadcasted_iota(jnp.int32, (CHUNK, DEPTH), 1)
    lhs[pl.ds(DUMMY, CHUNK), :] = (spare_lane == 4).astype(jnp.float32).astype(jnp.bfloat16)

    pick = lax.broadcasted_iota(jnp.int32, (DEPTH, 128), 0)

    def spread(rows, lo, scale):
        sel = jnp.where((pick % 16 >= lo[0]) & (pick % 16 <= lo[1]) & (pick // 16 >= lo[2]) & (pick // 16 <= lo[3]), scale, 0.0)
        return jnp.dot(rows, sel.astype(jnp.bfloat16), preferred_element_type=jnp.float32)

    def one_spread(f, _):
        start = pl.multiple_of(f * AUX, AUX)
        cfb[pl.ds(start, AUX), :] = spread(lhs[pl.ds(start, AUX), :], (5, 7, 0, 0), 1.0)
        acc[pl.ds(start, AUX), :] = jnp.zeros((AUX, 128), jnp.float32)
        return 0

    lax.fori_loop(0, NF, one_spread, 0, unroll=4)
    cfb[pl.ds(DUMMY, CHUNK), :] = jnp.zeros((CHUNK, 128), jnp.float32)
    acc[pl.ds(DUMMY, CHUNK), :] = jnp.zeros((CHUNK, 128), jnp.float32)
    acc_left[...] = jnp.zeros_like(acc_left)
    acc_right[...] = jnp.zeros_like(acc_right)

    for j, blk in enumerate(g_blocks):
        x, y, z, w, c = (blk[pl.ds(16 * k, 16), :] for k in range(5))
        lowest = jnp.minimum(lowest, w)
        s = x * x + y * y + z * z + w
        one = jnp.ones_like(x)
        zero = jnp.zeros_like(x)
        px, py, pz, ps = pieces(x), pieces(y), pieces(z), pieces(s)
        rows = [px[0], py[0], pz[0], ps[0], one, zero, zero, zero,
                px[1], py[1], pz[1], ps[1], px[2], py[2], pz[2], ps[2]]
        for r, value in enumerate(rows):
            put_rows(r, value)
        cg[pl.ds(j * 16, 16), :] = c

        def one_column(lg, _, j=j):
            start = pl.multiple_of((j * 16 + lg) * 16, 16)
            rhs[pl.ds(start, 16), :] = jnp.concatenate([take_rows(h, lg, 16) for h in range(2)], axis=1).astype(jnp.bfloat16)
            return 0

        lax.fori_loop(0, 16, one_column, 0, unroll=8)

    lane = lax.broadcasted_iota(jnp.int32, (8, AUX), 1)
    back = jnp.zeros((8, AUX), jnp.float32)
    for j, blk in enumerate(g_blocks):
        shift = lax.rem(32 * j - 32 * column + 256, 256)
        turned = pltpu.roll(blk[pl.ds(80, 8), :], shift, 1)
        back = jnp.where(lane // 32 == j, turned, back)
    slots[...] = back
    g_lane = lax.broadcasted_iota(jnp.int32, (16, AUX), 0).astype(jnp.float32)
    g_ids = jnp.concatenate([g_lane + (16 * meta[8 + j]).astype(jnp.float32) for j in range(8)], axis=0)
    for i, blk in enumerate(f_blocks):
        f_ids = g_lane + (16 * meta[4 + i]).astype(jnp.float32)
        f_plane = meta[16 + i]

        def table_of(row_f, row_g):
            odd = (row_f + row_g) - 2.0 * jnp.floor((row_f + row_g) * 0.5)
            less = (row_f < row_g).astype(jnp.float32)
            use = (odd == less) & (row_f != row_g)
            row_f = jnp.where(use, row_f, -1.0)
            left = (row_f == f_ids).astype(jnp.float32).astype(jnp.bfloat16)
            right = (row_g == g_ids).astype(jnp.float32).astype(jnp.bfloat16)
            return lax.dot_general(left, right, (((1,), (1,)), ((), ())), preferred_element_type=jnp.float32)

        there = table_of(blk[pl.ds(80 + plane, 1), :], blk[pl.ds(84 + plane, 1), :])
        back_i = table_of(slots[pl.ds(4 + f_plane, 1), :], slots[pl.ds(f_plane, 1), :])
        counts[pl.ds(16 * i, 16), :] = there + back_i
        sizes = blk[pl.ds(88, 1), :]
        eye = lax.broadcasted_iota(jnp.int32, (16, AUX), 0) == lax.broadcasted_iota(jnp.int32, (16, AUX), 1)
        size_col = jnp.sum(jnp.where(eye, sizes, 0.0), axis=1, keepdims=True)
        many = jnp.floor((size_col + (CHUNK - 1)) * (1.0 / CHUNK))
        chunks[pl.ds(16 * i, 16), :] = jnp.broadcast_to(many, (16, 128))

    need = jnp.sum(counts[...] * chunks[...], axis=0, keepdims=True)
    rounds = ((jnp.max(need) + 127.0) * (1.0 / 128.0)).astype(jnp.int32)
    safe = jnp.min(lowest) >= WIDTH_FLOOR
    ones16 = lax.broadcasted_iota(jnp.int32, (128, 128), 0).astype(jnp.float32)

    def step(g, p, exact):
        entries = [pl.multiple_of(table[p + u, g], CHUNK) for u in range(PER_TILE)]
        block = rhs[pl.ds(pl.multiple_of(g * 16, 16), 16), :]
        left = jnp.concatenate([lhs[pl.ds(e, CHUNK), :] for e in entries], axis=0)
        if exact:
            at = pl.multiple_of(g * 16, 16)
            part = block.astype(jnp.float32)
            own = [part[k:k + 1] + part[8 + k:9 + k] + part[12 + k:13 + k] for k in range(3)]
            dist = None
            for k in range(3):
                mine = sum(jnp.dot(left, jnp.where((pick % 16 == k) & (pick // 16 < 3), -0.5, 0.0).astype(jnp.bfloat16), preferred_element_type=jnp.float32) for _ in range(1))
                mine = jnp.concatenate([mine, mine], axis=1)
                gap = mine - own[k]
                dist = gap * gap if dist is None else dist + gap * gap
            wide = spread(left, (5, 7, 1, 1), 1.0)
            dist = dist + jnp.concatenate([wide, wide], axis=1)
            dist = dist + wg_row(g)
            kern = lax.rsqrt(dist)
        else:
            right = jnp.concatenate([block, block, block], axis=0)
            kern = lax.rsqrt(jnp.dot(left, right, preferred_element_type=jnp.float32))
        k0, k1 = kern[:, :128], kern[:, 128:]
        weight = cg[pl.ds(g, 1), :]
        first = k0 * weight[:, :128] + k1 * weight[:, 128:]
        rows_c = jnp.concatenate([cfb[pl.ds(e, CHUNK), :] for e in entries], axis=0)
        sec0 = jnp.sum((k0 * rows_c).reshape(-1, 8, 128), axis=0)
        sec1 = jnp.sum((k1 * rows_c).reshape(-1, 8, 128), axis=0)
        base = pl.multiple_of(g * 8, 8)
        acc_left[pl.ds(base, 8), :] = acc_left[pl.ds(base, 8), :] + sec0
        acc_right[pl.ds(base, 8), :] = acc_right[pl.ds(base, 8), :] + sec1
        for u, e in enumerate(entries):
            acc[pl.ds(e, CHUNK), :] = acc[pl.ds(e, CHUNK), :] + first[u * CHUNK:(u + 1) * CHUNK]
        more = p + PER_TILE < table[136, g]
        g_next = jnp.where(more, g, g + 1)
        p_next = jnp.where(more, p + PER_TILE, 0)
        over = g_next > NG - 1
        return jnp.minimum(g_next, NG - 1), jnp.where(over, 128, p_next)

    def wg_row(g):
        j = g // 16
        lg = g % 16
        row = jnp.zeros((1, AUX), jnp.float32)
        for k, blk in enumerate(g_blocks):
            row = jnp.where(j == k, blk[pl.ds(48 + lg, 1), :], row)
        return row

    def one_round(r, _):
        at_v[...] = ones16 + (128 * r).astype(jnp.float32)
        at = at_v[...]

        def scan(f, state):
            code, begin, total = state
            many = chunks[pl.ds(f, 1), :]
            hit = at >= total
            code = jnp.where(hit, f.astype(jnp.float32) * 16.0 + many, code)
            begin = jnp.where(hit, total, begin)
            return code, begin, total + counts[pl.ds(f, 1), :] * many

        at_f[...] = jnp.zeros((128, 128), jnp.float32)
        flat = at_f[...]
        code, begin, total = lax.fori_loop(0, NF, scan, (flat, flat, flat[0:1]), unroll=4)
        frag = jnp.floor(code * (1.0 / 16.0))
        many = code - 16.0 * frag
        offset = at - begin
        offset = offset - many * jnp.floor((offset + 0.5) / many)
        entry = (frag * CPF + offset) * CHUNK
        entry = jnp.where(at < total, entry, float(DUMMY))
        table_v[pl.ds(0, 128), :] = entry.astype(jnp.int32)
        table_v[pl.ds(128, 8), :] = jnp.full((8, 128), DUMMY, jnp.int32)
        left_over = jnp.clip(total - (128 * r).astype(jnp.float32), 0.0, 128.0)
        tiles = jnp.maximum(jnp.floor((left_over + (PER_TILE - 1)) * (1.0 / PER_TILE)), 1.0)
        tile_sum = jnp.sum(tiles, axis=1, keepdims=True)
        row8 = lax.broadcasted_iota(jnp.int32, (8, 128), 0)
        table_v[pl.ds(136, 8), :] = jnp.where(row8 == 0, left_over, tile_sum).astype(jnp.int32)
        copy = pltpu.make_async_copy(table_v, table, sem)
        copy.start()
        copy.wait()
        total_tiles = table[137, 0]

        def many_tiles(exact, width):
            def body(_, state):
                for _u in range(width):
                    state = step(*state, exact)
                return state

            lax.fori_loop(0, (total_tiles + (width - 1)) // width, body, (jnp.int32(0), jnp.int32(0)))

        @pl.when(safe)
        def _():
            many_tiles(False, UNROLL)

        @pl.when(jnp.logical_not(safe))
        def _():
            many_tiles(True, 1)

        return 0

    lax.fori_loop(0, rounds, one_round, 0)

    lanes = lax.broadcasted_iota(jnp.int32, (AUX, 128), 1)

    def collect(f, out):
        start = pl.multiple_of(f * AUX, AUX)
        col = jnp.sum(acc[pl.ds(start, AUX), :], axis=1, keepdims=True)
        return jnp.where(lanes == f, col, out)

    rows_out = lax.fori_loop(0, NF, collect, acc[pl.ds(DUMMY - AUX, AUX), :]).T
    outf_own[...] = rows_out[0:16]
    outf_near[...] = rows_out[16:32]
    outf_far[...] = rows_out[32:64]
    cols = []
    for part in (acc_left, acc_right):
        half = part[pl.ds(0, NG, stride=8), :]
        for r in range(1, 8):
            half = half + part[pl.ds(r, NG, stride=8), :]
        cols.append(half)
    cols = jnp.concatenate(cols, axis=1)
    out_own[...] = cols[0:16]
    out_near[...] = cols[16:32]
    out_far[...] = cols[32:64]
    out_sib[...] = cols[64:128]


def rectangle(meta, packets):
    vmem = pl.BlockSpec(memory_space=pltpu.VMEM)
    shape = lambda rows: jax.ShapeDtypeStruct((rows, AUX), jnp.float32)
    return pl.pallas_call(
        pair_kernel,
        out_shape=(shape(64), shape(32), shape(16), shape(16), shape(32), shape(16), shape(16)),
        in_specs=[pl.BlockSpec(memory_space=pltpu.SMEM)] + [vmem] * 11,
        out_specs=(vmem,) * 7,
        scratch_shapes=[
            pltpu.VMEM((DUMMY + CHUNK, DEPTH), jnp.bfloat16),
            pltpu.VMEM((DUMMY + CHUNK, 128), jnp.float32),
            pltpu.VMEM((DUMMY + CHUNK, 128), jnp.float32),
            pltpu.VMEM((NG * 8, 128), jnp.float32),
            pltpu.VMEM((NG * 8, 128), jnp.float32),
            pltpu.VMEM((NG * 16, AUX), jnp.bfloat16),
            pltpu.VMEM((NG, AUX), jnp.float32),
            pltpu.VMEM((2, DEPTH * 16, 128), jnp.float32),
            pltpu.VMEM((8, AUX), jnp.float32),
            pltpu.VMEM((NF, 128), jnp.float32),
            pltpu.VMEM((NF, 128), jnp.float32),
            pltpu.VMEM((128, 128), jnp.float32),
            pltpu.VMEM((128, 128), jnp.float32),
            pltpu.VMEM((144, 128), jnp.int32),
            pltpu.SMEM((144, 128), jnp.int32),
            pltpu.SemaphoreType.DMA,
        ],
        compiler_params=pltpu.CompilerParams(vmem_limit_bytes=56 * 2**20),
    )(meta, *packets)


def index_of(z, x, c):
    return (z * 4 + x) * 2 + c


def partners(move):
    return [
        (index_of(z, x, c), index_of(*move(z, x, c)))
        for z in range(4) for x in range(4) for c in range(2)
    ]


X_NEAR = partners(lambda z, x, c: (z, x ^ 1, c))
X_FAR = partners(lambda z, x, c: (z, 3 - x, c))
Z_NEAR = partners(lambda z, x, c: (z ^ 1, x, c))
Z_FAR = partners(lambda z, x, c: (3 - z, x, c))
CORE = partners(lambda z, x, c: (z, x, c ^ 1))


def swap(array, pairs):
    return lax.ppermute(array, "frag", pairs)


def local(coeffs, centres, frag_sizes, pairs):
    me = lax.axis_index("frag")
    z, x, c = me // 8, (me // 2) % 4, me % 2
    mask = (jnp.arange(AUX, dtype=jnp.int32)[None, :] < frag_sizes[:, None]).astype(jnp.float32)
    packet = jnp.concatenate(
        [
            centres.transpose(1, 0, 2).reshape(4 * FRAG_DEV, AUX),
            coeffs * mask,
            pairs.T.reshape(8, AUX).astype(jnp.float32),
            jnp.pad(frag_sizes.astype(jnp.float32)[None, :], ((0, 7), (0, AUX - FRAG_DEV))),
        ],
        axis=0,
    )
    zs = jnp.stack([z, z ^ 1, 3 - z, (3 - z) ^ 1])
    xs = jnp.stack([x, x ^ 1, 3 - x, (3 - x) ^ 1])
    f_dev = index_of(zs, x, c)
    g_dev = jnp.concatenate([index_of(z, xs, c), index_of(z, xs, c ^ 1)])
    zero = jnp.zeros((2,), jnp.int32)
    meta = jnp.concatenate([jnp.stack([z, 2 * x + c]), zero, f_dev, g_dev, zs]).astype(jnp.int32)

    x_near = swap(packet, X_NEAR)
    z_near = swap(packet, Z_NEAR)
    x_far = swap(packet, X_FAR)
    z_far = swap(packet, Z_FAR)
    x_last = swap(x_near, X_FAR)
    z_last = swap(z_near, Z_FAR)
    own_c = swap(packet, CORE)
    near_c = swap(x_near, CORE)
    far_c = swap(x_far, CORE)
    last_c = swap(x_last, CORE)

    g_sib, g_far, g_near, g_own, f_far, f_near, f_own = rectangle(
        meta,
        (packet, z_near, z_far, z_last, x_near, x_far, x_last, own_c, near_c, far_c, last_c),
    )
    f_back = swap(f_far, Z_FAR)
    sib_back = swap(g_sib, CORE)
    far_back = swap(g_far + sib_back[32:], X_FAR)
    f_last = swap(f_near + f_back[16:], Z_NEAR)
    near_back = swap(g_near + sib_back[16:32] + far_back[16:], X_NEAR)
    total = f_own + f_back[:16] + f_last + g_own + sib_back[:16] + far_back[:16] + near_back
    return total * mask


def solution(mesh):
    return jax.shard_map(
        local,
        mesh=mesh,
        in_specs=(
            P(("cplx", "frag"), None),
            P(("cplx", "frag"), None, None),
            P(("cplx", "frag")),
            P(("cplx", "frag"), None),
        ),
        out_specs=P(("cplx", "frag"), None),
        check_vma=False,
    )
```

```python
import functools

import jax
import jax.numpy as jnp
from jax import lax
from jax.experimental import pallas as pl
from jax.experimental.pallas import tpu as pltpu
from jax.sharding import PartitionSpec as P

FRAG_DEV = 16
AUX = 256
ROWS = 96
NF = 64
NG = 128
CHUNK = 32
CPF = AUX // CHUNK
WIDE = 4
NARROW = 8
SPAN = 64
DUMMY = NF * CPF
DEPTH = 48
UNROLL = 16
WIDTH_FLOOR = 1.0 / 32.0


def pieces(value):
    first = value.astype(jnp.bfloat16).astype(jnp.float32)
    rest = value - first
    second = rest.astype(jnp.bfloat16).astype(jnp.float32)
    return first, second, rest - second


def pair_kernel(meta, *refs):
    packets = refs[:11]
    out_sib, out_far, out_near, out_own, outf_far, outf_near, outf_own = refs[11:18]
    (lhs, rows_f, acc_left, acc_right, rhs, cg, build, slots, counts, sorted_counts, chunks,
     zeros_v, places, table_v, table, sem) = refs[18:]
    f_blocks = [packets[0], packets[1], packets[2], packets[3]]
    g_blocks = [packets[0]] + list(packets[4:])
    plane = meta[0]
    column = meta[1]

    def put_rows(r, value):
        for h in range(2):
            build[h, pl.ds(r * 16, 16), :] = value[:, 128 * h:128 * h + 128]

    def take_rows(h, at, count):
        return build.at[h][pl.ds(at, count, stride=16), :]

    lowest = None
    for i, blk in enumerate(f_blocks):
        x, y, z, w, c = (blk[pl.ds(16 * k, 16), :] for k in range(5))
        lowest = w if lowest is None else jnp.minimum(lowest, w)
        s = x * x + y * y + z * z + w
        one = jnp.ones_like(x)
        zero = jnp.zeros_like(x)
        px, py, pz = pieces(-2.0 * x), pieces(-2.0 * y), pieces(-2.0 * z)
        ps, pw, pc = pieces(s), pieces(w), pieces(c)
        for k in range(3):
            delta = one if k == 0 else zero
            extra = pc if k == 0 else (pw if k == 1 else (zero, zero, zero))
            rows = [px[k], py[k], pz[k], delta, ps[k], *extra,
                    px[k], py[k], pz[k], delta, px[k], py[k], pz[k], delta]
            for r, value in enumerate(rows):
                put_rows(16 * k + r, value)

        def one_row(lf, _, i=i):
            for h in range(2):
                feats = take_rows(h, lf, DEPTH).T
                feats = jnp.concatenate([feats, jnp.zeros((128, 128 - DEPTH), jnp.float32)], axis=1)
                lhs[pl.ds((i * 16 + lf) * CPF + 4 * h, 4)] = feats.astype(jnp.bfloat16).reshape(4, CHUNK, 128)
            return 0

        lax.fori_loop(0, 16, one_row, 0, unroll=4)
    spare_lane = lax.broadcasted_iota(jnp.int32, (CHUNK, 128), 1)
    lhs[DUMMY] = (spare_lane == 4).astype(jnp.float32).astype(jnp.bfloat16)

    pick = lax.broadcasted_iota(jnp.int32, (128, 128), 0)

    def spread(rows, lo, hi, scale):
        sel = jnp.where((pick >= lo) & (pick <= hi), scale, 0.0)
        return jnp.dot(rows, sel.astype(jnp.bfloat16), preferred_element_type=jnp.float32)

    def one_spread(f, _):
        value = spread(lhs[pl.ds(f * CPF, CPF)].reshape(AUX, 128), 5, 7, 1.0)
        rows_f[pl.ds(f * CPF, CPF), 0:CHUNK, :] = value.reshape(CPF, CHUNK, 128)
        rows_f[pl.ds(f * CPF, CPF), CHUNK:2 * CHUNK, :] = jnp.zeros((CPF, CHUNK, 128), jnp.float32)
        return 0

    lax.fori_loop(0, NF, one_spread, 0, unroll=4)
    rows_f[DUMMY] = jnp.zeros((2 * CHUNK, 128), jnp.float32)
    acc_left[...] = jnp.zeros_like(acc_left)
    acc_right[...] = jnp.zeros_like(acc_right)

    for j, blk in enumerate(g_blocks):
        x, y, z, w, c = (blk[pl.ds(16 * k, 16), :] for k in range(5))
        lowest = jnp.minimum(lowest, w)
        s = x * x + y * y + z * z + w
        one = jnp.ones_like(x)
        zero = jnp.zeros_like(x)
        px, py, pz, ps = pieces(x), pieces(y), pieces(z), pieces(s)
        rows = [px[0], py[0], pz[0], ps[0], one, zero, zero, zero,
                px[1], py[1], pz[1], ps[1], px[2], py[2], pz[2], ps[2]]
        for r, value in enumerate(rows):
            put_rows(r, value)
        cg[pl.ds(j * 16, 16), :] = c

        def one_column(lg, _, j=j):
            start = pl.multiple_of((j * 16 + lg) * 16, 16)
            rhs[pl.ds(start, 16), :] = jnp.concatenate([take_rows(h, lg, 16) for h in range(2)], axis=1).astype(jnp.bfloat16)
            return 0

        lax.fori_loop(0, 16, one_column, 0, unroll=8)

    lane = lax.broadcasted_iota(jnp.int32, (8, AUX), 1)
    back = jnp.zeros((8, AUX), jnp.float32)
    for j, blk in enumerate(g_blocks):
        shift = lax.rem(32 * j - 32 * column + 256, 256)
        turned = pltpu.roll(blk[pl.ds(80, 8), :], shift, 1)
        back = jnp.where(lane // 32 == j, turned, back)
    slots[...] = back
    g_lane = lax.broadcasted_iota(jnp.int32, (16, AUX), 0).astype(jnp.float32)
    g_ids = jnp.concatenate([g_lane + (16 * meta[8 + j]).astype(jnp.float32) for j in range(8)], axis=0)
    for i, blk in enumerate(f_blocks):
        f_ids = g_lane + (16 * meta[4 + i]).astype(jnp.float32)
        f_plane = meta[16 + i]

        def table_of(row_f, row_g):
            odd = (row_f + row_g) - 2.0 * jnp.floor((row_f + row_g) * 0.5)
            less = (row_f < row_g).astype(jnp.float32)
            use = (odd == less) & (row_f != row_g)
            row_f = jnp.where(use, row_f, -1.0)
            left = (row_f == f_ids).astype(jnp.float32).astype(jnp.bfloat16)
            right = (row_g == g_ids).astype(jnp.float32).astype(jnp.bfloat16)
            return lax.dot_general(left, right, (((1,), (1,)), ((), ())), preferred_element_type=jnp.float32)

        there = table_of(blk[pl.ds(80 + plane, 1), :], blk[pl.ds(84 + plane, 1), :])
        back_i = table_of(slots[pl.ds(4 + f_plane, 1), :], slots[pl.ds(f_plane, 1), :])
        counts[pl.ds(16 * i, 16), :] = there + back_i
        sizes = blk[pl.ds(88, 1), :]
        eye = lax.broadcasted_iota(jnp.int32, (16, AUX), 0) == lax.broadcasted_iota(jnp.int32, (16, AUX), 1)
        size_col = jnp.sum(jnp.where(eye, sizes, 0.0), axis=1, keepdims=True)
        many = jnp.floor((size_col + (CHUNK - 1)) * (1.0 / CHUNK))
        chunks[pl.ds(16 * i, 16), :] = jnp.broadcast_to(many, (16, 128))

    most = jnp.max(counts[...]).astype(jnp.int32)
    safe = jnp.min(lowest) >= WIDTH_FLOOR
    row8 = lax.broadcasted_iota(jnp.int32, (8, 128), 0)

    lane8 = lax.broadcasted_iota(jnp.int32, (8, 128), 1)
    sizes = jnp.zeros((8, 128), jnp.float32)
    for j, blk in enumerate(g_blocks):
        part = blk[pl.ds(88, 8), 0:128]
        part = part if j == 0 else pltpu.roll(part, 16 * j, 1)
        sizes = jnp.where(lane8 // 16 == j, part, sizes)
    is_wide = jnp.where((sizes > 128.0) & (row8 == 0), 1.0, 0.0)
    before = (lax.broadcasted_iota(jnp.int32, (128, 128), 0) < lax.broadcasted_iota(jnp.int32, (128, 128), 1))
    rank_wide = jnp.dot(is_wide.astype(jnp.bfloat16), before.astype(jnp.float32).astype(jnp.bfloat16), preferred_element_type=jnp.float32)
    n_wide = jnp.sum(is_wide)
    rank = jnp.where(is_wide > 0.0, rank_wide, n_wide + lane8.astype(jnp.float32) - rank_wide)
    slots[:, 0:128] = rank
    move = (slots[pl.ds(0, 1), 0:128] == pick.astype(jnp.float32)).astype(jnp.float32).astype(jnp.bfloat16)
    transposed = (((1,), (1,)), ((), ()))
    sorted_counts[...] = lax.dot_general(counts[...].astype(jnp.bfloat16), move, transposed, preferred_element_type=jnp.float32)
    order = lax.dot_general(lane8.astype(jnp.float32).astype(jnp.bfloat16), move, transposed, preferred_element_type=jnp.float32)
    per_tile = jnp.where(lane8.astype(jnp.float32) < n_wide, float(WIDE), float(NARROW))

    def step(r, p, last, kind):
        take = NARROW if kind == "narrow" else WIDE
        half = lax.div(p, 2)
        codes = [table[half + u, r] for u in range(take // 2)]
        at = []
        for e in codes:
            at += [e & 1023, (e >> 10) & 1023]
        times = (codes[0] >> 20).astype(jnp.float32)
        g = table[SPAN // 2 + 9, r]
        block = rhs[pl.ds(pl.multiple_of(g * 16, 16), 16), :]
        blank = jnp.zeros((128 - DEPTH, AUX), jnp.bfloat16)
        weight = cg[pl.ds(g, 1), :] * times
        base = pl.multiple_of(g * 8, 8)
        if kind == "narrow":
            left = jnp.concatenate(
                [jnp.concatenate([lhs[e] for e in at[:4]], axis=0), jnp.concatenate([lhs[e] for e in at[4:]], axis=0)], axis=1)
            thin = block[:, :128]
            none = jnp.zeros((128, 128), jnp.bfloat16)
            right = jnp.concatenate([thin, thin, thin, blank[:, :128]], axis=0)
            right = jnp.concatenate([jnp.concatenate([right, none], axis=1), jnp.concatenate([none, right], axis=1)], axis=0)
            kern = lax.rsqrt(jnp.dot(left, right, preferred_element_type=jnp.float32))
            ka, kb = kern[:, :128], kern[:, 128:]
            coef_a = jnp.concatenate([rows_f[e, 0:CHUNK, :] for e in at[:4]], axis=0)
            coef_b = jnp.concatenate([rows_f[e, 0:CHUNK, :] for e in at[4:]], axis=0)
            sec = jnp.sum((ka * coef_a + kb * coef_b).reshape(-1, 8, 128), axis=0)
            acc_left[pl.ds(base, 8), :] = acc_left[pl.ds(base, 8), :] + sec * times
            sums = [rows_f[e, CHUNK:2 * CHUNK, :] for e in at]
            first = [k[u * CHUNK:(u + 1) * CHUNK] * weight[:, :128] for k in (ka, kb) for u in range(4)]
        else:
            left = jnp.concatenate([lhs[e] for e in at], axis=0)
            if kind == "exact":
                part = block.astype(jnp.float32)
                dist = None
                for k in range(3):
                    mine = jnp.where(((pick % 16 == k) & (pick < DEPTH)), -0.5, 0.0).astype(jnp.bfloat16)
                    mine = jnp.dot(left, mine, preferred_element_type=jnp.float32)
                    other = part[k:k + 1] + part[8 + k:9 + k] + part[12 + k:13 + k]
                    gap = jnp.concatenate([mine, mine], axis=1) - other
                    dist = gap * gap if dist is None else dist + gap * gap
                wide = spread(left, 21, 23, 1.0)
                dist = dist + jnp.concatenate([wide, wide], axis=1) + width_row(g)
            else:
                right = jnp.concatenate([block, block, block, blank], axis=0)
                dist = jnp.dot(left, right, preferred_element_type=jnp.float32)
            kern = lax.rsqrt(dist)
            k0, k1 = kern[:, :128], kern[:, 128:]
            coef = jnp.concatenate([rows_f[e, 0:CHUNK, :] for e in at], axis=0)
            sec0 = jnp.sum((k0 * coef).reshape(-1, 8, 128), axis=0)
            sec1 = jnp.sum((k1 * coef).reshape(-1, 8, 128), axis=0)
            acc_left[pl.ds(base, 8), :] = acc_left[pl.ds(base, 8), :] + sec0 * times
            acc_right[pl.ds(base, 8), :] = acc_right[pl.ds(base, 8), :] + sec1 * times
            both = k0 * weight[:, :128] + k1 * weight[:, 128:]
            sums = [rows_f[e, CHUNK:2 * CHUNK, :] for e in at]
            first = [both[u * CHUNK:(u + 1) * CHUNK] for u in range(take)]
        for e, value, more in zip(at, sums, first):
            rows_f[e, CHUNK:2 * CHUNK, :] = value + more
        stay = p + take < table[SPAN // 2 + 8, r]
        r_next = jnp.where(stay, r, r + 1)
        p_next = jnp.where(stay, p + take, 0)
        over = r_next > last
        return jnp.minimum(r_next, last), jnp.where(over, SPAN, p_next)

    def width_row(g):
        row = jnp.zeros((1, AUX), jnp.float32)
        for k, blk in enumerate(g_blocks):
            row = jnp.where(g // 16 == k, blk[pl.ds(48 + g % 16, 1), :], row)
        return row

    def one_round(state):
        r, _ = state
        groups = SPAN // 8
        at = [(row8 + 8 * t + SPAN * r).astype(jnp.float32) for t in range(groups)]

        def one_class(m, state):
            vals, times, total = state
            times = tuple(jnp.where(a >= total, m.astype(jnp.float32), v) for a, v in zip(at, times))

            def scan(f, state):
                vals, total = state
                many = jnp.broadcast_to(chunks[pl.ds(f, 1), :], (8, 128))
                listed = jnp.broadcast_to(sorted_counts[pl.ds(f, 1), :], (8, 128))
                mark = (many + f.astype(jnp.float32) * 16.0) * 4096.0 + total
                vals = tuple(jnp.where(a >= total, mark, v) for a, v in zip(at, vals))
                return vals, total + jnp.where(listed == m.astype(jnp.float32), many, 0.0)

            vals, total = lax.fori_loop(0, NF, scan, (vals, total), unroll=8)
            vals = tuple(jnp.where(a >= total, -1.0, v) for a, v in zip(at, vals))
            total = jnp.floor((total + per_tile - 1.0) / per_tile) * per_tile
            return vals, times, total

        flat = zeros_v[...]
        none = (flat,) * groups
        vals, times, total = lax.fori_loop(1, most + 1, one_class, (none, none, flat))
        for t in range(groups):
            code = jnp.floor(vals[t] * (1.0 / 4096.0))
            offset = at[t] - (vals[t] - 4096.0 * code)
            frag = jnp.floor(code * (1.0 / 16.0))
            entry = jnp.where((vals[t] >= 0.0) & (at[t] < total), frag * CPF + offset, float(DUMMY))
            places[0, pl.ds(8 * t, 8), :] = entry
            places[1, pl.ds(8 * t, 8), :] = times[t]
        even = places.at[0][pl.ds(0, SPAN // 2, stride=2), :].astype(jnp.int32)
        odd = places.at[0][pl.ds(1, SPAN // 2, stride=2), :].astype(jnp.int32)
        often = places.at[1][pl.ds(0, SPAN // 2, stride=2), :].astype(jnp.int32)
        table_v[pl.ds(0, SPAN // 2), :] = even + odd * 1024 + often * 2**20
        table_v[pl.ds(SPAN // 2, 8), :] = jnp.full((8, 128), DUMMY * 1025, jnp.int32)
        left_over = jnp.clip(total - (SPAN * r).astype(jnp.float32), 0.0, float(SPAN))
        tiles = jnp.maximum(left_over / per_tile, 1.0)
        in_wide = lane8.astype(jnp.float32) < n_wide
        tiles_wide = jnp.sum(jnp.where(in_wide, tiles, 0.0), axis=1, keepdims=True)
        tiles_thin = jnp.sum(jnp.where(in_wide, 0.0, tiles), axis=1, keepdims=True)
        tiles_all = jnp.sum(jnp.maximum(left_over * (1.0 / WIDE), 1.0), axis=1, keepdims=True)
        info = left_over
        for k, row in enumerate((order, tiles_wide, tiles_thin, tiles_all, n_wide)):
            info = jnp.where(row8 == k + 1, row, info)
        table_v[pl.ds(SPAN // 2 + 8, 8), :] = info.astype(jnp.int32)
        longest = jnp.max(total).astype(jnp.int32)
        copy = pltpu.make_async_copy(table_v, table, sem)
        copy.start()
        copy.wait()
        info_at = SPAN // 2 + 8
        count_wide = table[info_at + 5, 0]

        def many_tiles(kind, width, tiles, begin, last):
            def body(_, state):
                for _u in range(width):
                    state = step(*state, last, kind)
                return state

            lax.fori_loop(0, (tiles + (width - 1)) // width, body, (begin, jnp.int32(0)))

        @pl.when(safe)
        def _():
            many_tiles("wide", UNROLL, table[info_at + 2, 0], jnp.int32(0), jnp.maximum(count_wide - 1, 0))
            many_tiles("narrow", UNROLL, table[info_at + 3, 0], jnp.minimum(count_wide, NG - 1), jnp.int32(NG - 1))

        @pl.when(jnp.logical_not(safe))
        def _():
            many_tiles("exact", 1, table[info_at + 4, 0], jnp.int32(0), jnp.int32(NG - 1))

        return r + 1, longest

    zeros_v[...] = jnp.zeros_like(zeros_v)
    lax.while_loop(lambda state: state[0] * SPAN < state[1], one_round, (jnp.int32(0), jnp.int32(1)))

    lanes = lax.broadcasted_iota(jnp.int32, (AUX, 128), 1)

    def collect(f, out):
        col = jnp.sum(rows_f[pl.ds(f * CPF, CPF), CHUNK:2 * CHUNK, :].reshape(AUX, 128), axis=1, keepdims=True)
        return jnp.where(lanes == f, col, out)

    rows_out = rows_f[pl.ds(0, CPF), 0:CHUNK, :].reshape(AUX, 128)
    rows_out = lax.fori_loop(0, NF, collect, rows_out).T
    outf_own[...] = rows_out[0:16]
    outf_near[...] = rows_out[16:32]
    outf_far[...] = rows_out[32:64]
    cols = []
    for part in (acc_left, acc_right):
        half = part[pl.ds(0, NG, stride=8), :]
        for r in range(1, 8):
            half = half + part[pl.ds(r, NG, stride=8), :]
        cols.append(half)
    cols = jnp.concatenate(cols, axis=1)
    out_own[...] = cols[0:16]
    out_near[...] = cols[16:32]
    out_far[...] = cols[32:64]
    out_sib[...] = cols[64:128]


def rectangle(meta, packets):
    vmem = pl.BlockSpec(memory_space=pltpu.VMEM)
    shape = lambda rows: jax.ShapeDtypeStruct((rows, AUX), jnp.float32)
    return pl.pallas_call(
        pair_kernel,
        out_shape=(shape(64), shape(32), shape(16), shape(16), shape(32), shape(16), shape(16)),
        in_specs=[pl.BlockSpec(memory_space=pltpu.SMEM)] + [vmem] * 11,
        out_specs=(vmem,) * 7,
        scratch_shapes=[
            pltpu.VMEM((DUMMY + 1, CHUNK, 128), jnp.bfloat16),
            pltpu.VMEM((DUMMY + 1, 2 * CHUNK, 128), jnp.float32),
            pltpu.VMEM((NG * 8, 128), jnp.float32),
            pltpu.VMEM((NG * 8, 128), jnp.float32),
            pltpu.VMEM((NG * 16, AUX), jnp.bfloat16),
            pltpu.VMEM((NG, AUX), jnp.float32),
            pltpu.VMEM((2, DEPTH * 16, 128), jnp.float32),
            pltpu.VMEM((8, AUX), jnp.float32),
            pltpu.VMEM((NF, 128), jnp.float32),
            pltpu.VMEM((NF, 128), jnp.float32),
            pltpu.VMEM((NF, 128), jnp.float32),
            pltpu.VMEM((8, 128), jnp.float32),
            pltpu.VMEM((2, SPAN, 128), jnp.float32),
            pltpu.VMEM((SPAN // 2 + 16, 128), jnp.int32),
            pltpu.SMEM((SPAN // 2 + 16, 128), jnp.int32),
            pltpu.SemaphoreType.DMA,
        ],
        compiler_params=pltpu.CompilerParams(vmem_limit_bytes=56 * 2**20),
    )(meta, *packets)


def index_of(z, x, c):
    return (z * 4 + x) * 2 + c


def partners(move):
    return [
        (index_of(z, x, c), index_of(*move(z, x, c)))
        for z in range(4) for x in range(4) for c in range(2)
    ]


X_NEAR = partners(lambda z, x, c: (z, x ^ 1, c))
X_FAR = partners(lambda z, x, c: (z, 3 - x, c))
Z_NEAR = partners(lambda z, x, c: (z ^ 1, x, c))
Z_FAR = partners(lambda z, x, c: (3 - z, x, c))
CORE = partners(lambda z, x, c: (z, x, c ^ 1))


def swap(array, pairs):
    return lax.ppermute(array, "frag", pairs)


def local(coeffs, centres, frag_sizes, pairs):
    me = lax.axis_index("frag")
    z, x, c = me // 8, (me // 2) % 4, me % 2
    mask = (jnp.arange(AUX, dtype=jnp.int32)[None, :] < frag_sizes[:, None]).astype(jnp.float32)
    packet = jnp.concatenate(
        [
            centres.transpose(1, 0, 2).reshape(4 * FRAG_DEV, AUX),
            coeffs * mask,
            pairs.T.reshape(8, AUX).astype(jnp.float32),
            jnp.pad(frag_sizes.astype(jnp.float32)[None, :], ((0, 7), (0, AUX - FRAG_DEV))),
        ],
        axis=0,
    )
    zs = jnp.stack([z, z ^ 1, 3 - z, (3 - z) ^ 1])
    xs = jnp.stack([x, x ^ 1, 3 - x, (3 - x) ^ 1])
    f_dev = index_of(zs, x, c)
    g_dev = jnp.concatenate([index_of(z, xs, c), index_of(z, xs, c ^ 1)])
    zero = jnp.zeros((2,), jnp.int32)
    meta = jnp.concatenate([jnp.stack([z, 2 * x + c]), zero, f_dev, g_dev, zs]).astype(jnp.int32)

    x_near = swap(packet, X_NEAR)
    z_near = swap(packet, Z_NEAR)
    x_far = swap(packet, X_FAR)
    z_far = swap(packet, Z_FAR)
    x_last = swap(x_near, X_FAR)
    z_last = swap(z_near, Z_FAR)
    own_c = swap(packet, CORE)
    near_c = swap(x_near, CORE)
    far_c = swap(x_far, CORE)
    last_c = swap(x_last, CORE)

    g_sib, g_far, g_near, g_own, f_far, f_near, f_own = rectangle(
        meta,
        (packet, z_near, z_far, z_last, x_near, x_far, x_last, own_c, near_c, far_c, last_c),
    )
    f_back = swap(f_far, Z_FAR)
    sib_back = swap(g_sib, CORE)
    far_back = swap(g_far + sib_back[32:], X_FAR)
    f_last = swap(f_near + f_back[16:], Z_NEAR)
    near_back = swap(g_near + sib_back[16:32] + far_back[16:], X_NEAR)
    total = f_own + f_back[:16] + f_last + g_own + sib_back[:16] + far_back[:16] + near_back
    return total * mask


def solution(mesh):
    return jax.shard_map(
        local,
        mesh=mesh,
        in_specs=(
            P(("cplx", "frag"), None),
            P(("cplx", "frag"), None, None),
            P(("cplx", "frag")),
            P(("cplx", "frag"), None),
        ),
        out_specs=P(("cplx", "frag"), None),
        check_vma=False,
    )
```

```python
import functools

import jax
import jax.numpy as jnp
from jax import lax
from jax.experimental import pallas as pl
from jax.experimental.pallas import tpu as pltpu
from jax.sharding import PartitionSpec as P

FRAG_DEV = 16
AUX = 256
ROWS = 96
NF = 64
NG = 128
CHUNK = 32
CPF = AUX // CHUNK
WIDE = 4
NARROW = 8
SPAN = 64
DUMMY = NF * CPF
DEPTH = 48
COL = 24
UNROLL = 16
WIDTH_FLOOR = 1.0 / 32.0


def pieces(value):
    first = value.astype(jnp.bfloat16).astype(jnp.float32)
    rest = value - first
    second = rest.astype(jnp.bfloat16).astype(jnp.float32)
    return first, second, rest - second


def pair_kernel(meta, *refs):
    packets = refs[:11]
    out_sib, out_far, out_near, out_own, outf_far, outf_near, outf_own = refs[11:18]
    (lhs, rows_f, cols_f, rhs, build, slots, counts, chunks, zeros_v, places, ends,
     table_v, tiles_v, table, tile_list, sem) = refs[18:]
    f_blocks = [packets[0], packets[1], packets[2], packets[3]]
    g_blocks = [packets[0]] + list(packets[4:])
    plane = meta[0]
    column = meta[1]

    def put_rows(r, value):
        for h in range(2):
            build[h, pl.ds(r * 16, 16), :] = value[:, 128 * h:128 * h + 128]

    def take_rows(h, at, count):
        return build.at[h][pl.ds(at, count, stride=16), :]

    lowest = None
    for i, blk in enumerate(f_blocks):
        x, y, z, w, c = (blk[pl.ds(16 * k, 16), :] for k in range(5))
        lowest = w if lowest is None else jnp.minimum(lowest, w)
        s = x * x + y * y + z * z + w
        one = jnp.ones_like(x)
        zero = jnp.zeros_like(x)
        px, py, pz = pieces(-2.0 * x), pieces(-2.0 * y), pieces(-2.0 * z)
        ps, pw, pc = pieces(s), pieces(w), pieces(c)
        for k in range(3):
            delta = one if k == 0 else zero
            extra = pc if k == 0 else (pw if k == 1 else (zero, zero, zero))
            rows = [px[k], py[k], pz[k], delta, ps[k], *extra,
                    px[k], py[k], pz[k], delta, px[k], py[k], pz[k], delta]
            for r, value in enumerate(rows):
                put_rows(16 * k + r, value)

        def one_row(lf, _, i=i):
            for h in range(2):
                feats = take_rows(h, lf, DEPTH).T
                feats = jnp.concatenate([feats, jnp.zeros((128, 128 - DEPTH), jnp.float32)], axis=1)
                lhs[pl.ds((i * 16 + lf) * CPF + 4 * h, 4)] = feats.astype(jnp.bfloat16).reshape(4, CHUNK, 128)
            return 0

        lax.fori_loop(0, 16, one_row, 0, unroll=4)
    spare_lane = lax.broadcasted_iota(jnp.int32, (CHUNK, 128), 1)
    lhs[DUMMY] = (spare_lane == 4).astype(jnp.float32).astype(jnp.bfloat16)

    pick = lax.broadcasted_iota(jnp.int32, (128, 128), 0)

    def spread(rows, lo, hi, scale):
        sel = jnp.where((pick >= lo) & (pick <= hi), scale, 0.0)
        return jnp.dot(rows, sel.astype(jnp.bfloat16), preferred_element_type=jnp.float32)

    def one_spread(f, _):
        value = spread(lhs[pl.ds(f * CPF, CPF)].reshape(AUX, 128), 5, 7, 1.0)
        rows_f[pl.ds(f * CPF, CPF), 0:CHUNK, :] = value.reshape(CPF, CHUNK, 128)
        rows_f[pl.ds(f * CPF, CPF), CHUNK:2 * CHUNK, :] = jnp.zeros((CPF, CHUNK, 128), jnp.float32)
        return 0

    lax.fori_loop(0, NF, one_spread, 0, unroll=4)
    rows_f[DUMMY] = jnp.zeros((2 * CHUNK, 128), jnp.float32)

    for j, blk in enumerate(g_blocks):
        x, y, z, w, c = (blk[pl.ds(16 * k, 16), :] for k in range(5))
        lowest = jnp.minimum(lowest, w)
        s = x * x + y * y + z * z + w
        one = jnp.ones_like(x)
        zero = jnp.zeros_like(x)
        px, py, pz, ps = pieces(x), pieces(y), pieces(z), pieces(s)
        rows = [px[0], py[0], pz[0], ps[0], one, zero, zero, zero,
                px[1], py[1], pz[1], ps[1], px[2], py[2], pz[2], ps[2]]
        for r, value in enumerate(rows):
            put_rows(r, value)

        def one_column(lg, _, j=j, blk=blk):
            start = pl.multiple_of((j * 16 + lg) * 16, 16)
            base = pl.multiple_of((j * 16 + lg) * COL, COL)
            cols_f[pl.ds(base, 16), :] = jnp.zeros((16, 128), jnp.float32)
            coef = blk[pl.ds(64 + lg, 1), :]
            for h in range(2):
                cols_f[pl.ds(base + 16 + h, 1), :] = coef[:, 128 * h:128 * h + 128]
            rhs[pl.ds(start, 16), :] = jnp.concatenate([take_rows(h, lg, 16) for h in range(2)], axis=1).astype(jnp.bfloat16)
            return 0

        lax.fori_loop(0, 16, one_column, 0, unroll=8)

    lane = lax.broadcasted_iota(jnp.int32, (8, AUX), 1)
    back = jnp.zeros((8, AUX), jnp.float32)
    for j, blk in enumerate(g_blocks):
        shift = lax.rem(32 * j - 32 * column + 256, 256)
        turned = pltpu.roll(blk[pl.ds(80, 8), :], shift, 1)
        back = jnp.where(lane // 32 == j, turned, back)
    slots[...] = back
    g_lane = lax.broadcasted_iota(jnp.int32, (16, AUX), 0).astype(jnp.float32)
    g_ids = jnp.concatenate([g_lane + (16 * meta[8 + j]).astype(jnp.float32) for j in range(8)], axis=0)
    for i, blk in enumerate(f_blocks):
        f_ids = g_lane + (16 * meta[4 + i]).astype(jnp.float32)
        f_plane = meta[16 + i]

        def table_of(row_f, row_g):
            odd = (row_f + row_g) - 2.0 * jnp.floor((row_f + row_g) * 0.5)
            less = (row_f < row_g).astype(jnp.float32)
            use = (odd == less) & (row_f != row_g)
            row_f = jnp.where(use, row_f, -1.0)
            left = (row_f == f_ids).astype(jnp.float32).astype(jnp.bfloat16)
            right = (row_g == g_ids).astype(jnp.float32).astype(jnp.bfloat16)
            return lax.dot_general(left, right, (((1,), (1,)), ((), ())), preferred_element_type=jnp.float32)

        there = table_of(blk[pl.ds(80 + plane, 1), :], blk[pl.ds(84 + plane, 1), :])
        back_i = table_of(slots[pl.ds(4 + f_plane, 1), :], slots[pl.ds(f_plane, 1), :])
        counts[pl.ds(16 * i, 16), :] = there + back_i
        sizes = blk[pl.ds(88, 1), :]
        eye = lax.broadcasted_iota(jnp.int32, (16, AUX), 0) == lax.broadcasted_iota(jnp.int32, (16, AUX), 1)
        size_col = jnp.sum(jnp.where(eye, sizes, 0.0), axis=1, keepdims=True)
        many = jnp.floor((size_col + (CHUNK - 1)) * (1.0 / CHUNK))
        chunks[pl.ds(16 * i, 16), :] = jnp.broadcast_to(many, (16, 128))

    most = jnp.max(counts[...]).astype(jnp.int32)
    safe = jnp.min(lowest) >= WIDTH_FLOOR
    row8 = lax.broadcasted_iota(jnp.int32, (8, 128), 0)

    lane8 = lax.broadcasted_iota(jnp.int32, (8, 128), 1)
    sizes = jnp.zeros((8, 128), jnp.float32)
    for j, blk in enumerate(g_blocks):
        part = blk[pl.ds(88, 8), 0:128]
        part = part if j == 0 else pltpu.roll(part, 16 * j, 1)
        sizes = jnp.where(lane8 // 16 == j, part, sizes)
    slots[:, 0:128] = sizes
    is_wide = jnp.where(jnp.broadcast_to(slots[pl.ds(0, 1), 0:128], (8, 128)) > 128.0, 1.0, 0.0)
    per_tile = jnp.where(is_wide > 0.0, float(WIDE), float(NARROW))
    contract = (((1,), (1,)), ((), ()))

    def step(code, kind):
        take = NARROW if kind == "narrow" else WIDE
        g, q = code & 127, code >> 7
        at = [table[q + u // WIDE, u % WIDE, g] for u in range(take)]
        times = (at[0] >> 10).astype(jnp.float32)
        at = [e & 1023 if u % WIDE == 0 else e for u, e in enumerate(at)]
        base = pl.multiple_of(g * COL, COL)
        block = rhs[pl.ds(pl.multiple_of(g * 16, 16), 16), :]
        blank = jnp.zeros((128 - DEPTH, AUX), jnp.bfloat16)
        if kind == "narrow":
            left = jnp.concatenate(
                [jnp.concatenate([lhs[e] for e in at[:4]], axis=0), jnp.concatenate([lhs[e] for e in at[4:]], axis=0)], axis=1)
            thin = block[:, :128]
            none = jnp.zeros((128, 128), jnp.bfloat16)
            right = jnp.concatenate([thin, thin, thin, blank[:, :128]], axis=0)
            right = jnp.concatenate([jnp.concatenate([right, none], axis=1), jnp.concatenate([none, right], axis=1)], axis=0)
            kern = lax.rsqrt(jnp.dot(left, right, preferred_element_type=jnp.float32))
            ka, kb = kern[:, :128], kern[:, 128:]
            coef_a = jnp.concatenate([rows_f[e, 0:CHUNK, :] for e in at[:4]], axis=0)
            coef_b = jnp.concatenate([rows_f[e, 0:CHUNK, :] for e in at[4:]], axis=0)
            sec = jnp.sum((ka * coef_a + kb * coef_b).reshape(-1, 8, 128), axis=0)
            cols_f[pl.ds(base, 8), :] = cols_f[pl.ds(base, 8), :] + sec * times
            weight = cols_f[pl.ds(base + 16, 1), :] * times
            sums = [rows_f[e, CHUNK:2 * CHUNK, :] for e in at]
            first = [k[u * CHUNK:(u + 1) * CHUNK] * weight for k in (ka, kb) for u in range(4)]
        else:
            left = jnp.concatenate([lhs[e] for e in at], axis=0)
            if kind == "exact":
                part = block.astype(jnp.float32)
                dist = None
                for k in range(3):
                    mine = jnp.where(((pick % 16 == k) & (pick < DEPTH)), -0.5, 0.0).astype(jnp.bfloat16)
                    mine = jnp.dot(left, mine, preferred_element_type=jnp.float32)
                    other = part[k:k + 1] + part[8 + k:9 + k] + part[12 + k:13 + k]
                    gap = jnp.concatenate([mine, mine], axis=1) - other
                    dist = gap * gap if dist is None else dist + gap * gap
                wide = spread(left, 21, 23, 1.0)
                dist = dist + jnp.concatenate([wide, wide], axis=1) + width_row(g)
            else:
                right = jnp.concatenate([block, block, block, blank], axis=0)
                dist = jnp.dot(left, right, preferred_element_type=jnp.float32)
            kern = lax.rsqrt(dist)
            k0, k1 = kern[:, :128], kern[:, 128:]
            coef = jnp.concatenate([rows_f[e, 0:CHUNK, :] for e in at], axis=0)
            sec0 = jnp.sum((k0 * coef).reshape(-1, 8, 128), axis=0)
            sec1 = jnp.sum((k1 * coef).reshape(-1, 8, 128), axis=0)
            cols_f[pl.ds(base, 8), :] = cols_f[pl.ds(base, 8), :] + sec0 * times
            cols_f[pl.ds(base + 8, 8), :] = cols_f[pl.ds(base + 8, 8), :] + sec1 * times
            both = k0 * (cols_f[pl.ds(base + 16, 1), :] * times) + k1 * (cols_f[pl.ds(base + 17, 1), :] * times)
            sums = [rows_f[e, CHUNK:2 * CHUNK, :] for e in at]
            first = [both[u * CHUNK:(u + 1) * CHUNK] for u in range(take)]
        for e, value, more in zip(at, sums, first):
            rows_f[e, CHUNK:2 * CHUNK, :] = value + more

    def width_row(g):
        row = jnp.zeros((1, AUX), jnp.float32)
        for k, blk in enumerate(g_blocks):
            row = jnp.where(g // 16 == k, blk[pl.ds(48 + g % 16, 1), :], row)
        return row

    def one_round(state):
        r, _ = state
        groups = SPAN // 8
        at = [(row8 + 8 * t + SPAN * r).astype(jnp.float32) for t in range(groups)]

        def one_class(m, state):
            vals, times, total = state
            times = tuple(jnp.where(a >= total, m.astype(jnp.float32), v) for a, v in zip(at, times))

            def scan(f, state):
                vals, total = state
                many = jnp.broadcast_to(chunks[pl.ds(f, 1), :], (8, 128))
                listed = jnp.broadcast_to(counts[pl.ds(f, 1), :], (8, 128))
                mark = (many + f.astype(jnp.float32) * 16.0) * 4096.0 + total
                vals = tuple(jnp.where(a >= total, mark, v) for a, v in zip(at, vals))
                return vals, total + jnp.where(listed == m.astype(jnp.float32), many, 0.0)

            vals, total = lax.fori_loop(0, NF, scan, (vals, total), unroll=8)
            vals = tuple(jnp.where(a >= total, -1.0, v) for a, v in zip(at, vals))
            total = jnp.floor((total + per_tile - 1.0) / per_tile) * per_tile
            return vals, times, total

        flat = zeros_v[...]
        none = (flat,) * groups
        vals, times, total = lax.fori_loop(1, most + 1, one_class, (none, none, flat))
        for t in range(groups):
            code = jnp.floor(vals[t] * (1.0 / 4096.0))
            offset = at[t] - (vals[t] - 4096.0 * code)
            frag = jnp.floor(code * (1.0 / 16.0))
            entry = jnp.where((vals[t] >= 0.0) & (at[t] < total), frag * CPF + offset, float(DUMMY))
            places[0, pl.ds(8 * t, 8), :] = entry
            places[1, pl.ds(8 * t, 8), :] = times[t]
        groups4 = SPAN // WIDE
        for u in range(WIDE):
            value = places.at[0][pl.ds(u, groups4, stride=WIDE), :]
            if u == 0:
                value = value + 1024.0 * places.at[1][pl.ds(u, groups4, stride=WIDE), :]
            table_v[pl.ds(0, groups4), u, :] = value.astype(jnp.int32)
        table_v[pl.ds(groups4, 2)] = jnp.full((2, WIDE, 128), DUMMY, jnp.int32)
        left_over = jnp.clip(total - (SPAN * r).astype(jnp.float32), 0.0, float(SPAN))
        tiles = left_over / per_tile
        tiles_wide = tiles * is_wide
        tiles_thin = tiles - tiles_wide
        for k, tiles in enumerate((tiles_wide, tiles_thin)):
            ends[k] = lax.dot_general(upto, jnp.concatenate([tiles] * 16, axis=0).astype(jnp.bfloat16), contract, preferred_element_type=jnp.float32)
        number = [(lane8 + 128 * row8 + 1024 * k).astype(jnp.float32) for k in range(2)]

        def seek(c, state):
            out = []
            column = (c + 1).astype(jnp.float32)
            for k, (where, begin) in enumerate(state):
                end = jnp.broadcast_to(ends.at[k // 2][pl.ds(c, 1), :], (8, 128))
                hit = number[k % 2] >= end
                out.append((jnp.where(hit, column, where), jnp.where(hit, end, begin)))
            return tuple(out)

        found = lax.fori_loop(0, NG, seek, ((flat, flat),) * 3, unroll=8)
        for k, (where, begin) in enumerate(found):
            place = (number[k % 2] - begin) * (1.0 if k < 2 else 2.0) * 128.0 + where
            place = jnp.where(where < float(NG), place, float(groups4 * 128))
            tiles_v[pl.ds(8 * k, 8), :] = place.astype(jnp.int32)
        info = jnp.where(row8 == 0, jnp.sum(tiles_wide, axis=1, keepdims=True), jnp.sum(tiles_thin, axis=1, keepdims=True))
        tiles_v[pl.ds(24, 8), :] = info.astype(jnp.int32)
        longest = jnp.max(total).astype(jnp.int32)
        copies = [pltpu.make_async_copy(table_v, table, sem.at[0]), pltpu.make_async_copy(tiles_v, tile_list, sem.at[1])]
        for copy in copies:
            copy.start()
        for copy in copies:
            copy.wait()
        count_wide, count_thin = tile_list[24, 0], tile_list[25, 0]

        def many_tiles(kind, first_row, count):
            def body(i, _):
                row, col = first_row + (i >> 3), (i & 7) * UNROLL
                for u in range(UNROLL):
                    step(tile_list[row, col + u], kind)
                return 0

            lax.fori_loop(0, (count + (UNROLL - 1)) // UNROLL, body, 0)

        @pl.when(safe)
        def _():
            many_tiles("wide", 0, count_wide)
            many_tiles("narrow", 16, count_thin)

        @pl.when(jnp.logical_not(safe))
        def _():
            def wide_one(t, _):
                step(tile_list[t >> 7, t & 127], "exact")
                return 0

            def thin_one(t, _):
                step(tile_list[16 + (t >> 8), (t & 255) >> 1] + 128 * (t & 1), "exact")
                return 0

            lax.fori_loop(0, count_wide, wide_one, 0)
            lax.fori_loop(0, 2 * count_thin, thin_one, 0)

        return r + 1, longest

    zeros_v[...] = jnp.zeros_like(zeros_v)
    upto = (lax.broadcasted_iota(jnp.int32, (128, 128), 1) <= pick).astype(jnp.float32).astype(jnp.bfloat16)
    lax.while_loop(lambda state: state[0] * SPAN < state[1], one_round, (jnp.int32(0), jnp.int32(1)))

    lanes = lax.broadcasted_iota(jnp.int32, (AUX, 128), 1)

    def collect(f, out):
        col = jnp.sum(rows_f[pl.ds(f * CPF, CPF), CHUNK:2 * CHUNK, :].reshape(AUX, 128), axis=1, keepdims=True)
        return jnp.where(lanes == f, col, out)

    rows_out = rows_f[pl.ds(0, CPF), 0:CHUNK, :].reshape(AUX, 128)
    rows_out = lax.fori_loop(0, NF, collect, rows_out).T
    outf_own[...] = rows_out[0:16]
    outf_near[...] = rows_out[16:32]
    outf_far[...] = rows_out[32:64]
    cols = []
    for h in range(2):
        half = cols_f[pl.ds(8 * h, NG, stride=COL), :]
        for r in range(1, 8):
            half = half + cols_f[pl.ds(8 * h + r, NG, stride=COL), :]
        cols.append(half)
    cols = jnp.concatenate(cols, axis=1)
    out_own[...] = cols[0:16]
    out_near[...] = cols[16:32]
    out_far[...] = cols[32:64]
    out_sib[...] = cols[64:128]


def rectangle(meta, packets):
    vmem = pl.BlockSpec(memory_space=pltpu.VMEM)
    shape = lambda rows: jax.ShapeDtypeStruct((rows, AUX), jnp.float32)
    return pl.pallas_call(
        pair_kernel,
        out_shape=(shape(64), shape(32), shape(16), shape(16), shape(32), shape(16), shape(16)),
        in_specs=[pl.BlockSpec(memory_space=pltpu.SMEM)] + [vmem] * 11,
        out_specs=(vmem,) * 7,
        scratch_shapes=[
            pltpu.VMEM((DUMMY + 1, CHUNK, 128), jnp.bfloat16),
            pltpu.VMEM((DUMMY + 1, 2 * CHUNK, 128), jnp.float32),
            pltpu.VMEM((NG * COL, 128), jnp.float32),
            pltpu.VMEM((NG * 16, AUX), jnp.bfloat16),
            pltpu.VMEM((2, DEPTH * 16, 128), jnp.float32),
            pltpu.VMEM((8, AUX), jnp.float32),
            pltpu.VMEM((NF, 128), jnp.float32),
            pltpu.VMEM((NF, 128), jnp.float32),
            pltpu.VMEM((8, 128), jnp.float32),
            pltpu.VMEM((2, SPAN, 128), jnp.float32),
            pltpu.VMEM((2, 128, 128), jnp.float32),
            pltpu.VMEM((SPAN // WIDE + 2, WIDE, 128), jnp.int32),
            pltpu.VMEM((32, 128), jnp.int32),
            pltpu.SMEM((SPAN // WIDE + 2, WIDE, 128), jnp.int32),
            pltpu.SMEM((32, 128), jnp.int32),
            pltpu.SemaphoreType.DMA((2,)),
        ],
        compiler_params=pltpu.CompilerParams(vmem_limit_bytes=56 * 2**20),
    )(meta, *packets)


def index_of(z, x, c):
    return (z * 4 + x) * 2 + c


def partners(move):
    return [
        (index_of(z, x, c), index_of(*move(z, x, c)))
        for z in range(4) for x in range(4) for c in range(2)
    ]


X_NEAR = partners(lambda z, x, c: (z, x ^ 1, c))
X_FAR = partners(lambda z, x, c: (z, 3 - x, c))
Z_NEAR = partners(lambda z, x, c: (z ^ 1, x, c))
Z_FAR = partners(lambda z, x, c: (3 - z, x, c))
CORE = partners(lambda z, x, c: (z, x, c ^ 1))


def swap(array, pairs):
    return lax.ppermute(array, "frag", pairs)


def local(coeffs, centres, frag_sizes, pairs):
    me = lax.axis_index("frag")
    z, x, c = me // 8, (me // 2) % 4, me % 2
    mask = (jnp.arange(AUX, dtype=jnp.int32)[None, :] < frag_sizes[:, None]).astype(jnp.float32)
    packet = jnp.concatenate(
        [
            centres.transpose(1, 0, 2).reshape(4 * FRAG_DEV, AUX),
            coeffs * mask,
            pairs.T.reshape(8, AUX).astype(jnp.float32),
            jnp.pad(frag_sizes.astype(jnp.float32)[None, :], ((0, 7), (0, AUX - FRAG_DEV))),
        ],
        axis=0,
    )
    zs = jnp.stack([z, z ^ 1, 3 - z, (3 - z) ^ 1])
    xs = jnp.stack([x, x ^ 1, 3 - x, (3 - x) ^ 1])
    f_dev = index_of(zs, x, c)
    g_dev = jnp.concatenate([index_of(z, xs, c), index_of(z, xs, c ^ 1)])
    zero = jnp.zeros((2,), jnp.int32)
    meta = jnp.concatenate([jnp.stack([z, 2 * x + c]), zero, f_dev, g_dev, zs]).astype(jnp.int32)

    x_near = swap(packet, X_NEAR)
    z_near = swap(packet, Z_NEAR)
    x_far = swap(packet, X_FAR)
    z_far = swap(packet, Z_FAR)
    x_last = swap(x_near, X_FAR)
    z_last = swap(z_near, Z_FAR)
    own_c = swap(packet, CORE)
    near_c = swap(x_near, CORE)
    far_c = swap(x_far, CORE)
    last_c = swap(x_last, CORE)

    g_sib, g_far, g_near, g_own, f_far, f_near, f_own = rectangle(
        meta,
        (packet, z_near, z_far, z_last, x_near, x_far, x_last, own_c, near_c, far_c, last_c),
    )
    f_back = swap(f_far, Z_FAR)
    sib_back = swap(g_sib, CORE)
    far_back = swap(g_far + sib_back[32:], X_FAR)
    f_last = swap(f_near + f_back[16:], Z_NEAR)
    near_back = swap(g_near + sib_back[16:32] + far_back[16:], X_NEAR)
    total = f_own + f_back[:16] + f_last + g_own + sib_back[:16] + far_back[:16] + near_back
    return total * mask


def solution(mesh):
    return jax.shard_map(
        local,
        mesh=mesh,
        in_specs=(
            P(("cplx", "frag"), None),
            P(("cplx", "frag"), None, None),
            P(("cplx", "frag")),
            P(("cplx", "frag"), None),
        ),
        out_specs=P(("cplx", "frag"), None),
        check_vma=False,
    )
```

```python
import functools

import jax
import jax.numpy as jnp
from jax import lax
from jax.experimental import pallas as pl
from jax.experimental.pallas import tpu as pltpu
from jax.sharding import PartitionSpec as P

FRAG_DEV = 16
AUX = 256
ROWS = 96
NF = 64
NG = 128
CHUNK = 32
CPF = AUX // CHUNK
WIDE = 4
NARROW = 8
SPAN = 64
DUMMY = NF * CPF
DEPTH = 48
BATCH = 8
WIDTH_FLOOR = 1.0 / 32.0


def pieces(value):
    first = value.astype(jnp.bfloat16).astype(jnp.float32)
    rest = value - first
    second = rest.astype(jnp.bfloat16).astype(jnp.float32)
    return first, second, rest - second


def pair_kernel(meta, *refs):
    packets = refs[:11]
    out_sib, out_far, out_near, out_own, outf_far, outf_near, outf_own = refs[11:18]
    (lhs, rows_c, rows_s, cols_s, cols_c, rhs, build, slots, counts, chunks, zeros_v, places, ends,
     table_v, tiles_v, dist_a, dist_b, table, tile_list, held_a, held_b, sem) = refs[18:]
    f_blocks = [packets[0], packets[1], packets[2], packets[3]]
    g_blocks = [packets[0]] + list(packets[4:])
    plane = meta[0]
    column = meta[1]

    def put_rows(r, value):
        for h in range(2):
            build[h, pl.ds(r * 16, 16), :] = value[:, 128 * h:128 * h + 128]

    def take_rows(h, at, count):
        return build.at[h][pl.ds(at, count, stride=16), :]

    lowest = None
    for i, blk in enumerate(f_blocks):
        x, y, z, w, c = (blk[pl.ds(16 * k, 16), :] for k in range(5))
        lowest = w if lowest is None else jnp.minimum(lowest, w)
        s = x * x + y * y + z * z + w
        one = jnp.ones_like(x)
        zero = jnp.zeros_like(x)
        px, py, pz = pieces(-2.0 * x), pieces(-2.0 * y), pieces(-2.0 * z)
        ps, pw, pc = pieces(s), pieces(w), pieces(c)
        for k in range(3):
            delta = one if k == 0 else zero
            extra = pc if k == 0 else (pw if k == 1 else (zero, zero, zero))
            rows = [px[k], py[k], pz[k], delta, ps[k], *extra,
                    px[k], py[k], pz[k], delta, px[k], py[k], pz[k], delta]
            for r, value in enumerate(rows):
                put_rows(16 * k + r, value)

        def one_row(lf, _, i=i):
            for h in range(2):
                feats = take_rows(h, lf, DEPTH).T
                feats = jnp.concatenate([feats, jnp.zeros((128, 128 - DEPTH), jnp.float32)], axis=1)
                lhs[pl.ds((i * 16 + lf) * CPF + 4 * h, 4)] = feats.astype(jnp.bfloat16).reshape(4, CHUNK, 128)
            return 0

        lax.fori_loop(0, 16, one_row, 0, unroll=4)
    spare_lane = lax.broadcasted_iota(jnp.int32, (CHUNK, 128), 1)
    lhs[DUMMY] = (spare_lane == 4).astype(jnp.float32).astype(jnp.bfloat16)

    pick = lax.broadcasted_iota(jnp.int32, (128, 128), 0)

    def spread(rows, lo, hi, scale):
        sel = jnp.where((pick >= lo) & (pick <= hi), scale, 0.0)
        return jnp.dot(rows, sel.astype(jnp.bfloat16), preferred_element_type=jnp.float32)

    def one_spread(f, _):
        value = spread(lhs[pl.ds(f * CPF, CPF)].reshape(AUX, 128), 5, 7, 1.0)
        rows_c[pl.ds(f * CPF, CPF)] = value.reshape(CPF, CHUNK, 128)
        rows_s[pl.ds(f * CPF, CPF)] = jnp.zeros((CPF, CHUNK, 128), jnp.float32)
        return 0

    lax.fori_loop(0, NF, one_spread, 0, unroll=4)
    rows_c[DUMMY] = jnp.zeros((CHUNK, 128), jnp.float32)
    rows_s[DUMMY] = jnp.zeros((CHUNK, 128), jnp.float32)

    for j, blk in enumerate(g_blocks):
        x, y, z, w, c = (blk[pl.ds(16 * k, 16), :] for k in range(5))
        lowest = jnp.minimum(lowest, w)
        s = x * x + y * y + z * z + w
        one = jnp.ones_like(x)
        zero = jnp.zeros_like(x)
        px, py, pz, ps = pieces(x), pieces(y), pieces(z), pieces(s)
        rows = [px[0], py[0], pz[0], ps[0], one, zero, zero, zero,
                px[1], py[1], pz[1], ps[1], px[2], py[2], pz[2], ps[2]]
        for r, value in enumerate(rows):
            put_rows(r, value)

        def one_column(lg, _, j=j, blk=blk):
            start = pl.multiple_of((j * 16 + lg) * 16, 16)
            load = pl.multiple_of((j * 16 + lg) * 8, 8)
            cols_s[pl.ds(start, 16), :] = jnp.zeros((16, 128), jnp.float32)
            coef = blk[pl.ds(64 + lg, 1), :]
            for h in range(2):
                cols_c[pl.ds(load + h, 1), :] = coef[:, 128 * h:128 * h + 128]
            rhs[pl.ds(start, 16), :] = jnp.concatenate([take_rows(h, lg, 16) for h in range(2)], axis=1).astype(jnp.bfloat16)
            return 0

        lax.fori_loop(0, 16, one_column, 0, unroll=8)

    lane = lax.broadcasted_iota(jnp.int32, (8, AUX), 1)
    back = jnp.zeros((8, AUX), jnp.float32)
    for j, blk in enumerate(g_blocks):
        shift = lax.rem(32 * j - 32 * column + 256, 256)
        turned = pltpu.roll(blk[pl.ds(80, 8), :], shift, 1)
        back = jnp.where(lane // 32 == j, turned, back)
    slots[...] = back
    g_lane = lax.broadcasted_iota(jnp.int32, (16, AUX), 0).astype(jnp.float32)
    g_ids = jnp.concatenate([g_lane + (16 * meta[8 + j]).astype(jnp.float32) for j in range(8)], axis=0)
    for i, blk in enumerate(f_blocks):
        f_ids = g_lane + (16 * meta[4 + i]).astype(jnp.float32)
        f_plane = meta[16 + i]

        def table_of(row_f, row_g):
            odd = (row_f + row_g) - 2.0 * jnp.floor((row_f + row_g) * 0.5)
            less = (row_f < row_g).astype(jnp.float32)
            use = (odd == less) & (row_f != row_g)
            row_f = jnp.where(use, row_f, -1.0)
            left = (row_f == f_ids).astype(jnp.float32).astype(jnp.bfloat16)
            right = (row_g == g_ids).astype(jnp.float32).astype(jnp.bfloat16)
            return lax.dot_general(left, right, (((1,), (1,)), ((), ())), preferred_element_type=jnp.float32)

        there = table_of(blk[pl.ds(80 + plane, 1), :], blk[pl.ds(84 + plane, 1), :])
        back_i = table_of(slots[pl.ds(4 + f_plane, 1), :], slots[pl.ds(f_plane, 1), :])
        counts[pl.ds(16 * i, 16), :] = there + back_i
        sizes = blk[pl.ds(88, 1), :]
        eye = lax.broadcasted_iota(jnp.int32, (16, AUX), 0) == lax.broadcasted_iota(jnp.int32, (16, AUX), 1)
        size_col = jnp.sum(jnp.where(eye, sizes, 0.0), axis=1, keepdims=True)
        many = jnp.floor((size_col + (CHUNK - 1)) * (1.0 / CHUNK))
        chunks[pl.ds(16 * i, 16), :] = jnp.broadcast_to(many, (16, 128))

    most = jnp.max(counts[...]).astype(jnp.int32)
    safe = jnp.min(lowest) >= WIDTH_FLOOR
    row8 = lax.broadcasted_iota(jnp.int32, (8, 128), 0)

    lane8 = lax.broadcasted_iota(jnp.int32, (8, 128), 1)
    sizes = jnp.zeros((8, 128), jnp.float32)
    for j, blk in enumerate(g_blocks):
        part = blk[pl.ds(88, 8), 0:128]
        part = part if j == 0 else pltpu.roll(part, 16 * j, 1)
        sizes = jnp.where(lane8 // 16 == j, part, sizes)
    slots[:, 0:128] = sizes
    is_wide = jnp.where(jnp.broadcast_to(slots[pl.ds(0, 1), 0:128], (8, 128)) > 128.0, 1.0, 0.0)
    per_tile = jnp.where(is_wide > 0.0, float(WIDE), float(NARROW))
    contract = (((1,), (1,)), ((), ()))

    blank = jnp.zeros((128 - DEPTH, 128), jnp.bfloat16)
    none = jnp.zeros((128, 128), jnp.bfloat16)

    def chunks_of(code, take):
        g, q = code & 127, code >> 7
        at = [table[q + u // WIDE, u % WIDE, g] for u in range(take)]
        times = at[0] >> 10
        return g, times, [e & 1023 if u % WIDE == 0 else e for u, e in enumerate(at)]

    def fetch(code, kind, dist, held, u):
        g, times, at = chunks_of(code, NARROW if kind == "narrow" else WIDE)
        for k, value in enumerate([g, times] + at):
            held[u, k] = value
        block = rhs[pl.ds(pl.multiple_of(g * 16, 16), 16), :]
        left = jnp.concatenate([lhs[e] for e in at[:4]], axis=0)
        if kind == "narrow":
            left = jnp.concatenate([left, jnp.concatenate([lhs[e] for e in at[4:]], axis=0)], axis=1)
            thin = block[:, :128]
            right = jnp.concatenate([thin, thin, thin, blank], axis=0)
            right = jnp.concatenate([jnp.concatenate([right, none], axis=1), jnp.concatenate([none, right], axis=1)], axis=0)
        else:
            right = jnp.concatenate([block, block, block, jnp.concatenate([blank, blank], axis=1)], axis=0)
        dist[u] = jnp.dot(left, right, preferred_element_type=jnp.float32)

    def gather(at):
        return jnp.concatenate([rows_c[e] for e in at], axis=0)

    def fold(value):
        return jnp.sum(value.reshape(-1, 8, 128), axis=0)

    def apply(kern, kind, g, times, at):
        times = times.astype(jnp.float32)
        base = pl.multiple_of(g * 16, 16)
        load = pl.multiple_of(g * 8, 8)
        k0, k1 = kern[:, :128], kern[:, 128:]
        weight = cols_c[pl.ds(load, 1), :] * times
        if kind == "narrow":
            second = fold(k0 * gather(at[:4]) + k1 * gather(at[4:]))
            cols_s[pl.ds(base, 8), :] = cols_s[pl.ds(base, 8), :] + second * times
            first = [k[u * CHUNK:(u + 1) * CHUNK] * weight for k in (k0, k1) for u in range(4)]
        else:
            coef = gather(at)
            cols_s[pl.ds(base, 8), :] = cols_s[pl.ds(base, 8), :] + fold(k0 * coef) * times
            cols_s[pl.ds(base + 8, 8), :] = cols_s[pl.ds(base + 8, 8), :] + fold(k1 * coef) * times
            both = k0 * weight + k1 * (cols_c[pl.ds(load + 1, 1), :] * times)
            first = [both[u * CHUNK:(u + 1) * CHUNK] for u in range(4)]
        sums = [rows_s[e] for e in at]
        for e, value, more in zip(at, sums, first):
            rows_s[e] = value + more

    def exact(code):
        g, times, at = chunks_of(code, WIDE)
        left = jnp.concatenate([lhs[e] for e in at], axis=0)
        part = rhs[pl.ds(pl.multiple_of(g * 16, 16), 16), :].astype(jnp.float32)
        wide = spread(left, 21, 23, 1.0)
        dist = jnp.concatenate([wide, wide], axis=1) + width_row(g)
        for k in range(3):
            mine = jnp.where(((pick % 16 == k) & (pick < DEPTH)), -0.5, 0.0).astype(jnp.bfloat16)
            mine = jnp.dot(left, mine, preferred_element_type=jnp.float32)
            other = part[k:k + 1] + part[8 + k:9 + k] + part[12 + k:13 + k]
            gap = jnp.concatenate([mine, mine], axis=1) - other
            dist = dist + gap * gap
        apply(lax.rsqrt(dist), "wide", g, times, at)

    def width_row(g):
        row = jnp.zeros((1, AUX), jnp.float32)
        for k, blk in enumerate(g_blocks):
            row = jnp.where(g // 16 == k, blk[pl.ds(48 + g % 16, 1), :], row)
        return row

    def one_round(state):
        r, _ = state
        groups = SPAN // 8
        at = [(row8 + 8 * t + SPAN * r).astype(jnp.float32) for t in range(groups)]

        def one_class(m, state):
            vals, times, total = state
            times = tuple(jnp.where(a >= total, m.astype(jnp.float32), v) for a, v in zip(at, times))

            def scan(f, state):
                vals, total = state
                many = jnp.broadcast_to(chunks[pl.ds(f, 1), :], (8, 128))
                listed = jnp.broadcast_to(counts[pl.ds(f, 1), :], (8, 128))
                mark = (many + f.astype(jnp.float32) * 16.0) * 4096.0 + total
                vals = tuple(jnp.where(a >= total, mark, v) for a, v in zip(at, vals))
                return vals, total + jnp.where(listed == m.astype(jnp.float32), many, 0.0)

            vals, total = lax.fori_loop(0, NF, scan, (vals, total), unroll=8)
            vals = tuple(jnp.where(a >= total, -1.0, v) for a, v in zip(at, vals))
            total = jnp.floor((total + per_tile - 1.0) / per_tile) * per_tile
            return vals, times, total

        flat = zeros_v[...]
        none = (flat,) * groups
        vals, times, total = lax.fori_loop(1, most + 1, one_class, (none, none, flat))
        for t in range(groups):
            code = jnp.floor(vals[t] * (1.0 / 4096.0))
            offset = at[t] - (vals[t] - 4096.0 * code)
            frag = jnp.floor(code * (1.0 / 16.0))
            entry = jnp.where((vals[t] >= 0.0) & (at[t] < total), frag * CPF + offset, float(DUMMY))
            places[0, pl.ds(8 * t, 8), :] = entry
            places[1, pl.ds(8 * t, 8), :] = times[t]
        groups4 = SPAN // WIDE
        for u in range(WIDE):
            value = places.at[0][pl.ds(u, groups4, stride=WIDE), :]
            if u == 0:
                value = value + 1024.0 * places.at[1][pl.ds(u, groups4, stride=WIDE), :]
            table_v[pl.ds(0, groups4), u, :] = value.astype(jnp.int32)
        table_v[pl.ds(groups4, 2)] = jnp.full((2, WIDE, 128), DUMMY, jnp.int32)
        left_over = jnp.clip(total - (SPAN * r).astype(jnp.float32), 0.0, float(SPAN))
        tiles = left_over / per_tile
        tiles_wide = tiles * is_wide
        tiles_thin = tiles - tiles_wide
        for k, tiles in enumerate((tiles_wide, tiles_thin)):
            ends[k] = lax.dot_general(upto, jnp.concatenate([tiles] * 16, axis=0).astype(jnp.bfloat16), contract, preferred_element_type=jnp.float32)
        number = [(lane8 + 128 * row8 + 1024 * k).astype(jnp.float32) for k in range(2)]

        def seek(c, state):
            out = []
            column = (c + 1).astype(jnp.float32)
            for k, (where, begin) in enumerate(state):
                end = jnp.broadcast_to(ends.at[k // 2][pl.ds(c, 1), :], (8, 128))
                hit = number[k % 2] >= end
                out.append((jnp.where(hit, column, where), jnp.where(hit, end, begin)))
            return tuple(out)

        found = lax.fori_loop(0, NG, seek, ((flat, flat),) * 3, unroll=8)
        for k, (where, begin) in enumerate(found):
            place = (number[k % 2] - begin) * (1.0 if k < 2 else 2.0) * 128.0 + where
            place = jnp.where(where < float(NG), place, float(groups4 * 128))
            tiles_v[pl.ds(8 * k, 8), :] = place.astype(jnp.int32)
        info = jnp.where(row8 == 0, jnp.sum(tiles_wide, axis=1, keepdims=True), jnp.sum(tiles_thin, axis=1, keepdims=True))
        tiles_v[pl.ds(24, 8), :] = info.astype(jnp.int32)
        longest = jnp.max(total).astype(jnp.int32)
        copies = [pltpu.make_async_copy(table_v, table, sem.at[0]), pltpu.make_async_copy(tiles_v, tile_list, sem.at[1])]
        for copy in copies:
            copy.start()
        for copy in copies:
            copy.wait()
        count_wide, count_thin = tile_list[24, 0], tile_list[25, 0]

        def many_tiles(kind, first_row, last, count):
            take = NARROW if kind == "narrow" else WIDE

            def fetch_batch(b, dist, held):
                b = jnp.minimum(b, last)
                row, col = first_row + (b >> 4), (b & 15) * BATCH
                for u in range(BATCH):
                    fetch(tile_list[row, col + u], kind, dist, held, u)

            def apply_batch(dist, held):
                for u in range(BATCH):
                    at = [held[u, 2 + k] for k in range(take)]
                    apply(lax.rsqrt(dist[u]), kind, held[u, 0], held[u, 1], at)

            def body(i, _):
                fetch_batch(2 * i + 1, dist_b, held_b)
                apply_batch(dist_a, held_a)
                fetch_batch(2 * i + 2, dist_a, held_a)
                apply_batch(dist_b, held_b)
                return 0

            fetch_batch(jnp.int32(0), dist_a, held_a)
            lax.fori_loop(0, (count + (2 * BATCH - 1)) // (2 * BATCH), body, 0)

        @pl.when(safe)
        def _():
            many_tiles("wide", 0, 255, count_wide)
            many_tiles("narrow", 16, 127, count_thin)

        @pl.when(jnp.logical_not(safe))
        def _():
            def wide_one(t, _):
                exact(tile_list[t >> 7, t & 127])
                return 0

            def thin_one(t, _):
                exact(tile_list[16 + (t >> 8), (t & 255) >> 1] + 128 * (t & 1))
                return 0

            lax.fori_loop(0, count_wide, wide_one, 0)
            lax.fori_loop(0, 2 * count_thin, thin_one, 0)

        return r + 1, longest

    zeros_v[...] = jnp.zeros_like(zeros_v)
    upto = (lax.broadcasted_iota(jnp.int32, (128, 128), 1) <= pick).astype(jnp.float32).astype(jnp.bfloat16)
    lax.while_loop(lambda state: state[0] * SPAN < state[1], one_round, (jnp.int32(0), jnp.int32(1)))

    lanes = lax.broadcasted_iota(jnp.int32, (AUX, 128), 1)

    def collect(f, out):
        col = jnp.sum(rows_s[pl.ds(f * CPF, CPF)].reshape(AUX, 128), axis=1, keepdims=True)
        return jnp.where(lanes == f, col, out)

    rows_out = rows_c[pl.ds(0, CPF)].reshape(AUX, 128)
    rows_out = lax.fori_loop(0, NF, collect, rows_out).T
    outf_own[...] = rows_out[0:16]
    outf_near[...] = rows_out[16:32]
    outf_far[...] = rows_out[32:64]
    cols = []
    for h in range(2):
        half = cols_s[pl.ds(8 * h, NG, stride=16), :]
        for r in range(1, 8):
            half = half + cols_s[pl.ds(8 * h + r, NG, stride=16), :]
        cols.append(half)
    cols = jnp.concatenate(cols, axis=1)
    out_own[...] = cols[0:16]
    out_near[...] = cols[16:32]
    out_far[...] = cols[32:64]
    out_sib[...] = cols[64:128]


def rectangle(meta, packets):
    vmem = pl.BlockSpec(memory_space=pltpu.VMEM)
    shape = lambda rows: jax.ShapeDtypeStruct((rows, AUX), jnp.float32)
    return pl.pallas_call(
        pair_kernel,
        out_shape=(shape(64), shape(32), shape(16), shape(16), shape(32), shape(16), shape(16)),
        in_specs=[pl.BlockSpec(memory_space=pltpu.SMEM)] + [vmem] * 11,
        out_specs=(vmem,) * 7,
        scratch_shapes=[
            pltpu.VMEM((DUMMY + 1, CHUNK, 128), jnp.bfloat16),
            pltpu.VMEM((DUMMY + 1, CHUNK, 128), jnp.float32),
            pltpu.VMEM((DUMMY + 1, CHUNK, 128), jnp.float32),
            pltpu.VMEM((NG * 16, 128), jnp.float32),
            pltpu.VMEM((NG * 8, 128), jnp.float32),
            pltpu.VMEM((NG * 16, AUX), jnp.bfloat16),
            pltpu.VMEM((2, DEPTH * 16, 128), jnp.float32),
            pltpu.VMEM((8, AUX), jnp.float32),
            pltpu.VMEM((NF, 128), jnp.float32),
            pltpu.VMEM((NF, 128), jnp.float32),
            pltpu.VMEM((8, 128), jnp.float32),
            pltpu.VMEM((2, SPAN, 128), jnp.float32),
            pltpu.VMEM((2, 128, 128), jnp.float32),
            pltpu.VMEM((SPAN // WIDE + 2, WIDE, 128), jnp.int32),
            pltpu.VMEM((32, 128), jnp.int32),
            pltpu.VMEM((BATCH, 128, AUX), jnp.float32),
            pltpu.VMEM((BATCH, 128, AUX), jnp.float32),
            pltpu.SMEM((SPAN // WIDE + 2, WIDE, 128), jnp.int32),
            pltpu.SMEM((32, 128), jnp.int32),
            pltpu.SMEM((BATCH, 16), jnp.int32),
            pltpu.SMEM((BATCH, 16), jnp.int32),
            pltpu.SemaphoreType.DMA((2,)),
        ],
        compiler_params=pltpu.CompilerParams(vmem_limit_bytes=56 * 2**20),
    )(meta, *packets)


def index_of(z, x, c):
    return (z * 4 + x) * 2 + c


def partners(move):
    return [
        (index_of(z, x, c), index_of(*move(z, x, c)))
        for z in range(4) for x in range(4) for c in range(2)
    ]


X_NEAR = partners(lambda z, x, c: (z, x ^ 1, c))
X_FAR = partners(lambda z, x, c: (z, 3 - x, c))
Z_NEAR = partners(lambda z, x, c: (z ^ 1, x, c))
Z_FAR = partners(lambda z, x, c: (3 - z, x, c))
CORE = partners(lambda z, x, c: (z, x, c ^ 1))


def swap(array, pairs):
    return lax.ppermute(array, "frag", pairs)


def local(coeffs, centres, frag_sizes, pairs):
    me = lax.axis_index("frag")
    z, x, c = me // 8, (me // 2) % 4, me % 2
    mask = (jnp.arange(AUX, dtype=jnp.int32)[None, :] < frag_sizes[:, None]).astype(jnp.float32)
    packet = jnp.concatenate(
        [
            centres.transpose(1, 0, 2).reshape(4 * FRAG_DEV, AUX),
            coeffs * mask,
            pairs.T.reshape(8, AUX).astype(jnp.float32),
            jnp.pad(frag_sizes.astype(jnp.float32)[None, :], ((0, 7), (0, AUX - FRAG_DEV))),
        ],
        axis=0,
    )
    zs = jnp.stack([z, z ^ 1, 3 - z, (3 - z) ^ 1])
    xs = jnp.stack([x, x ^ 1, 3 - x, (3 - x) ^ 1])
    f_dev = index_of(zs, x, c)
    g_dev = jnp.concatenate([index_of(z, xs, c), index_of(z, xs, c ^ 1)])
    zero = jnp.zeros((2,), jnp.int32)
    meta = jnp.concatenate([jnp.stack([z, 2 * x + c]), zero, f_dev, g_dev, zs]).astype(jnp.int32)

    x_near = swap(packet, X_NEAR)
    z_near = swap(packet, Z_NEAR)
    x_far = swap(packet, X_FAR)
    z_far = swap(packet, Z_FAR)
    x_last = swap(x_near, X_FAR)
    z_last = swap(z_near, Z_FAR)
    own_c = swap(packet, CORE)
    near_c = swap(x_near, CORE)
    far_c = swap(x_far, CORE)
    last_c = swap(x_last, CORE)

    g_sib, g_far, g_near, g_own, f_far, f_near, f_own = rectangle(
        meta,
        (packet, z_near, z_far, z_last, x_near, x_far, x_last, own_c, near_c, far_c, last_c),
    )
    f_back = swap(f_far, Z_FAR)
    sib_back = swap(g_sib, CORE)
    far_back = swap(g_far + sib_back[32:], X_FAR)
    f_last = swap(f_near + f_back[16:], Z_NEAR)
    near_back = swap(g_near + sib_back[16:32] + far_back[16:], X_NEAR)
    total = f_own + f_back[:16] + f_last + g_own + sib_back[:16] + far_back[:16] + near_back
    return total * mask


def solution(mesh):
    return jax.shard_map(
        local,
        mesh=mesh,
        in_specs=(
            P(("cplx", "frag"), None),
            P(("cplx", "frag"), None, None),
            P(("cplx", "frag")),
            P(("cplx", "frag"), None),
        ),
        out_specs=P(("cplx", "frag"), None),
        check_vma=False,
    )
```

```python
import functools

import jax
import jax.numpy as jnp
from jax import lax
from jax.experimental import pallas as pl
from jax.experimental.pallas import tpu as pltpu
from jax.sharding import PartitionSpec as P

FRAG_DEV = 16
AUX = 256
ROWS = 96
NF = 64
NG = 128
CHUNK = 32
CPF = AUX // CHUNK
WIDE = 4
NARROW = 8
SPAN = 64
DUMMY = NF * CPF
DEPTH = 48
BATCH = 16
SHIFT = 3
WIDTH_FLOOR = 1.0 / 32.0


def pieces(value):
    first = value.astype(jnp.bfloat16).astype(jnp.float32)
    rest = value - first
    second = rest.astype(jnp.bfloat16).astype(jnp.float32)
    return first, second, rest - second


def pair_kernel(meta, *refs):
    packets = refs[:11]
    out_sib, out_far, out_near, out_own, outf_far, outf_near, outf_own = refs[11:18]
    (lhs, rows_c, rows_s, cols_s, cols_c, rhs, build, slots, counts, chunks, zeros_v, places, ends,
     table_v, tiles_v, row_sums, table, tile_list, sem) = refs[18:]
    f_blocks = [packets[0], packets[1], packets[2], packets[3]]
    g_blocks = [packets[0]] + list(packets[4:])
    plane = meta[0]
    column = meta[1]

    def put_rows(r, value):
        for h in range(2):
            build[h, pl.ds(r * 16, 16), :] = value[:, 128 * h:128 * h + 128]

    def take_rows(h, at, count):
        return build.at[h][pl.ds(at, count, stride=16), :]

    lowest = None
    for i, blk in enumerate(f_blocks):
        x, y, z, w, c = (blk[pl.ds(16 * k, 16), :] for k in range(5))
        lowest = w if lowest is None else jnp.minimum(lowest, w)
        s = x * x + y * y + z * z + w
        one = jnp.ones_like(x)
        zero = jnp.zeros_like(x)
        px, py, pz = pieces(-2.0 * x), pieces(-2.0 * y), pieces(-2.0 * z)
        ps, pw, pc = pieces(s), pieces(w), pieces(c)
        for k in range(3):
            delta = one if k == 0 else zero
            extra = pc if k == 0 else (pw if k == 1 else (zero, zero, zero))
            rows = [px[k], py[k], pz[k], delta, ps[k], *extra,
                    px[k], py[k], pz[k], delta, px[k], py[k], pz[k], delta]
            for r, value in enumerate(rows):
                put_rows(16 * k + r, value)

        def one_row(lf, _, i=i):
            for h in range(2):
                feats = take_rows(h, lf, DEPTH).T
                feats = jnp.concatenate([feats, jnp.zeros((128, 128 - DEPTH), jnp.float32)], axis=1)
                lhs[pl.ds((i * 16 + lf) * CPF + 4 * h, 4)] = feats.astype(jnp.bfloat16).reshape(4, CHUNK, 128)
            return 0

        lax.fori_loop(0, 16, one_row, 0, unroll=4)
    spare_lane = lax.broadcasted_iota(jnp.int32, (CHUNK, 128), 1)
    lhs[DUMMY] = (spare_lane == 4).astype(jnp.float32).astype(jnp.bfloat16)

    pick = lax.broadcasted_iota(jnp.int32, (128, 128), 0)

    def spread(rows, lo, hi, scale):
        sel = jnp.where((pick >= lo) & (pick <= hi), scale, 0.0)
        return jnp.dot(rows, sel.astype(jnp.bfloat16), preferred_element_type=jnp.float32)

    def one_spread(f, _):
        value = spread(lhs[pl.ds(f * CPF, CPF)].reshape(AUX, 128), 5, 7, 1.0)
        rows_c[pl.ds(f * CPF, CPF)] = value.reshape(CPF, CHUNK, 128)
        rows_s[pl.ds(f * CPF, CPF)] = jnp.zeros((CPF, CHUNK, 128), jnp.float32)
        return 0

    lax.fori_loop(0, NF, one_spread, 0, unroll=4)
    rows_c[DUMMY] = jnp.zeros((CHUNK, 128), jnp.float32)
    rows_s[DUMMY] = jnp.zeros((CHUNK, 128), jnp.float32)

    for j, blk in enumerate(g_blocks):
        x, y, z, w, c = (blk[pl.ds(16 * k, 16), :] for k in range(5))
        lowest = jnp.minimum(lowest, w)
        s = x * x + y * y + z * z + w
        one = jnp.ones_like(x)
        zero = jnp.zeros_like(x)
        px, py, pz, ps = pieces(x), pieces(y), pieces(z), pieces(s)
        rows = [px[0], py[0], pz[0], ps[0], one, zero, zero, zero,
                px[1], py[1], pz[1], ps[1], px[2], py[2], pz[2], ps[2]]
        for r, value in enumerate(rows):
            put_rows(r, value)

        def one_column(lg, _, j=j, blk=blk):
            start = pl.multiple_of((j * 16 + lg) * 16, 16)
            load = pl.multiple_of((j * 16 + lg) * 8, 8)
            cols_s[pl.ds(start, 16), :] = jnp.zeros((16, 128), jnp.float32)
            coef = blk[pl.ds(64 + lg, 1), :]
            for h in range(2):
                cols_c[pl.ds(load + h, 1), :] = coef[:, 128 * h:128 * h + 128]
            rhs[pl.ds(start, 16), :] = jnp.concatenate([take_rows(h, lg, 16) for h in range(2)], axis=1).astype(jnp.bfloat16)
            return 0

        lax.fori_loop(0, 16, one_column, 0, unroll=8)

    lane = lax.broadcasted_iota(jnp.int32, (8, AUX), 1)
    back = jnp.zeros((8, AUX), jnp.float32)
    for j, blk in enumerate(g_blocks):
        shift = lax.rem(32 * j - 32 * column + 256, 256)
        turned = pltpu.roll(blk[pl.ds(80, 8), :], shift, 1)
        back = jnp.where(lane // 32 == j, turned, back)
    slots[...] = back
    g_lane = lax.broadcasted_iota(jnp.int32, (16, AUX), 0).astype(jnp.float32)
    g_ids = jnp.concatenate([g_lane + (16 * meta[8 + j]).astype(jnp.float32) for j in range(8)], axis=0)
    for i, blk in enumerate(f_blocks):
        f_ids = g_lane + (16 * meta[4 + i]).astype(jnp.float32)
        f_plane = meta[16 + i]

        def table_of(row_f, row_g):
            odd = (row_f + row_g) - 2.0 * jnp.floor((row_f + row_g) * 0.5)
            less = (row_f < row_g).astype(jnp.float32)
            use = (odd == less) & (row_f != row_g)
            row_f = jnp.where(use, row_f, -1.0)
            left = (row_f == f_ids).astype(jnp.float32).astype(jnp.bfloat16)
            right = (row_g == g_ids).astype(jnp.float32).astype(jnp.bfloat16)
            return lax.dot_general(left, right, (((1,), (1,)), ((), ())), preferred_element_type=jnp.float32)

        there = table_of(blk[pl.ds(80 + plane, 1), :], blk[pl.ds(84 + plane, 1), :])
        back_i = table_of(slots[pl.ds(4 + f_plane, 1), :], slots[pl.ds(f_plane, 1), :])
        counts[pl.ds(16 * i, 16), :] = there + back_i
        sizes = blk[pl.ds(88, 1), :]
        eye = lax.broadcasted_iota(jnp.int32, (16, AUX), 0) == lax.broadcasted_iota(jnp.int32, (16, AUX), 1)
        size_col = jnp.sum(jnp.where(eye, sizes, 0.0), axis=1, keepdims=True)
        many = jnp.floor((size_col + (CHUNK - 1)) * (1.0 / CHUNK))
        chunks[pl.ds(16 * i, 16), :] = jnp.broadcast_to(many, (16, 128))

    most = jnp.max(counts[...]).astype(jnp.int32)
    safe = jnp.min(lowest) >= WIDTH_FLOOR
    row8 = lax.broadcasted_iota(jnp.int32, (8, 128), 0)

    lane8 = lax.broadcasted_iota(jnp.int32, (8, 128), 1)
    sizes = jnp.zeros((8, 128), jnp.float32)
    for j, blk in enumerate(g_blocks):
        part = blk[pl.ds(88, 8), 0:128]
        part = part if j == 0 else pltpu.roll(part, 16 * j, 1)
        sizes = jnp.where(lane8 // 16 == j, part, sizes)
    slots[:, 0:128] = sizes
    is_wide = jnp.where(jnp.broadcast_to(slots[pl.ds(0, 1), 0:128], (8, 128)) > 128.0, 1.0, 0.0)
    per_tile = jnp.where(is_wide > 0.0, float(WIDE), float(NARROW))
    contract = (((1,), (1,)), ((), ()))

    blank = jnp.zeros((128 - DEPTH, 128), jnp.bfloat16)
    none = jnp.zeros((128, 128), jnp.bfloat16)

    def chunks_of(code, take):
        g, q = code & 127, code >> 7
        views = [table.at[q + v, :, pl.ds(g, 1)] for v in range(take // WIDE)]
        at = [views[u // WIDE][u % WIDE, 0] for u in range(take)]
        times = at[0] >> 10
        return g, times, [e & 1023 if u % WIDE == 0 else e for u, e in enumerate(at)]

    def distances(g, at, kind):
        block = rhs[pl.ds(pl.multiple_of(g * 16, 16), 16), :]
        left = jnp.concatenate([lhs[e] for e in at[:4]], axis=0)
        if kind == "narrow":
            left = jnp.concatenate([left, jnp.concatenate([lhs[e] for e in at[4:]], axis=0)], axis=1)
            thin = block[:, :128]
            right = jnp.concatenate([thin, thin, thin, blank], axis=0)
            right = jnp.concatenate([jnp.concatenate([right, none], axis=1), jnp.concatenate([none, right], axis=1)], axis=0)
        else:
            right = jnp.concatenate([block, block, block, jnp.concatenate([blank, blank], axis=1)], axis=0)
        return jnp.dot(left, right, preferred_element_type=jnp.float32)

    def gather(at):
        return jnp.concatenate([rows_c[e] for e in at], axis=0)

    def fold(value):
        return jnp.sum(value.reshape(-1, 8, 128), axis=0)

    def apply(kern, kind, g, times, at):
        times = times.astype(jnp.float32)
        base = pl.multiple_of(g * 16, 16)
        load = pl.multiple_of(g * 8, 8)
        k0, k1 = kern[:, :128], kern[:, 128:]
        weight = cols_c[pl.ds(load, 1), :] * times
        if kind == "narrow":
            second = fold(k0 * gather(at[:4]) + k1 * gather(at[4:]))
            cols_s[pl.ds(base, 8), :] = cols_s[pl.ds(base, 8), :] + second * times
            first = [k[u * CHUNK:(u + 1) * CHUNK] * weight for k in (k0, k1) for u in range(4)]
        else:
            coef = gather(at)
            cols_s[pl.ds(base, 8), :] = cols_s[pl.ds(base, 8), :] + fold(k0 * coef) * times
            cols_s[pl.ds(base + 8, 8), :] = cols_s[pl.ds(base + 8, 8), :] + fold(k1 * coef) * times
            both = k0 * weight + k1 * (cols_c[pl.ds(load + 1, 1), :] * times)
            first = [both[u * CHUNK:(u + 1) * CHUNK] for u in range(4)]
        sums = [rows_s[e] for e in at]
        for e, value, more in zip(at, sums, first):
            rows_s[e] = value + more

    def exact(code):
        g, times, at = chunks_of(code, WIDE)
        left = jnp.concatenate([lhs[e] for e in at], axis=0)
        part = rhs[pl.ds(pl.multiple_of(g * 16, 16), 16), :].astype(jnp.float32)
        wide = spread(left, 21, 23, 1.0)
        dist = jnp.concatenate([wide, wide], axis=1) + width_row(g)
        for k in range(3):
            mine = jnp.where(((pick % 16 == k) & (pick < DEPTH)), -0.5, 0.0).astype(jnp.bfloat16)
            mine = jnp.dot(left, mine, preferred_element_type=jnp.float32)
            other = part[k:k + 1] + part[8 + k:9 + k] + part[12 + k:13 + k]
            gap = jnp.concatenate([mine, mine], axis=1) - other
            dist = dist + gap * gap
        apply(lax.rsqrt(dist), "wide", g, times, at)

    def width_row(g):
        row = jnp.zeros((1, AUX), jnp.float32)
        for k, blk in enumerate(g_blocks):
            row = jnp.where(g // 16 == k, blk[pl.ds(48 + g % 16, 1), :], row)
        return row

    def one_round(state):
        r, _ = state
        groups = SPAN // 8
        at = [(row8 + 8 * t + SPAN * r).astype(jnp.float32) for t in range(groups)]

        def one_class(m, state):
            vals, times, total = state
            times = tuple(jnp.where(a >= total, m.astype(jnp.float32), v) for a, v in zip(at, times))

            def scan(f, state):
                vals, total = state
                many = jnp.broadcast_to(chunks[pl.ds(f, 1), :], (8, 128))
                listed = jnp.broadcast_to(counts[pl.ds(f, 1), :], (8, 128))
                mark = (many + f.astype(jnp.float32) * 16.0) * 4096.0 + total
                vals = tuple(jnp.where(a >= total, mark, v) for a, v in zip(at, vals))
                return vals, total + jnp.where(listed == m.astype(jnp.float32), many, 0.0)

            vals, total = lax.fori_loop(0, NF, scan, (vals, total), unroll=8)
            vals = tuple(jnp.where(a >= total, -1.0, v) for a, v in zip(at, vals))
            total = jnp.floor((total + per_tile - 1.0) / per_tile) * per_tile
            return vals, times, total

        flat = zeros_v[...]
        none = (flat,) * groups
        vals, times, total = lax.fori_loop(1, most + 1, one_class, (none, none, flat))
        for t in range(groups):
            code = jnp.floor(vals[t] * (1.0 / 4096.0))
            offset = at[t] - (vals[t] - 4096.0 * code)
            frag = jnp.floor(code * (1.0 / 16.0))
            entry = jnp.where((vals[t] >= 0.0) & (at[t] < total), frag * CPF + offset, float(DUMMY))
            places[0, pl.ds(8 * t, 8), :] = entry
            places[1, pl.ds(8 * t, 8), :] = times[t]
        groups4 = SPAN // WIDE
        for u in range(WIDE):
            value = places.at[0][pl.ds(u, groups4, stride=WIDE), :]
            if u == 0:
                value = value + 1024.0 * places.at[1][pl.ds(u, groups4, stride=WIDE), :]
            table_v[pl.ds(0, groups4), u, :] = value.astype(jnp.int32)
        table_v[pl.ds(groups4, 2)] = jnp.full((2, WIDE, 128), DUMMY, jnp.int32)
        left_over = jnp.clip(total - (SPAN * r).astype(jnp.float32), 0.0, float(SPAN))
        tiles = left_over / per_tile
        tiles_wide = tiles * is_wide
        tiles_thin = tiles - tiles_wide
        for k, tiles in enumerate((tiles_wide, tiles_thin)):
            ends[k] = lax.dot_general(upto, jnp.concatenate([tiles] * 16, axis=0).astype(jnp.bfloat16), contract, preferred_element_type=jnp.float32)
        number = [(lane8 + 128 * row8 + 1024 * k).astype(jnp.float32) for k in range(2)]

        def seek(c, state):
            out = []
            column = (c + 1).astype(jnp.float32)
            for k, (where, begin) in enumerate(state):
                end = jnp.broadcast_to(ends.at[k // 2][pl.ds(c, 1), :], (8, 128))
                hit = number[k % 2] >= end
                out.append((jnp.where(hit, column, where), jnp.where(hit, end, begin)))
            return tuple(out)

        found = lax.fori_loop(0, NG, seek, ((flat, flat),) * 3, unroll=8)
        for k, (where, begin) in enumerate(found):
            place = (number[k % 2] - begin) * (1.0 if k < 2 else 2.0) * 128.0 + where
            place = jnp.where(where < float(NG), place, float(groups4 * 128))
            tiles_v[pl.ds(8 * k, 8), :] = place.astype(jnp.int32)
        info = jnp.where(row8 == 0, jnp.sum(tiles_wide, axis=1, keepdims=True), jnp.sum(tiles_thin, axis=1, keepdims=True))
        tiles_v[pl.ds(24, 8), :] = info.astype(jnp.int32)
        longest = jnp.max(total).astype(jnp.int32)
        copies = [pltpu.make_async_copy(table_v, table, sem.at[0]), pltpu.make_async_copy(tiles_v, tile_list, sem.at[1])]
        for copy in copies:
            copy.start()
        for copy in copies:
            copy.wait()
        count_wide, count_thin = tile_list[24, 0], tile_list[25, 0]

        def many_tiles(kind, first_row, count):
            take = NARROW if kind == "narrow" else WIDE

            def body(b, _):
                row, col = first_row + lax.shift_right_logical(b, SHIFT), (b & (128 // BATCH - 1)) * BATCH
                for u in range(BATCH):
                    g, times, at = chunks_of(tile_list[row, col + u], take)
                    apply(lax.rsqrt(distances(g, at, kind)), kind, g, times, at)
                return 0

            lax.fori_loop(0, (count + (BATCH - 1)) // BATCH, body, 0)

        @pl.when(safe)
        def _():
            many_tiles("wide", 0, count_wide)
            many_tiles("narrow", 16, count_thin)

        @pl.when(jnp.logical_not(safe))
        def _():
            def wide_one(t, _):
                exact(tile_list[t >> 7, t & 127])
                return 0

            def thin_one(t, _):
                exact(tile_list[16 + (t >> 8), (t & 255) >> 1] + 128 * (t & 1))
                return 0

            lax.fori_loop(0, count_wide, wide_one, 0)
            lax.fori_loop(0, 2 * count_thin, thin_one, 0)

        return r + 1, longest

    zeros_v[...] = jnp.zeros_like(zeros_v)
    upto = (lax.broadcasted_iota(jnp.int32, (128, 128), 1) <= pick).astype(jnp.float32).astype(jnp.bfloat16)
    lax.while_loop(lambda state: state[0] * SPAN < state[1], one_round, (jnp.int32(0), jnp.int32(1)))

    ones8 = jnp.ones((8, 256), jnp.bfloat16)

    def collect(f, _):
        value = rows_s[pl.ds(f * CPF, CPF)].reshape(AUX, 128)
        high = value.astype(jnp.bfloat16)
        low = (value - high.astype(jnp.float32)).astype(jnp.bfloat16)
        row = lax.dot_general(ones8, jnp.concatenate([high, low], axis=1), contract, preferred_element_type=jnp.float32)
        for h in range(2):
            row_sums[h, pl.ds(f, 1), :] = row[0:1, 128 * h:128 * h + 128]
        return 0

    lax.fori_loop(0, NF, collect, 0, unroll=8)
    rows_out = jnp.concatenate([row_sums[0], row_sums[1]], axis=1)
    outf_own[...] = rows_out[0:16]
    outf_near[...] = rows_out[16:32]
    outf_far[...] = rows_out[32:64]
    cols = []
    for h in range(2):
        half = cols_s[pl.ds(8 * h, NG, stride=16), :]
        for r in range(1, 8):
            half = half + cols_s[pl.ds(8 * h + r, NG, stride=16), :]
        cols.append(half)
    cols = jnp.concatenate(cols, axis=1)
    out_own[...] = cols[0:16]
    out_near[...] = cols[16:32]
    out_far[...] = cols[32:64]
    out_sib[...] = cols[64:128]


def rectangle(meta, packets):
    vmem = pl.BlockSpec(memory_space=pltpu.VMEM)
    shape = lambda rows: jax.ShapeDtypeStruct((rows, AUX), jnp.float32)
    return pl.pallas_call(
        pair_kernel,
        out_shape=(shape(64), shape(32), shape(16), shape(16), shape(32), shape(16), shape(16)),
        in_specs=[pl.BlockSpec(memory_space=pltpu.SMEM)] + [vmem] * 11,
        out_specs=(vmem,) * 7,
        scratch_shapes=[
            pltpu.VMEM((DUMMY + 1, CHUNK, 128), jnp.bfloat16),
            pltpu.VMEM((DUMMY + 1, CHUNK, 128), jnp.float32),
            pltpu.VMEM((DUMMY + 1, CHUNK, 128), jnp.float32),
            pltpu.VMEM((NG * 16, 128), jnp.float32),
            pltpu.VMEM((NG * 8, 128), jnp.float32),
            pltpu.VMEM((NG * 16, AUX), jnp.bfloat16),
            pltpu.VMEM((2, DEPTH * 16, 128), jnp.float32),
            pltpu.VMEM((8, AUX), jnp.float32),
            pltpu.VMEM((NF, 128), jnp.float32),
            pltpu.VMEM((NF, 128), jnp.float32),
            pltpu.VMEM((8, 128), jnp.float32),
            pltpu.VMEM((2, SPAN, 128), jnp.float32),
            pltpu.VMEM((2, 128, 128), jnp.float32),
            pltpu.VMEM((SPAN // WIDE + 2, WIDE, 128), jnp.int32),
            pltpu.VMEM((32, 128), jnp.int32),
            pltpu.VMEM((2, NF, 128), jnp.float32),
            pltpu.SMEM((SPAN // WIDE + 2, WIDE, 128), jnp.int32),
            pltpu.SMEM((32, 128), jnp.int32),
            pltpu.SemaphoreType.DMA((2,)),
        ],
        compiler_params=pltpu.CompilerParams(vmem_limit_bytes=56 * 2**20),
    )(meta, *packets)


def index_of(z, x, c):
    return (z * 4 + x) * 2 + c


def partners(move):
    return [
        (index_of(z, x, c), index_of(*move(z, x, c)))
        for z in range(4) for x in range(4) for c in range(2)
    ]


X_NEAR = partners(lambda z, x, c: (z, x ^ 1, c))
X_FAR = partners(lambda z, x, c: (z, 3 - x, c))
Z_NEAR = partners(lambda z, x, c: (z ^ 1, x, c))
Z_FAR = partners(lambda z, x, c: (3 - z, x, c))
CORE = partners(lambda z, x, c: (z, x, c ^ 1))


def swap(array, pairs):
    return lax.ppermute(array, "frag", pairs)


def local(coeffs, centres, frag_sizes, pairs):
    me = lax.axis_index("frag")
    z, x, c = me // 8, (me // 2) % 4, me % 2
    mask = (jnp.arange(AUX, dtype=jnp.int32)[None, :] < frag_sizes[:, None]).astype(jnp.float32)
    packet = jnp.concatenate(
        [
            centres.transpose(1, 0, 2).reshape(4 * FRAG_DEV, AUX),
            coeffs * mask,
            pairs.T.reshape(8, AUX).astype(jnp.float32),
            jnp.pad(frag_sizes.astype(jnp.float32)[None, :], ((0, 7), (0, AUX - FRAG_DEV))),
        ],
        axis=0,
    )
    zs = jnp.stack([z, z ^ 1, 3 - z, (3 - z) ^ 1])
    xs = jnp.stack([x, x ^ 1, 3 - x, (3 - x) ^ 1])
    f_dev = index_of(zs, x, c)
    g_dev = jnp.concatenate([index_of(z, xs, c), index_of(z, xs, c ^ 1)])
    zero = jnp.zeros((2,), jnp.int32)
    meta = jnp.concatenate([jnp.stack([z, 2 * x + c]), zero, f_dev, g_dev, zs]).astype(jnp.int32)

    x_near = swap(packet, X_NEAR)
    z_near = swap(packet, Z_NEAR)
    x_far = swap(packet, X_FAR)
    z_far = swap(packet, Z_FAR)
    x_last = swap(x_near, X_FAR)
    z_last = swap(z_near, Z_FAR)
    own_c = swap(packet, CORE)
    near_c = swap(x_near, CORE)
    far_c = swap(x_far, CORE)
    last_c = swap(x_last, CORE)

    g_sib, g_far, g_near, g_own, f_far, f_near, f_own = rectangle(
        meta,
        (packet, z_near, z_far, z_last, x_near, x_far, x_last, own_c, near_c, far_c, last_c),
    )
    f_back = swap(f_far, Z_FAR)
    sib_back = swap(g_sib, CORE)
    far_back = swap(g_far + sib_back[32:], X_FAR)
    f_last = swap(f_near + f_back[16:], Z_NEAR)
    near_back = swap(g_near + sib_back[16:32] + far_back[16:], X_NEAR)
    total = f_own + f_back[:16] + f_last + g_own + sib_back[:16] + far_back[:16] + near_back
    return total * mask


def solution(mesh):
    return jax.shard_map(
        local,
        mesh=mesh,
        in_specs=(
            P(("cplx", "frag"), None),
            P(("cplx", "frag"), None, None),
            P(("cplx", "frag")),
            P(("cplx", "frag"), None),
        ),
        out_specs=P(("cplx", "frag"), None),
        check_vma=False,
    )
```

```python
import functools

import jax
import jax.numpy as jnp
from jax import lax
from jax.experimental import pallas as pl
from jax.experimental.pallas import tpu as pltpu
from jax.sharding import PartitionSpec as P

FRAG_DEV = 16
AUX = 256
ROWS = 96
NF = 64
NG = 128
CHUNK = 32
CPF = AUX // CHUNK
WIDE = 4
NARROW = 8
SPAN = 96
WIDE_ROWS = 24
THIN_ROWS = 16
LIST_ROWS = WIDE_ROWS + THIN_ROWS
DUMMY = NF * CPF
DEPTH = 48
BATCH = 16
SHIFT = 3
WIDTH_FLOOR = 1.0 / 32.0


def pieces(value):
    first = value.astype(jnp.bfloat16).astype(jnp.float32)
    rest = value - first
    second = rest.astype(jnp.bfloat16).astype(jnp.float32)
    return first, second, rest - second


def pair_kernel(meta, *refs):
    packets = refs[:11]
    out_sib, out_far, out_near, out_own, outf_far, outf_near, outf_own = refs[11:18]
    (lhs, rows_c, rows_s, cols_s, cols_c, rhs, build, slots, counts, chunks, zeros_v, places, ends,
     table_v, tiles_v, row_sums, table, tile_list, sem) = refs[18:]
    f_blocks = [packets[0], packets[1], packets[2], packets[3]]
    g_blocks = [packets[0]] + list(packets[4:])
    plane = meta[0]
    column = meta[1]

    def put_rows(r, value):
        for h in range(2):
            build[h, pl.ds(r * 16, 16), :] = value[:, 128 * h:128 * h + 128]

    def take_rows(h, at, count):
        return build.at[h][pl.ds(at, count, stride=16), :]

    lowest = None
    for i, blk in enumerate(f_blocks):
        x, y, z, w, c = (blk[pl.ds(16 * k, 16), :] for k in range(5))
        lowest = w if lowest is None else jnp.minimum(lowest, w)
        s = x * x + y * y + z * z + w
        one = jnp.ones_like(x)
        zero = jnp.zeros_like(x)
        px, py, pz = pieces(-2.0 * x), pieces(-2.0 * y), pieces(-2.0 * z)
        ps, pw, pc = pieces(s), pieces(w), pieces(c)
        for k in range(3):
            delta = one if k == 0 else zero
            extra = pc if k == 0 else (pw if k == 1 else (zero, zero, zero))
            rows = [px[k], py[k], pz[k], delta, ps[k], *extra,
                    px[k], py[k], pz[k], delta, px[k], py[k], pz[k], delta]
            for r, value in enumerate(rows):
                put_rows(16 * k + r, value)

        def one_row(lf, _, i=i):
            for h in range(2):
                feats = take_rows(h, lf, DEPTH).T
                feats = jnp.concatenate([feats, jnp.zeros((128, 128 - DEPTH), jnp.float32)], axis=1)
                lhs[pl.ds((i * 16 + lf) * CPF + 4 * h, 4)] = feats.astype(jnp.bfloat16).reshape(4, CHUNK, 128)
            return 0

        lax.fori_loop(0, 16, one_row, 0, unroll=16)
    spare_lane = lax.broadcasted_iota(jnp.int32, (CHUNK, 128), 1)
    lhs[DUMMY] = (spare_lane == 4).astype(jnp.float32).astype(jnp.bfloat16)

    pick = lax.broadcasted_iota(jnp.int32, (128, 128), 0)

    def spread(rows, lo, hi, scale):
        sel = jnp.where((pick >= lo) & (pick <= hi), scale, 0.0)
        return jnp.dot(rows, sel.astype(jnp.bfloat16), preferred_element_type=jnp.float32)

    def one_spread(f, _):
        value = spread(lhs[pl.ds(f * CPF, CPF)].reshape(AUX, 128), 5, 7, 1.0)
        rows_c[pl.ds(f * CPF, CPF)] = value.reshape(CPF, CHUNK, 128)
        rows_s[pl.ds(f * CPF, CPF)] = jnp.zeros((CPF, CHUNK, 128), jnp.float32)
        return 0

    lax.fori_loop(0, NF, one_spread, 0, unroll=16)
    rows_c[DUMMY] = jnp.zeros((CHUNK, 128), jnp.float32)
    rows_s[DUMMY] = jnp.zeros((CHUNK, 128), jnp.float32)

    for j, blk in enumerate(g_blocks):
        x, y, z, w, c = (blk[pl.ds(16 * k, 16), :] for k in range(5))
        lowest = jnp.minimum(lowest, w)
        s = x * x + y * y + z * z + w
        one = jnp.ones_like(x)
        zero = jnp.zeros_like(x)
        px, py, pz, ps = pieces(x), pieces(y), pieces(z), pieces(s)
        rows = [px[0], py[0], pz[0], ps[0], one, zero, zero, zero,
                px[1], py[1], pz[1], ps[1], px[2], py[2], pz[2], ps[2]]
        for r, value in enumerate(rows):
            put_rows(r, value)

        def one_column(lg, _, j=j, blk=blk):
            start = pl.multiple_of((j * 16 + lg) * 16, 16)
            load = pl.multiple_of((j * 16 + lg) * 8, 8)
            cols_s[pl.ds(start, 16), :] = jnp.zeros((16, 128), jnp.float32)
            coef = blk[pl.ds(64 + lg, 1), :]
            for h in range(2):
                cols_c[pl.ds(load + h, 1), :] = coef[:, 128 * h:128 * h + 128]
            rhs[pl.ds(start, 16), :] = jnp.concatenate([take_rows(h, lg, 16) for h in range(2)], axis=1).astype(jnp.bfloat16)
            return 0

        lax.fori_loop(0, 16, one_column, 0, unroll=16)

    lane = lax.broadcasted_iota(jnp.int32, (8, AUX), 1)
    back = jnp.zeros((8, AUX), jnp.float32)
    for j, blk in enumerate(g_blocks):
        shift = lax.rem(32 * j - 32 * column + 256, 256)
        turned = pltpu.roll(blk[pl.ds(80, 8), :], shift, 1)
        back = jnp.where(lane // 32 == j, turned, back)
    slots[...] = back
    g_lane = lax.broadcasted_iota(jnp.int32, (16, AUX), 0).astype(jnp.float32)
    g_ids = jnp.concatenate([g_lane + (16 * meta[8 + j]).astype(jnp.float32) for j in range(8)], axis=0)
    for i, blk in enumerate(f_blocks):
        f_ids = g_lane + (16 * meta[4 + i]).astype(jnp.float32)
        f_plane = meta[16 + i]

        def table_of(row_f, row_g):
            odd = (row_f + row_g) - 2.0 * jnp.floor((row_f + row_g) * 0.5)
            less = (row_f < row_g).astype(jnp.float32)
            use = (odd == less) & (row_f != row_g)
            row_f = jnp.where(use, row_f, -1.0)
            left = (row_f == f_ids).astype(jnp.float32).astype(jnp.bfloat16)
            right = (row_g == g_ids).astype(jnp.float32).astype(jnp.bfloat16)
            return lax.dot_general(left, right, (((1,), (1,)), ((), ())), preferred_element_type=jnp.float32)

        there = table_of(blk[pl.ds(80 + plane, 1), :], blk[pl.ds(84 + plane, 1), :])
        back_i = table_of(slots[pl.ds(4 + f_plane, 1), :], slots[pl.ds(f_plane, 1), :])
        counts[pl.ds(16 * i, 16), :] = there + back_i
        sizes = blk[pl.ds(88, 1), :]
        eye = lax.broadcasted_iota(jnp.int32, (16, AUX), 0) == lax.broadcasted_iota(jnp.int32, (16, AUX), 1)
        size_col = jnp.sum(jnp.where(eye, sizes, 0.0), axis=1, keepdims=True)
        many = jnp.floor((size_col + (CHUNK - 1)) * (1.0 / CHUNK))
        chunks[pl.ds(16 * i, 16), :] = jnp.broadcast_to(many, (16, 128))

    most = jnp.max(counts[...]).astype(jnp.int32)
    safe = jnp.min(lowest) >= WIDTH_FLOOR
    row8 = lax.broadcasted_iota(jnp.int32, (8, 128), 0)

    lane8 = lax.broadcasted_iota(jnp.int32, (8, 128), 1)
    sizes = jnp.zeros((8, 128), jnp.float32)
    for j, blk in enumerate(g_blocks):
        part = blk[pl.ds(88, 8), 0:128]
        part = part if j == 0 else pltpu.roll(part, 16 * j, 1)
        sizes = jnp.where(lane8 // 16 == j, part, sizes)
    slots[:, 0:128] = sizes
    is_wide = jnp.where(jnp.broadcast_to(slots[pl.ds(0, 1), 0:128], (8, 128)) > 128.0, 1.0, 0.0)
    per_tile = jnp.where(is_wide > 0.0, float(WIDE), float(NARROW))
    contract = (((1,), (1,)), ((), ()))

    blank = jnp.zeros((128 - DEPTH, 128), jnp.bfloat16)
    none = jnp.zeros((128, 128), jnp.bfloat16)

    def chunks_of(code, take):
        g, q = code & 127, code >> 7
        views = [table.at[q + v, :, pl.ds(g, 1)] for v in range(take // WIDE)]
        at = [views[u // WIDE][u % WIDE, 0] for u in range(take)]
        times = at[0] >> 10
        return g, times, [e & 1023 if u % WIDE == 0 else e for u, e in enumerate(at)]

    def distances(g, at, kind):
        block = rhs[pl.ds(pl.multiple_of(g * 16, 16), 16), :]
        left = jnp.concatenate([lhs[e] for e in at[:4]], axis=0)
        if kind == "narrow":
            left = jnp.concatenate([left, jnp.concatenate([lhs[e] for e in at[4:]], axis=0)], axis=1)
            thin = block[:, :128]
            right = jnp.concatenate([thin, thin, thin, blank], axis=0)
            right = jnp.concatenate([jnp.concatenate([right, none], axis=1), jnp.concatenate([none, right], axis=1)], axis=0)
        else:
            right = jnp.concatenate([block, block, block, jnp.concatenate([blank, blank], axis=1)], axis=0)
        return jnp.dot(left, right, preferred_element_type=jnp.float32)

    def gather(at):
        return jnp.concatenate([rows_c[e] for e in at], axis=0)

    def fold(value):
        return jnp.sum(value.reshape(-1, 8, 128), axis=0)

    def apply(kern, kind, g, times, at):
        times = times.astype(jnp.float32)
        base = pl.multiple_of(g * 16, 16)
        load = pl.multiple_of(g * 8, 8)
        k0, k1 = kern[:, :128], kern[:, 128:]
        weight = cols_c[pl.ds(load, 1), :] * times
        if kind == "narrow":
            second = fold(k0 * gather(at[:4]) + k1 * gather(at[4:]))
            cols_s[pl.ds(base, 8), :] = cols_s[pl.ds(base, 8), :] + second * times
            first = [k[u * CHUNK:(u + 1) * CHUNK] * weight for k in (k0, k1) for u in range(4)]
        else:
            coef = gather(at)
            cols_s[pl.ds(base, 8), :] = cols_s[pl.ds(base, 8), :] + fold(k0 * coef) * times
            cols_s[pl.ds(base + 8, 8), :] = cols_s[pl.ds(base + 8, 8), :] + fold(k1 * coef) * times
            both = k0 * weight + k1 * (cols_c[pl.ds(load + 1, 1), :] * times)
            first = [both[u * CHUNK:(u + 1) * CHUNK] for u in range(4)]
        sums = [rows_s[e] for e in at]
        for e, value, more in zip(at, sums, first):
            rows_s[e] = value + more

    def exact(code):
        g, times, at = chunks_of(code, WIDE)
        left = jnp.concatenate([lhs[e] for e in at], axis=0)
        part = rhs[pl.ds(pl.multiple_of(g * 16, 16), 16), :].astype(jnp.float32)
        wide = spread(left, 21, 23, 1.0)
        dist = jnp.concatenate([wide, wide], axis=1) + width_row(g)
        for k in range(3):
            mine = jnp.where(((pick % 16 == k) & (pick < DEPTH)), -0.5, 0.0).astype(jnp.bfloat16)
            mine = jnp.dot(left, mine, preferred_element_type=jnp.float32)
            other = part[k:k + 1] + part[8 + k:9 + k] + part[12 + k:13 + k]
            gap = jnp.concatenate([mine, mine], axis=1) - other
            dist = dist + gap * gap
        apply(lax.rsqrt(dist), "wide", g, times, at)

    def width_row(g):
        row = jnp.zeros((1, AUX), jnp.float32)
        for k, blk in enumerate(g_blocks):
            row = jnp.where(g // 16 == k, blk[pl.ds(48 + g % 16, 1), :], row)
        return row

    def one_round(state):
        r, _ = state
        groups = SPAN // 8
        at = [(row8 + 8 * t + SPAN * r).astype(jnp.float32) for t in range(groups)]

        def one_class(m, state):
            vals, times, total = state
            times = tuple(jnp.where(a >= total, m.astype(jnp.float32), v) for a, v in zip(at, times))

            def scan(f, state):
                vals, total = state
                many = jnp.broadcast_to(chunks[pl.ds(f, 1), :], (8, 128))
                listed = jnp.broadcast_to(counts[pl.ds(f, 1), :], (8, 128))
                mark = (many + f.astype(jnp.float32) * 16.0) * 4096.0 + total
                vals = tuple(jnp.where(a >= total, mark, v) for a, v in zip(at, vals))
                return vals, total + jnp.where(listed == m.astype(jnp.float32), many, 0.0)

            vals, total = lax.fori_loop(0, NF, scan, (vals, total), unroll=8)
            vals = tuple(jnp.where(a >= total, -1.0, v) for a, v in zip(at, vals))
            total = jnp.floor((total + per_tile - 1.0) / per_tile) * per_tile
            return vals, times, total

        flat = zeros_v[...]
        none = (flat,) * groups
        vals, times, total = lax.fori_loop(1, most + 1, one_class, (none, none, flat))
        for t in range(groups):
            code = jnp.floor(vals[t] * (1.0 / 4096.0))
            offset = at[t] - (vals[t] - 4096.0 * code)
            frag = jnp.floor(code * (1.0 / 16.0))
            entry = jnp.where((vals[t] >= 0.0) & (at[t] < total), frag * CPF + offset, float(DUMMY))
            places[0, pl.ds(8 * t, 8), :] = entry
            places[1, pl.ds(8 * t, 8), :] = times[t]
        groups4 = SPAN // WIDE
        for u in range(WIDE):
            value = places.at[0][pl.ds(u, groups4, stride=WIDE), :]
            if u == 0:
                value = value + 1024.0 * places.at[1][pl.ds(u, groups4, stride=WIDE), :]
            table_v[pl.ds(0, groups4), u, :] = value.astype(jnp.int32)
        table_v[pl.ds(groups4, 2)] = jnp.full((2, WIDE, 128), DUMMY, jnp.int32)
        left_over = jnp.clip(total - (SPAN * r).astype(jnp.float32), 0.0, float(SPAN))
        tiles = left_over / per_tile
        tiles_wide = tiles * is_wide
        tiles_thin = tiles - tiles_wide
        for k, tiles in enumerate((tiles_wide, tiles_thin)):
            ends[k] = lax.dot_general(upto, jnp.concatenate([tiles] * 16, axis=0).astype(jnp.bfloat16), contract, preferred_element_type=jnp.float32)
        number = [(lane8 + 128 * row8 + 1024 * k).astype(jnp.float32) for k in range(WIDE_ROWS // 8)]
        kinds = [(0, k) for k in range(WIDE_ROWS // 8)] + [(1, k) for k in range(THIN_ROWS // 8)]

        def seek(c, state):
            out = []
            column = (c + 1).astype(jnp.float32)
            edges = [jnp.broadcast_to(ends.at[n][pl.ds(c, 1), :], (8, 128)) for n in range(2)]
            for (thin, k), (where, begin) in zip(kinds, state):
                end = edges[thin]
                hit = number[k] >= end
                out.append((jnp.where(hit, column, where), jnp.where(hit, end, begin)))
            return tuple(out)

        found = lax.fori_loop(0, NG, seek, ((flat, flat),) * len(kinds), unroll=16)
        for (thin, k), (where, begin) in zip(kinds, found):
            place = (number[k] - begin) * (128.0 * (1 + thin)) + where
            place = jnp.where(where < float(NG), place, float(groups4 * 128))
            tiles_v[pl.ds(thin * WIDE_ROWS + 8 * k, 8), :] = place.astype(jnp.int32)
        info = jnp.where(row8 == 0, jnp.sum(tiles_wide, axis=1, keepdims=True), jnp.sum(tiles_thin, axis=1, keepdims=True))
        tiles_v[pl.ds(LIST_ROWS, 8), :] = info.astype(jnp.int32)
        longest = jnp.max(total).astype(jnp.int32)
        copies = [pltpu.make_async_copy(table_v, table, sem.at[0]), pltpu.make_async_copy(tiles_v, tile_list, sem.at[1])]
        for copy in copies:
            copy.start()
        for copy in copies:
            copy.wait()
        count_wide, count_thin = tile_list[LIST_ROWS, 0], tile_list[LIST_ROWS + 1, 0]

        def many_tiles(kind, first_row, count):
            take = NARROW if kind == "narrow" else WIDE

            def body(b, _):
                row, col = first_row + lax.shift_right_logical(b, SHIFT), (b & (128 // BATCH - 1)) * BATCH
                for u in range(BATCH):
                    g, times, at = chunks_of(tile_list[row, col + u], take)
                    apply(lax.rsqrt(distances(g, at, kind)), kind, g, times, at)
                return 0

            lax.fori_loop(0, (count + (BATCH - 1)) // BATCH, body, 0)

        @pl.when(safe)
        def _():
            many_tiles("wide", 0, count_wide)
            many_tiles("narrow", WIDE_ROWS, count_thin)

        @pl.when(jnp.logical_not(safe))
        def _():
            def wide_one(t, _):
                exact(tile_list[t >> 7, t & 127])
                return 0

            def thin_one(t, _):
                exact(tile_list[WIDE_ROWS + (t >> 8), (t & 255) >> 1] + 128 * (t & 1))
                return 0

            lax.fori_loop(0, count_wide, wide_one, 0)
            lax.fori_loop(0, 2 * count_thin, thin_one, 0)

        return r + 1, longest

    zeros_v[...] = jnp.zeros_like(zeros_v)
    upto = (lax.broadcasted_iota(jnp.int32, (128, 128), 1) <= pick).astype(jnp.float32).astype(jnp.bfloat16)
    lax.while_loop(lambda state: state[0] * SPAN < state[1], one_round, (jnp.int32(0), jnp.int32(1)))

    ones8 = jnp.ones((8, 256), jnp.bfloat16)

    def collect(f, _):
        value = rows_s[pl.ds(f * CPF, CPF)].reshape(AUX, 128)
        high = value.astype(jnp.bfloat16)
        low = (value - high.astype(jnp.float32)).astype(jnp.bfloat16)
        row = lax.dot_general(ones8, jnp.concatenate([high, low], axis=1), contract, preferred_element_type=jnp.float32)
        for h in range(2):
            row_sums[h, pl.ds(f, 1), :] = row[0:1, 128 * h:128 * h + 128]
        return 0

    lax.fori_loop(0, NF, collect, 0, unroll=16)
    rows_out = jnp.concatenate([row_sums[0], row_sums[1]], axis=1)
    outf_own[...] = rows_out[0:16]
    outf_near[...] = rows_out[16:32]
    outf_far[...] = rows_out[32:64]
    cols = []
    for h in range(2):
        half = cols_s[pl.ds(8 * h, NG, stride=16), :]
        for r in range(1, 8):
            half = half + cols_s[pl.ds(8 * h + r, NG, stride=16), :]
        cols.append(half)
    cols = jnp.concatenate(cols, axis=1)
    out_own[...] = cols[0:16]
    out_near[...] = cols[16:32]
    out_far[...] = cols[32:64]
    out_sib[...] = cols[64:128]


def rectangle(meta, packets):
    vmem = pl.BlockSpec(memory_space=pltpu.VMEM)
    shape = lambda rows: jax.ShapeDtypeStruct((rows, AUX), jnp.float32)
    return pl.pallas_call(
        pair_kernel,
        out_shape=(shape(64), shape(32), shape(16), shape(16), shape(32), shape(16), shape(16)),
        in_specs=[pl.BlockSpec(memory_space=pltpu.SMEM)] + [vmem] * 11,
        out_specs=(vmem,) * 7,
        scratch_shapes=[
            pltpu.VMEM((DUMMY + 1, CHUNK, 128), jnp.bfloat16),
            pltpu.VMEM((DUMMY + 1, CHUNK, 128), jnp.float32),
            pltpu.VMEM((DUMMY + 1, CHUNK, 128), jnp.float32),
            pltpu.VMEM((NG * 16, 128), jnp.float32),
            pltpu.VMEM((NG * 8, 128), jnp.float32),
            pltpu.VMEM((NG * 16, AUX), jnp.bfloat16),
            pltpu.VMEM((2, DEPTH * 16, 128), jnp.float32),
            pltpu.VMEM((8, AUX), jnp.float32),
            pltpu.VMEM((NF, 128), jnp.float32),
            pltpu.VMEM((NF, 128), jnp.float32),
            pltpu.VMEM((8, 128), jnp.float32),
            pltpu.VMEM((2, SPAN, 128), jnp.float32),
            pltpu.VMEM((2, 128, 128), jnp.float32),
            pltpu.VMEM((SPAN // WIDE + 2, WIDE, 128), jnp.int32),
            pltpu.VMEM((LIST_ROWS + 8, 128), jnp.int32),
            pltpu.VMEM((2, NF, 128), jnp.float32),
            pltpu.SMEM((SPAN // WIDE + 2, WIDE, 128), jnp.int32),
            pltpu.SMEM((LIST_ROWS + 8, 128), jnp.int32),
            pltpu.SemaphoreType.DMA((2,)),
        ],
        compiler_params=pltpu.CompilerParams(vmem_limit_bytes=56 * 2**20),
    )(meta, *packets)


def index_of(z, x, c):
    return (z * 4 + x) * 2 + c


def partners(move):
    return [
        (index_of(z, x, c), index_of(*move(z, x, c)))
        for z in range(4) for x in range(4) for c in range(2)
    ]


X_NEAR = partners(lambda z, x, c: (z, x ^ 1, c))
X_FAR = partners(lambda z, x, c: (z, 3 - x, c))
Z_NEAR = partners(lambda z, x, c: (z ^ 1, x, c))
Z_FAR = partners(lambda z, x, c: (3 - z, x, c))
CORE = partners(lambda z, x, c: (z, x, c ^ 1))


def swap(array, pairs):
    return lax.ppermute(array, "frag", pairs)


def local(coeffs, centres, frag_sizes, pairs):
    me = lax.axis_index("frag")
    z, x, c = me // 8, (me // 2) % 4, me % 2
    mask = (jnp.arange(AUX, dtype=jnp.int32)[None, :] < frag_sizes[:, None]).astype(jnp.float32)
    packet = jnp.concatenate(
        [
            centres.transpose(1, 0, 2).reshape(4 * FRAG_DEV, AUX),
            coeffs * mask,
            pairs.T.reshape(8, AUX).astype(jnp.float32),
            jnp.pad(frag_sizes.astype(jnp.float32)[None, :], ((0, 7), (0, AUX - FRAG_DEV))),
        ],
        axis=0,
    )
    zs = jnp.stack([z, z ^ 1, 3 - z, (3 - z) ^ 1])
    xs = jnp.stack([x, x ^ 1, 3 - x, (3 - x) ^ 1])
    f_dev = index_of(zs, x, c)
    g_dev = jnp.concatenate([index_of(z, xs, c), index_of(z, xs, c ^ 1)])
    zero = jnp.zeros((2,), jnp.int32)
    meta = jnp.concatenate([jnp.stack([z, 2 * x + c]), zero, f_dev, g_dev, zs]).astype(jnp.int32)

    x_near = swap(packet, X_NEAR)
    z_near = swap(packet, Z_NEAR)
    x_far = swap(packet, X_FAR)
    z_far = swap(packet, Z_FAR)
    x_last = swap(x_near, X_FAR)
    z_last = swap(z_near, Z_FAR)
    own_c = swap(packet, CORE)
    near_c = swap(x_near, CORE)
    far_c = swap(x_far, CORE)
    last_c = swap(x_last, CORE)

    g_sib, g_far, g_near, g_own, f_far, f_near, f_own = rectangle(
        meta,
        (packet, z_near, z_far, z_last, x_near, x_far, x_last, own_c, near_c, far_c, last_c),
    )
    f_back = swap(f_far, Z_FAR)
    sib_back = swap(g_sib, CORE)
    far_back = swap(g_far + sib_back[32:], X_FAR)
    f_last = swap(f_near + f_back[16:], Z_NEAR)
    near_back = swap(g_near + sib_back[16:32] + far_back[16:], X_NEAR)
    total = f_own + f_back[:16] + f_last + g_own + sib_back[:16] + far_back[:16] + near_back
    return total * mask


def solution(mesh):
    return jax.shard_map(
        local,
        mesh=mesh,
        in_specs=(
            P(("cplx", "frag"), None),
            P(("cplx", "frag"), None, None),
            P(("cplx", "frag")),
            P(("cplx", "frag"), None),
        ),
        out_specs=P(("cplx", "frag"), None),
        check_vma=False,
    )
```

```python
import functools

import jax
import jax.numpy as jnp
from jax import lax
from jax.experimental import pallas as pl
from jax.experimental.pallas import tpu as pltpu
from jax.sharding import PartitionSpec as P

FRAG_DEV = 16
AUX = 256
ROWS = 96
NF = 64
NG = 128
CHUNK = 32
CPF = AUX // CHUNK
WIDE = 4
NARROW = 8
SPAN = 96
WIDE_ROWS = 24
THIN_ROWS = 16
LIST_ROWS = WIDE_ROWS + THIN_ROWS
DUMMY = NF * CPF
DEPTH = 48
BATCH = 16
SHIFT = 3
WIDTH_FLOOR = 1.0 / 32.0


def pieces(value):
    first = value.astype(jnp.bfloat16).astype(jnp.float32)
    rest = value - first
    second = rest.astype(jnp.bfloat16).astype(jnp.float32)
    return first, second, rest - second


def pack_kernel(coeffs, centres, sizes, pairs, out):
    for k in range(4):
        out[pl.ds(16 * k, 16), :] = centres[:, k, :]
    row = sizes[...].astype(jnp.float32)
    square = (FRAG_DEV, FRAG_DEV)
    eye = lax.broadcasted_iota(jnp.int32, square, 0) == lax.broadcasted_iota(jnp.int32, square, 1)
    column = jnp.sum(jnp.where(eye, row, 0.0), axis=1, keepdims=True)
    lane = lax.broadcasted_iota(jnp.int32, (FRAG_DEV, AUX), 1).astype(jnp.float32)
    out[pl.ds(64, 16), :] = coeffs[...] * (lane < column).astype(jnp.float32)
    out[pl.ds(88, 8), :] = jnp.zeros((8, AUX), jnp.float32)
    out[pl.ds(88, 1), 0:FRAG_DEV] = row
    for r in range(8):
        out[pl.ds(80 + r, 1), :] = pairs[r // 4:r // 4 + 1, AUX * (r % 4):AUX * (r % 4) + AUX].astype(jnp.float32)


def pair_kernel(*refs):
    sources, refs = refs[:11], refs[11:]
    out_sib, out_far, out_near, out_own, outf_far, outf_near, outf_own = refs[:7]
    (lhs, rows_c, rows_s, cols_s, cols_c, rhs, build, slots, counts, chunks, zeros_v, places, ends,
     table_v, tiles_v, row_sums, table, tile_list, sem) = refs[7:26]
    packets, arrived = refs[26:37], refs[37]
    loads = [pltpu.make_async_copy(a, b, arrived.at[k]) for k, (a, b) in enumerate(zip(sources, packets))]
    for load in loads:
        load.start()
    f_blocks = [packets[0], packets[1], packets[2], packets[3]]
    g_blocks = [packets[0]] + list(packets[4:])
    me = lax.axis_index("frag")
    plane, column = lax.div(me, 8), lax.rem(me, 8)
    zs = [plane, plane ^ 1, 3 - plane, (3 - plane) ^ 1]
    f_devs = [8 * at + column for at in zs]
    line, core = lax.div(column, 2), lax.rem(column, 2)
    xs = [line, line ^ 1, 3 - line, (3 - line) ^ 1]
    g_devs = [8 * plane + 2 * at + c for c in (core, 1 - core) for at in xs]

    def put_rows(r, value):
        for h in range(2):
            build[h, pl.ds(r * 16, 16), :] = value[:, 128 * h:128 * h + 128]

    def take_rows(h, at, count):
        return build.at[h][pl.ds(at, count, stride=16), :]

    lowest = None
    for i, blk in enumerate(f_blocks):
        loads[i].wait()
        x, y, z, w, c = (blk[pl.ds(16 * k, 16), :] for k in range(5))
        lowest = w if lowest is None else jnp.minimum(lowest, w)
        s = x * x + y * y + z * z + w
        one = jnp.ones_like(x)
        zero = jnp.zeros_like(x)
        px, py, pz = pieces(-2.0 * x), pieces(-2.0 * y), pieces(-2.0 * z)
        ps, pw, pc = pieces(s), pieces(w), pieces(c)
        for k in range(3):
            delta = one if k == 0 else zero
            extra = pc if k == 0 else (pw if k == 1 else (zero, zero, zero))
            rows = [px[k], py[k], pz[k], delta, ps[k], *extra,
                    px[k], py[k], pz[k], delta, px[k], py[k], pz[k], delta]
            for r, value in enumerate(rows):
                put_rows(16 * k + r, value)

        def one_row(lf, _, i=i):
            for h in range(2):
                feats = take_rows(h, lf, DEPTH).T
                feats = jnp.concatenate([feats, jnp.zeros((128, 128 - DEPTH), jnp.float32)], axis=1)
                lhs[pl.ds((i * 16 + lf) * CPF + 4 * h, 4)] = feats.astype(jnp.bfloat16).reshape(4, CHUNK, 128)
            return 0

        lax.fori_loop(0, 16, one_row, 0, unroll=16)
    spare_lane = lax.broadcasted_iota(jnp.int32, (CHUNK, 128), 1)
    lhs[DUMMY] = (spare_lane == 4).astype(jnp.float32).astype(jnp.bfloat16)

    pick = lax.broadcasted_iota(jnp.int32, (128, 128), 0)

    def spread(rows, lo, hi, scale):
        sel = jnp.where((pick >= lo) & (pick <= hi), scale, 0.0)
        return jnp.dot(rows, sel.astype(jnp.bfloat16), preferred_element_type=jnp.float32)

    def one_spread(f, _):
        value = spread(lhs[pl.ds(f * CPF, CPF)].reshape(AUX, 128), 5, 7, 1.0)
        rows_c[pl.ds(f * CPF, CPF)] = value.reshape(CPF, CHUNK, 128)
        rows_s[pl.ds(f * CPF, CPF)] = jnp.zeros((CPF, CHUNK, 128), jnp.float32)
        return 0

    lax.fori_loop(0, NF, one_spread, 0, unroll=16)
    rows_c[DUMMY] = jnp.zeros((CHUNK, 128), jnp.float32)
    rows_s[DUMMY] = jnp.zeros((CHUNK, 128), jnp.float32)

    for load in loads[4:]:
        load.wait()
    for j, blk in enumerate(g_blocks):
        x, y, z, w, c = (blk[pl.ds(16 * k, 16), :] for k in range(5))
        lowest = jnp.minimum(lowest, w)
        s = x * x + y * y + z * z + w
        one = jnp.ones_like(x)
        zero = jnp.zeros_like(x)
        px, py, pz, ps = pieces(x), pieces(y), pieces(z), pieces(s)
        rows = [px[0], py[0], pz[0], ps[0], one, zero, zero, zero,
                px[1], py[1], pz[1], ps[1], px[2], py[2], pz[2], ps[2]]
        for r, value in enumerate(rows):
            put_rows(r, value)

        def one_column(lg, _, j=j, blk=blk):
            start = pl.multiple_of((j * 16 + lg) * 16, 16)
            load = pl.multiple_of((j * 16 + lg) * 8, 8)
            cols_s[pl.ds(start, 16), :] = jnp.zeros((16, 128), jnp.float32)
            coef = blk[pl.ds(64 + lg, 1), :]
            for h in range(2):
                cols_c[pl.ds(load + h, 1), :] = coef[:, 128 * h:128 * h + 128]
            rhs[pl.ds(start, 16), :] = jnp.concatenate([take_rows(h, lg, 16) for h in range(2)], axis=1).astype(jnp.bfloat16)
            return 0

        lax.fori_loop(0, 16, one_column, 0, unroll=16)

    lane = lax.broadcasted_iota(jnp.int32, (8, AUX), 1)
    back = jnp.zeros((8, AUX), jnp.float32)
    for j, blk in enumerate(g_blocks):
        shift = lax.rem(32 * j - 32 * column + 256, 256)
        turned = pltpu.roll(blk[pl.ds(80, 8), :], shift, 1)
        back = jnp.where(lane // 32 == j, turned, back)
    slots[...] = back
    g_lane = lax.broadcasted_iota(jnp.int32, (16, AUX), 0).astype(jnp.float32)
    g_ids = jnp.concatenate([g_lane + (16 * g_devs[j]).astype(jnp.float32) for j in range(8)], axis=0)
    for i, blk in enumerate(f_blocks):
        f_ids = g_lane + (16 * f_devs[i]).astype(jnp.float32)
        f_plane = zs[i]

        def table_of(row_f, row_g):
            odd = (row_f + row_g) - 2.0 * jnp.floor((row_f + row_g) * 0.5)
            less = (row_f < row_g).astype(jnp.float32)
            use = (odd == less) & (row_f != row_g)
            row_f = jnp.where(use, row_f, -1.0)
            left = (row_f == f_ids).astype(jnp.float32).astype(jnp.bfloat16)
            right = (row_g == g_ids).astype(jnp.float32).astype(jnp.bfloat16)
            return lax.dot_general(left, right, (((1,), (1,)), ((), ())), preferred_element_type=jnp.float32)

        there = table_of(blk[pl.ds(80 + plane, 1), :], blk[pl.ds(84 + plane, 1), :])
        back_i = table_of(slots[pl.ds(4 + f_plane, 1), :], slots[pl.ds(f_plane, 1), :])
        counts[pl.ds(16 * i, 16), :] = there + back_i
        sizes = blk[pl.ds(88, 1), :]
        eye = lax.broadcasted_iota(jnp.int32, (16, AUX), 0) == lax.broadcasted_iota(jnp.int32, (16, AUX), 1)
        size_col = jnp.sum(jnp.where(eye, sizes, 0.0), axis=1, keepdims=True)
        many = jnp.floor((size_col + (CHUNK - 1)) * (1.0 / CHUNK))
        chunks[pl.ds(16 * i, 16), :] = jnp.broadcast_to(many, (16, 128))

    most = jnp.max(counts[...]).astype(jnp.int32)
    safe = jnp.min(lowest) >= WIDTH_FLOOR
    row8 = lax.broadcasted_iota(jnp.int32, (8, 128), 0)

    lane8 = lax.broadcasted_iota(jnp.int32, (8, 128), 1)
    sizes = jnp.zeros((8, 128), jnp.float32)
    for j, blk in enumerate(g_blocks):
        part = blk[pl.ds(88, 8), 0:128]
        part = part if j == 0 else pltpu.roll(part, 16 * j, 1)
        sizes = jnp.where(lane8 // 16 == j, part, sizes)
    slots[:, 0:128] = sizes
    is_wide = jnp.where(jnp.broadcast_to(slots[pl.ds(0, 1), 0:128], (8, 128)) > 128.0, 1.0, 0.0)
    per_tile = jnp.where(is_wide > 0.0, float(WIDE), float(NARROW))
    contract = (((1,), (1,)), ((), ()))

    blank = jnp.zeros((128 - DEPTH, 128), jnp.bfloat16)
    none = jnp.zeros((128, 128), jnp.bfloat16)

    def chunks_of(code, take):
        g, q = code & 127, code >> 7
        views = [table.at[q + v, :, pl.ds(g, 1)] for v in range(take // WIDE)]
        at = [views[u // WIDE][u % WIDE, 0] for u in range(take)]
        times = at[0] >> 10
        return g, times, [e & 1023 if u % WIDE == 0 else e for u, e in enumerate(at)]

    def distances(g, at, kind):
        block = rhs[pl.ds(pl.multiple_of(g * 16, 16), 16), :]
        left = jnp.concatenate([lhs[e] for e in at[:4]], axis=0)
        if kind == "narrow":
            left = jnp.concatenate([left, jnp.concatenate([lhs[e] for e in at[4:]], axis=0)], axis=1)
            thin = block[:, :128]
            right = jnp.concatenate([thin, thin, thin, blank], axis=0)
            right = jnp.concatenate([jnp.concatenate([right, none], axis=1), jnp.concatenate([none, right], axis=1)], axis=0)
        else:
            right = jnp.concatenate([block, block, block, jnp.concatenate([blank, blank], axis=1)], axis=0)
        return jnp.dot(left, right, preferred_element_type=jnp.float32)

    def gather(at):
        return jnp.concatenate([rows_c[e] for e in at], axis=0)

    def fold(value):
        return jnp.sum(value.reshape(-1, 8, 128), axis=0)

    def apply(kern, kind, g, times, at):
        times = times.astype(jnp.float32)
        base = pl.multiple_of(g * 16, 16)
        load = pl.multiple_of(g * 8, 8)
        k0, k1 = kern[:, :128], kern[:, 128:]
        weight = cols_c[pl.ds(load, 1), :] * times
        if kind == "narrow":
            second = fold(k0 * gather(at[:4]) + k1 * gather(at[4:]))
            cols_s[pl.ds(base, 8), :] = cols_s[pl.ds(base, 8), :] + second * times
            first = [k[u * CHUNK:(u + 1) * CHUNK] * weight for k in (k0, k1) for u in range(4)]
        else:
            coef = gather(at)
            cols_s[pl.ds(base, 8), :] = cols_s[pl.ds(base, 8), :] + fold(k0 * coef) * times
            cols_s[pl.ds(base + 8, 8), :] = cols_s[pl.ds(base + 8, 8), :] + fold(k1 * coef) * times
            both = k0 * weight + k1 * (cols_c[pl.ds(load + 1, 1), :] * times)
            first = [both[u * CHUNK:(u + 1) * CHUNK] for u in range(4)]
        sums = [rows_s[e] for e in at]
        for e, value, more in zip(at, sums, first):
            rows_s[e] = value + more

    def exact(code):
        g, times, at = chunks_of(code, WIDE)
        left = jnp.concatenate([lhs[e] for e in at], axis=0)
        part = rhs[pl.ds(pl.multiple_of(g * 16, 16), 16), :].astype(jnp.float32)
        wide = spread(left, 21, 23, 1.0)
        dist = jnp.concatenate([wide, wide], axis=1) + width_row(g)
        for k in range(3):
            mine = jnp.where(((pick % 16 == k) & (pick < DEPTH)), -0.5, 0.0).astype(jnp.bfloat16)
            mine = jnp.dot(left, mine, preferred_element_type=jnp.float32)
            other = part[k:k + 1] + part[8 + k:9 + k] + part[12 + k:13 + k]
            gap = jnp.concatenate([mine, mine], axis=1) - other
            dist = dist + gap * gap
        apply(lax.rsqrt(dist), "wide", g, times, at)

    def width_row(g):
        row = jnp.zeros((1, AUX), jnp.float32)
        for k, blk in enumerate(g_blocks):
            row = jnp.where(g // 16 == k, blk[pl.ds(48 + g % 16, 1), :], row)
        return row

    def one_round(state):
        r, _ = state
        groups = SPAN // 8
        at = [(row8 + 8 * t + SPAN * r).astype(jnp.float32) for t in range(groups)]

        def one_class(m, state):
            vals, times, total = state
            times = tuple(jnp.where(a >= total, m.astype(jnp.float32), v) for a, v in zip(at, times))

            def scan(f, state):
                vals, total = state
                many = jnp.broadcast_to(chunks[pl.ds(f, 1), :], (8, 128))
                listed = jnp.broadcast_to(counts[pl.ds(f, 1), :], (8, 128))
                mark = (many + f.astype(jnp.float32) * 16.0) * 4096.0 + total
                vals = tuple(jnp.where(a >= total, mark, v) for a, v in zip(at, vals))
                return vals, total + jnp.where(listed == m.astype(jnp.float32), many, 0.0)

            vals, total = lax.fori_loop(0, NF, scan, (vals, total), unroll=8)
            vals = tuple(jnp.where(a >= total, -1.0, v) for a, v in zip(at, vals))
            total = jnp.floor((total + per_tile - 1.0) / per_tile) * per_tile
            return vals, times, total

        flat = zeros_v[...]
        none = (flat,) * groups
        vals, times, total = lax.fori_loop(1, most + 1, one_class, (none, none, flat))
        for t in range(groups):
            code = jnp.floor(vals[t] * (1.0 / 4096.0))
            offset = at[t] - (vals[t] - 4096.0 * code)
            frag = jnp.floor(code * (1.0 / 16.0))
            entry = jnp.where((vals[t] >= 0.0) & (at[t] < total), frag * CPF + offset, float(DUMMY))
            places[0, pl.ds(8 * t, 8), :] = entry
            places[1, pl.ds(8 * t, 8), :] = times[t]
        groups4 = SPAN // WIDE
        for u in range(WIDE):
            value = places.at[0][pl.ds(u, groups4, stride=WIDE), :]
            if u == 0:
                value = value + 1024.0 * places.at[1][pl.ds(u, groups4, stride=WIDE), :]
            table_v[pl.ds(0, groups4), u, :] = value.astype(jnp.int32)
        table_v[pl.ds(groups4, 2)] = jnp.full((2, WIDE, 128), DUMMY, jnp.int32)
        left_over = jnp.clip(total - (SPAN * r).astype(jnp.float32), 0.0, float(SPAN))
        tiles = left_over / per_tile
        tiles_wide = tiles * is_wide
        tiles_thin = tiles - tiles_wide
        for k, tiles in enumerate((tiles_wide, tiles_thin)):
            ends[k] = lax.dot_general(upto, jnp.concatenate([tiles] * 16, axis=0).astype(jnp.bfloat16), contract, preferred_element_type=jnp.float32)
        number = [(lane8 + 128 * row8 + 1024 * k).astype(jnp.float32) for k in range(WIDE_ROWS // 8)]
        kinds = [(0, k) for k in range(WIDE_ROWS // 8)] + [(1, k) for k in range(THIN_ROWS // 8)]

        def seek(c, state):
            out = []
            column = (c + 1).astype(jnp.float32)
            edges = [jnp.broadcast_to(ends.at[n][pl.ds(c, 1), :], (8, 128)) for n in range(2)]
            for (thin, k), (where, begin) in zip(kinds, state):
                end = edges[thin]
                hit = number[k] >= end
                out.append((jnp.where(hit, column, where), jnp.where(hit, end, begin)))
            return tuple(out)

        found = lax.fori_loop(0, NG, seek, ((flat, flat),) * len(kinds), unroll=16)
        for (thin, k), (where, begin) in zip(kinds, found):
            place = (number[k] - begin) * (128.0 * (1 + thin)) + where
            place = jnp.where(where < float(NG), place, float(groups4 * 128))
            tiles_v[pl.ds(thin * WIDE_ROWS + 8 * k, 8), :] = place.astype(jnp.int32)
        info = jnp.where(row8 == 0, jnp.sum(tiles_wide, axis=1, keepdims=True), jnp.sum(tiles_thin, axis=1, keepdims=True))
        tiles_v[pl.ds(LIST_ROWS, 8), :] = info.astype(jnp.int32)
        longest = jnp.max(total).astype(jnp.int32)
        copies = [pltpu.make_async_copy(table_v, table, sem.at[0]), pltpu.make_async_copy(tiles_v, tile_list, sem.at[1])]
        for copy in copies:
            copy.start()
        for copy in copies:
            copy.wait()
        count_wide, count_thin = tile_list[LIST_ROWS, 0], tile_list[LIST_ROWS + 1, 0]

        def many_tiles(kind, first_row, count):
            take = NARROW if kind == "narrow" else WIDE

            def body(b, _):
                row, col = first_row + lax.shift_right_logical(b, SHIFT), (b & (128 // BATCH - 1)) * BATCH
                for u in range(BATCH):
                    g, times, at = chunks_of(tile_list[row, col + u], take)
                    apply(lax.rsqrt(distances(g, at, kind)), kind, g, times, at)
                return 0

            lax.fori_loop(0, (count + (BATCH - 1)) // BATCH, body, 0)

        @pl.when(safe)
        def _():
            many_tiles("wide", 0, count_wide)
            many_tiles("narrow", WIDE_ROWS, count_thin)

        @pl.when(jnp.logical_not(safe))
        def _():
            def wide_one(t, _):
                exact(tile_list[t >> 7, t & 127])
                return 0

            def thin_one(t, _):
                exact(tile_list[WIDE_ROWS + (t >> 8), (t & 255) >> 1] + 128 * (t & 1))
                return 0

            lax.fori_loop(0, count_wide, wide_one, 0)
            lax.fori_loop(0, 2 * count_thin, thin_one, 0)

        return r + 1, longest

    zeros_v[...] = jnp.zeros_like(zeros_v)
    upto = (lax.broadcasted_iota(jnp.int32, (128, 128), 1) <= pick).astype(jnp.float32).astype(jnp.bfloat16)
    lax.while_loop(lambda state: state[0] * SPAN < state[1], one_round, (jnp.int32(0), jnp.int32(1)))

    ones8 = jnp.ones((8, 256), jnp.bfloat16)

    def collect(f, _):
        value = rows_s[pl.ds(f * CPF, CPF)].reshape(AUX, 128)
        high = value.astype(jnp.bfloat16)
        low = (value - high.astype(jnp.float32)).astype(jnp.bfloat16)
        row = lax.dot_general(ones8, jnp.concatenate([high, low], axis=1), contract, preferred_element_type=jnp.float32)
        for h in range(2):
            row_sums[h, pl.ds(f, 1), :] = row[0:1, 128 * h:128 * h + 128]
        return 0

    lax.fori_loop(0, NF, collect, 0, unroll=16)
    rows_out = jnp.concatenate([row_sums[0], row_sums[1]], axis=1)
    outf_own[...] = rows_out[0:16]
    outf_near[...] = rows_out[16:32]
    outf_far[...] = rows_out[32:64]
    cols = []
    for h in range(2):
        half = cols_s[pl.ds(8 * h, NG, stride=16), :]
        for r in range(1, 8):
            half = half + cols_s[pl.ds(8 * h + r, NG, stride=16), :]
        cols.append(half)
    cols = jnp.concatenate(cols, axis=1)
    out_own[...] = cols[0:16]
    out_near[...] = cols[16:32]
    out_far[...] = cols[32:64]
    out_sib[...] = cols[64:128]


def rectangle(packets):
    vmem = pl.BlockSpec(memory_space=pltpu.VMEM)
    shape = lambda rows: jax.ShapeDtypeStruct((rows, AUX), jnp.float32)
    return pl.pallas_call(
        pair_kernel,
        out_shape=(shape(64), shape(32), shape(16), shape(16), shape(32), shape(16), shape(16)),
        in_specs=[pl.BlockSpec(memory_space=pl.ANY)] * 11,
        out_specs=(vmem,) * 7,
        scratch_shapes=[
            pltpu.VMEM((DUMMY + 1, CHUNK, 128), jnp.bfloat16),
            pltpu.VMEM((DUMMY + 1, CHUNK, 128), jnp.float32),
            pltpu.VMEM((DUMMY + 1, CHUNK, 128), jnp.float32),
            pltpu.VMEM((NG * 16, 128), jnp.float32),
            pltpu.VMEM((NG * 8, 128), jnp.float32),
            pltpu.VMEM((NG * 16, AUX), jnp.bfloat16),
            pltpu.VMEM((2, DEPTH * 16, 128), jnp.float32),
            pltpu.VMEM((8, AUX), jnp.float32),
            pltpu.VMEM((NF, 128), jnp.float32),
            pltpu.VMEM((NF, 128), jnp.float32),
            pltpu.VMEM((8, 128), jnp.float32),
            pltpu.VMEM((2, SPAN, 128), jnp.float32),
            pltpu.VMEM((2, 128, 128), jnp.float32),
            pltpu.VMEM((SPAN // WIDE + 2, WIDE, 128), jnp.int32),
            pltpu.VMEM((LIST_ROWS + 8, 128), jnp.int32),
            pltpu.VMEM((2, NF, 128), jnp.float32),
            pltpu.SMEM((SPAN // WIDE + 2, WIDE, 128), jnp.int32),
            pltpu.SMEM((LIST_ROWS + 8, 128), jnp.int32),
            pltpu.SemaphoreType.DMA((2,)),
        ]
        + [pltpu.VMEM((ROWS, AUX), jnp.float32)] * 11
        + [
            pltpu.SemaphoreType.DMA((11,)),
        ],
        compiler_params=pltpu.CompilerParams(vmem_limit_bytes=56 * 2**20),
    )(*packets)


def index_of(z, x, c):
    return (z * 4 + x) * 2 + c


def partners(move):
    return [
        (index_of(z, x, c), index_of(*move(z, x, c)))
        for z in range(4) for x in range(4) for c in range(2)
    ]


X_NEAR = partners(lambda z, x, c: (z, x ^ 1, c))
X_FAR = partners(lambda z, x, c: (z, 3 - x, c))
Z_NEAR = partners(lambda z, x, c: (z ^ 1, x, c))
Z_FAR = partners(lambda z, x, c: (3 - z, x, c))
X_LAST = partners(lambda z, x, c: (z, x ^ 2, c))
Z_LAST = partners(lambda z, x, c: (z ^ 2, x, c))
CORE = partners(lambda z, x, c: (z, x, c ^ 1))


def swap(array, pairs):
    return lax.ppermute(array, "frag", pairs)


def local(coeffs, centres, frag_sizes, pairs):
    mask = (jnp.arange(AUX, dtype=jnp.int32)[None, :] < frag_sizes[:, None]).astype(jnp.float32)
    vmem = pl.BlockSpec(memory_space=pltpu.VMEM)
    packet = pl.pallas_call(
        pack_kernel,
        out_shape=jax.ShapeDtypeStruct((ROWS, AUX), jnp.float32),
        in_specs=[vmem] * 4,
        out_specs=vmem,
    )(coeffs, centres, frag_sizes.reshape(1, FRAG_DEV), pairs.T)

    x_near = swap(packet, X_NEAR)
    x_far = swap(packet, X_FAR)
    x_last = swap(packet, X_LAST)
    z_near = swap(packet, Z_NEAR)
    z_far = swap(packet, Z_FAR)
    z_last = swap(packet, Z_LAST)
    own_c = swap(packet, CORE)
    near_c = swap(x_near, CORE)
    far_c = swap(x_far, CORE)
    last_c = swap(x_last, CORE)

    g_sib, g_far, g_near, g_own, f_far, f_near, f_own = rectangle(
        (packet, z_near, z_far, z_last, x_near, x_far, x_last, own_c, near_c, far_c, last_c),
    )
    f_back = swap(f_far, Z_FAR)
    sib_back = swap(g_sib, CORE)
    far_back = swap(g_far + sib_back[32:], X_FAR)
    f_last = swap(f_near + f_back[16:], Z_NEAR)
    near_back = swap(g_near + sib_back[16:32] + far_back[16:], X_NEAR)
    total = f_own + f_back[:16] + f_last + g_own + sib_back[:16] + far_back[:16] + near_back
    return total * mask


def solution(mesh):
    return jax.shard_map(
        local,
        mesh=mesh,
        in_specs=(
            P(("cplx", "frag"), None),
            P(("cplx", "frag"), None, None),
            P(("cplx", "frag")),
            P(("cplx", "frag"), None),
        ),
        out_specs=P(("cplx", "frag"), None),
        check_vma=False,
    )
```

```python
import functools

import jax
import jax.numpy as jnp
from jax import lax
from jax.experimental import pallas as pl
from jax.experimental.pallas import tpu as pltpu
from jax.sharding import PartitionSpec as P

FRAG_DEV = 16
AUX = 256
ROWS = 96
NF = 64
NG = 128
CHUNK = 32
CPF = AUX // CHUNK
WIDE = 4
NARROW = 8
SPAN = 96
WIDE_ROWS = 24
THIN_ROWS = 16
LIST_ROWS = WIDE_ROWS + THIN_ROWS
DUMMY = NF * CPF
DEPTH = 48
BATCH = 16
SHIFT = 3
WIDTH_FLOOR = 1.0 / 32.0


def pieces(value):
    first = value.astype(jnp.bfloat16).astype(jnp.float32)
    rest = value - first
    second = rest.astype(jnp.bfloat16).astype(jnp.float32)
    return first, second, rest - second


def pack_kernel(coeffs, centres, sizes, pairs, out):
    for k in range(4):
        out[pl.ds(16 * k, 16), :] = centres[:, k, :]
    row = sizes[...].astype(jnp.float32)
    square = (FRAG_DEV, FRAG_DEV)
    eye = lax.broadcasted_iota(jnp.int32, square, 0) == lax.broadcasted_iota(jnp.int32, square, 1)
    column = jnp.sum(jnp.where(eye, row, 0.0), axis=1, keepdims=True)
    lane = lax.broadcasted_iota(jnp.int32, (FRAG_DEV, AUX), 1).astype(jnp.float32)
    out[pl.ds(64, 16), :] = coeffs[...] * (lane < column).astype(jnp.float32)
    out[pl.ds(88, 8), :] = jnp.zeros((8, AUX), jnp.float32)
    out[pl.ds(88, 1), 0:FRAG_DEV] = row
    for r in range(8):
        out[pl.ds(80 + r, 1), :] = pairs[r // 4:r // 4 + 1, AUX * (r % 4):AUX * (r % 4) + AUX].astype(jnp.float32)


def pair_kernel(*refs):
    sources, refs = refs[:11], refs[11:]
    out_far, out_near, out_own, outf_far, outf_near, outf_own = refs[:6]
    (lhs, rows_c, rows_s, cols_s, cols_c, rhs, build, slots, counts, chunks, zeros_v, places, ends,
     table_v, tiles_v, row_sums, table, tile_list, sem) = refs[6:25]
    packets, arrived = refs[25:36], refs[36]
    loads = [pltpu.make_async_copy(a, b, arrived.at[k]) for k, (a, b) in enumerate(zip(sources, packets))]
    for load in loads:
        load.start()
    f_blocks = [packets[0], packets[1], packets[2], packets[3]]
    g_blocks = [packets[0]] + list(packets[4:])
    me = lax.axis_index("frag")
    plane, column = lax.div(me, 8), lax.rem(me, 8)
    zs = [plane, plane ^ 1, 3 - plane, (3 - plane) ^ 1]
    f_devs = [8 * at + column for at in zs]
    line, core = lax.div(column, 2), lax.rem(column, 2)
    xs = [line, line ^ 1, 3 - line, (3 - line) ^ 1]
    g_devs = [8 * plane + 2 * at + c for c in (core, 1 - core) for at in xs]

    def put_rows(r, value):
        for h in range(2):
            build[h, pl.ds(r * 16, 16), :] = value[:, 128 * h:128 * h + 128]

    def take_rows(h, at, count):
        return build.at[h][pl.ds(at, count, stride=16), :]

    lowest = None
    for i, blk in enumerate(f_blocks):
        loads[i].wait()
        x, y, z, w, c = (blk[pl.ds(16 * k, 16), :] for k in range(5))
        lowest = w if lowest is None else jnp.minimum(lowest, w)
        s = x * x + y * y + z * z + w
        one = jnp.ones_like(x)
        zero = jnp.zeros_like(x)
        px, py, pz = pieces(-2.0 * x), pieces(-2.0 * y), pieces(-2.0 * z)
        ps, pw, pc = pieces(s), pieces(w), pieces(c)
        for k in range(3):
            delta = one if k == 0 else zero
            extra = pc if k == 0 else (pw if k == 1 else (zero, zero, zero))
            rows = [px[k], py[k], pz[k], delta, ps[k], *extra,
                    px[k], py[k], pz[k], delta, px[k], py[k], pz[k], delta]
            for r, value in enumerate(rows):
                put_rows(16 * k + r, value)

        def one_row(lf, _, i=i):
            for h in range(2):
                feats = take_rows(h, lf, DEPTH).T
                feats = jnp.concatenate([feats, jnp.zeros((128, 128 - DEPTH), jnp.float32)], axis=1)
                lhs[pl.ds((i * 16 + lf) * CPF + 4 * h, 4), 0:CHUNK, :] = feats.astype(jnp.bfloat16).reshape(4, CHUNK, 128)
            return 0

        lax.fori_loop(0, 16, one_row, 0, unroll=16)
    spare_lane = lax.broadcasted_iota(jnp.int32, (CHUNK, 128), 1)
    lhs[DUMMY, 0:CHUNK, :] = (spare_lane == 4).astype(jnp.float32).astype(jnp.bfloat16)

    pick = lax.broadcasted_iota(jnp.int32, (128, 128), 0)

    def spread(rows, lo, hi, scale):
        sel = jnp.where((pick >= lo) & (pick <= hi), scale, 0.0)
        return jnp.dot(rows, sel.astype(jnp.bfloat16), preferred_element_type=jnp.float32)

    def one_spread(f, _):
        value = spread(lhs[pl.ds(f * CPF, CPF), 0:CHUNK, :].reshape(AUX, 128), 5, 7, 1.0)
        rows_c[pl.ds(f * CPF, CPF)] = value.reshape(CPF, CHUNK, 128)
        rows_s[pl.ds(f * CPF, CPF)] = jnp.zeros((CPF, CHUNK, 128), jnp.float32)
        return 0

    lax.fori_loop(0, NF, one_spread, 0, unroll=16)
    rows_c[DUMMY] = jnp.zeros((CHUNK, 128), jnp.float32)
    rows_s[DUMMY] = jnp.zeros((CHUNK, 128), jnp.float32)

    for load in loads[4:]:
        load.wait()
    for j, blk in enumerate(g_blocks):
        x, y, z, w, c = (blk[pl.ds(16 * k, 16), :] for k in range(5))
        lowest = jnp.minimum(lowest, w)
        s = x * x + y * y + z * z + w
        one = jnp.ones_like(x)
        zero = jnp.zeros_like(x)
        px, py, pz, ps = pieces(x), pieces(y), pieces(z), pieces(s)
        rows = [px[0], py[0], pz[0], ps[0], one, zero, zero, zero,
                px[1], py[1], pz[1], ps[1], px[2], py[2], pz[2], ps[2]]
        for r, value in enumerate(rows):
            put_rows(r, value)

        def one_column(lg, _, j=j, blk=blk):
            cols_s[j * 16 + lg] = jnp.zeros((16, 128), jnp.float32)
            coef = blk[pl.ds(64 + lg, 1), :]
            for h in range(2):
                cols_c[j * 16 + lg, h:h + 1, :] = coef[:, 128 * h:128 * h + 128]
            rhs[j * 16 + lg] = jnp.concatenate([take_rows(h, lg, 16) for h in range(2)], axis=1).astype(jnp.bfloat16)
            return 0

        lax.fori_loop(0, 16, one_column, 0, unroll=16)

    lane = lax.broadcasted_iota(jnp.int32, (8, AUX), 1)
    back = jnp.zeros((8, AUX), jnp.float32)
    for j, blk in enumerate(g_blocks):
        shift = lax.rem(32 * j - 32 * column + 256, 256)
        turned = pltpu.roll(blk[pl.ds(80, 8), :], shift, 1)
        back = jnp.where(lane // 32 == j, turned, back)
    slots[...] = back
    g_lane = lax.broadcasted_iota(jnp.int32, (16, AUX), 0).astype(jnp.float32)
    g_ids = jnp.concatenate([g_lane + (16 * g_devs[j]).astype(jnp.float32) for j in range(8)], axis=0)
    for i, blk in enumerate(f_blocks):
        f_ids = g_lane + (16 * f_devs[i]).astype(jnp.float32)
        f_plane = zs[i]

        def table_of(row_f, row_g):
            odd = (row_f + row_g) - 2.0 * jnp.floor((row_f + row_g) * 0.5)
            less = (row_f < row_g).astype(jnp.float32)
            use = (odd == less) & (row_f != row_g)
            row_f = jnp.where(use, row_f, -1.0)
            left = (row_f == f_ids).astype(jnp.float32).astype(jnp.bfloat16)
            right = (row_g == g_ids).astype(jnp.float32).astype(jnp.bfloat16)
            return lax.dot_general(left, right, (((1,), (1,)), ((), ())), preferred_element_type=jnp.float32)

        there = table_of(blk[pl.ds(80 + plane, 1), :], blk[pl.ds(84 + plane, 1), :])
        back_i = table_of(slots[pl.ds(4 + f_plane, 1), :], slots[pl.ds(f_plane, 1), :])
        counts[pl.ds(16 * i, 16), :] = there + back_i
        sizes = blk[pl.ds(88, 1), :]
        eye = lax.broadcasted_iota(jnp.int32, (16, AUX), 0) == lax.broadcasted_iota(jnp.int32, (16, AUX), 1)
        size_col = jnp.sum(jnp.where(eye, sizes, 0.0), axis=1, keepdims=True)
        many = jnp.floor((size_col + (CHUNK - 1)) * (1.0 / CHUNK))
        chunks[pl.ds(16 * i, 16), :] = jnp.broadcast_to(many, (16, 128))

    most = jnp.max(counts[...]).astype(jnp.int32)
    safe = jnp.min(lowest) >= WIDTH_FLOOR
    row8 = lax.broadcasted_iota(jnp.int32, (8, 128), 0)

    lane8 = lax.broadcasted_iota(jnp.int32, (8, 128), 1)
    sizes = jnp.zeros((8, 128), jnp.float32)
    for j, blk in enumerate(g_blocks):
        part = blk[pl.ds(88, 8), 0:128]
        part = part if j == 0 else pltpu.roll(part, 16 * j, 1)
        sizes = jnp.where(lane8 // 16 == j, part, sizes)
    slots[:, 0:128] = sizes
    is_wide = jnp.where(jnp.broadcast_to(slots[pl.ds(0, 1), 0:128], (8, 128)) > 128.0, 1.0, 0.0)
    per_tile = jnp.where(is_wide > 0.0, float(WIDE), float(NARROW))
    contract = (((1,), (1,)), ((), ()))

    blank = jnp.zeros((128 - DEPTH, 128), jnp.bfloat16)
    none = jnp.zeros((128, 128), jnp.bfloat16)

    def chunks_of(code, take):
        g, q = code & 127, code >> 7
        views = [table.at[q + v, :, pl.ds(g, 1)] for v in range(take // WIDE)]
        at = [views[u // WIDE][u % WIDE, 0] for u in range(take)]
        times = at[0] >> 10
        return g, times, [e & 1023 if u % WIDE == 0 else e for u, e in enumerate(at)]

    def distances(g, at, kind):
        block = rhs[g]
        left = jnp.concatenate([lhs[e, 0:CHUNK, :] for e in at[:4]], axis=0)
        if kind == "narrow":
            left = jnp.concatenate([left, jnp.concatenate([lhs[e, 0:CHUNK, :] for e in at[4:]], axis=0)], axis=1)
            thin = block[:, :128]
            right = jnp.concatenate([thin, thin, thin, blank], axis=0)
            right = jnp.concatenate([jnp.concatenate([right, none], axis=1), jnp.concatenate([none, right], axis=1)], axis=0)
        else:
            right = jnp.concatenate([block, block, block, jnp.concatenate([blank, blank], axis=1)], axis=0)
        return jnp.dot(left, right, preferred_element_type=jnp.float32)

    def gather(at):
        return jnp.concatenate([rows_c[e] for e in at], axis=0)

    def fold(value):
        return jnp.sum(value.reshape(-1, 8, 128), axis=0)

    def apply(kern, kind, g, times, at):
        times = times.astype(jnp.float32)
        k0, k1 = kern[:, :128], kern[:, 128:]
        weight = cols_c[g, 0:1, :] * times
        if kind == "narrow":
            second = fold(k0 * gather(at[:4]) + k1 * gather(at[4:]))
            cols_s[g, 0:8, :] = cols_s[g, 0:8, :] + second * times
            first = [k[u * CHUNK:(u + 1) * CHUNK] * weight for k in (k0, k1) for u in range(4)]
        else:
            coef = gather(at)
            cols_s[g, 0:8, :] = cols_s[g, 0:8, :] + fold(k0 * coef) * times
            cols_s[g, 8:16, :] = cols_s[g, 8:16, :] + fold(k1 * coef) * times
            both = k0 * weight + k1 * (cols_c[g, 1:2, :] * times)
            first = [both[u * CHUNK:(u + 1) * CHUNK] for u in range(4)]
        sums = [rows_s[e] for e in at]
        for e, value, more in zip(at, sums, first):
            rows_s[e] = value + more

    def exact(code):
        g, times, at = chunks_of(code, WIDE)
        left = jnp.concatenate([lhs[e, 0:CHUNK, :] for e in at], axis=0)
        part = rhs[g].astype(jnp.float32)
        wide = spread(left, 21, 23, 1.0)
        dist = jnp.concatenate([wide, wide], axis=1) + width_row(g)
        for k in range(3):
            mine = jnp.where(((pick % 16 == k) & (pick < DEPTH)), -0.5, 0.0).astype(jnp.bfloat16)
            mine = jnp.dot(left, mine, preferred_element_type=jnp.float32)
            other = part[k:k + 1] + part[8 + k:9 + k] + part[12 + k:13 + k]
            gap = jnp.concatenate([mine, mine], axis=1) - other
            dist = dist + gap * gap
        apply(lax.rsqrt(dist), "wide", g, times, at)

    def width_row(g):
        row = jnp.zeros((1, AUX), jnp.float32)
        for k, blk in enumerate(g_blocks):
            row = jnp.where(g // 16 == k, blk[pl.ds(48 + g % 16, 1), :], row)
        return row

    def one_round(state):
        r, _ = state
        groups = SPAN // 8
        at = [(row8 + 8 * t + SPAN * r).astype(jnp.float32) for t in range(groups)]

        def one_class(m, state):
            vals, times, total = state
            times = tuple(jnp.where(a >= total, m.astype(jnp.float32), v) for a, v in zip(at, times))

            def scan(f, state):
                vals, total = state
                many = jnp.broadcast_to(chunks[pl.ds(f, 1), :], (8, 128))
                listed = jnp.broadcast_to(counts[pl.ds(f, 1), :], (8, 128))
                mark = (many + f.astype(jnp.float32) * 16.0) * 4096.0 + total
                vals = tuple(jnp.where(a >= total, mark, v) for a, v in zip(at, vals))
                return vals, total + jnp.where(listed == m.astype(jnp.float32), many, 0.0)

            vals, total = lax.fori_loop(0, NF, scan, (vals, total), unroll=8)
            vals = tuple(jnp.where(a >= total, -1.0, v) for a, v in zip(at, vals))
            total = jnp.floor((total + per_tile - 1.0) / per_tile) * per_tile
            return vals, times, total

        flat = zeros_v[...]
        none = (flat,) * groups
        vals, times, total = lax.fori_loop(1, most + 1, one_class, (none, none, flat))
        for t in range(groups):
            code = jnp.floor(vals[t] * (1.0 / 4096.0))
            offset = at[t] - (vals[t] - 4096.0 * code)
            frag = jnp.floor(code * (1.0 / 16.0))
            entry = jnp.where((vals[t] >= 0.0) & (at[t] < total), frag * CPF + offset, float(DUMMY))
            places[0, pl.ds(8 * t, 8), :] = entry
            places[1, pl.ds(8 * t, 8), :] = times[t]
        groups4 = SPAN // WIDE
        for u in range(WIDE):
            value = places.at[0][pl.ds(u, groups4, stride=WIDE), :]
            if u == 0:
                value = value + 1024.0 * places.at[1][pl.ds(u, groups4, stride=WIDE), :]
            table_v[pl.ds(0, groups4), u, :] = value.astype(jnp.int32)
        table_v[pl.ds(groups4, 2)] = jnp.full((2, WIDE, 128), DUMMY, jnp.int32)
        left_over = jnp.clip(total - (SPAN * r).astype(jnp.float32), 0.0, float(SPAN))
        tiles = left_over / per_tile
        tiles_wide = tiles * is_wide
        tiles_thin = tiles - tiles_wide
        for k, tiles in enumerate((tiles_wide, tiles_thin)):
            ends[k] = lax.dot_general(upto, jnp.concatenate([tiles] * 16, axis=0).astype(jnp.bfloat16), contract, preferred_element_type=jnp.float32)
        number = [(lane8 + 128 * row8 + 1024 * k).astype(jnp.float32) for k in range(WIDE_ROWS // 8)]
        kinds = [(0, k) for k in range(WIDE_ROWS // 8)] + [(1, k) for k in range(THIN_ROWS // 8)]

        def seek(c, state):
            out = []
            column = (c + 1).astype(jnp.float32)
            edges = [jnp.broadcast_to(ends.at[n][pl.ds(c, 1), :], (8, 128)) for n in range(2)]
            for (thin, k), (where, begin) in zip(kinds, state):
                end = edges[thin]
                hit = number[k] >= end
                out.append((jnp.where(hit, column, where), jnp.where(hit, end, begin)))
            return tuple(out)

        found = lax.fori_loop(0, NG, seek, ((flat, flat),) * len(kinds), unroll=16)
        for (thin, k), (where, begin) in zip(kinds, found):
            place = (number[k] - begin) * (128.0 * (1 + thin)) + where
            place = jnp.where(where < float(NG), place, float(groups4 * 128))
            tiles_v[pl.ds(thin * WIDE_ROWS + 8 * k, 8), :] = place.astype(jnp.int32)
        info = jnp.where(row8 == 0, jnp.sum(tiles_wide, axis=1, keepdims=True), jnp.sum(tiles_thin, axis=1, keepdims=True))
        tiles_v[pl.ds(LIST_ROWS, 8), :] = info.astype(jnp.int32)
        longest = jnp.max(total).astype(jnp.int32)
        copies = [pltpu.make_async_copy(table_v, table, sem.at[0]), pltpu.make_async_copy(tiles_v, tile_list, sem.at[1])]
        for copy in copies:
            copy.start()
        for copy in copies:
            copy.wait()
        count_wide, count_thin = tile_list[LIST_ROWS, 0], tile_list[LIST_ROWS + 1, 0]

        def many_tiles(kind, first_row, count):
            take = NARROW if kind == "narrow" else WIDE

            def body(b, _):
                row, col = first_row + lax.shift_right_logical(b, SHIFT), (b & (128 // BATCH - 1)) * BATCH
                for u in range(BATCH):
                    g, times, at = chunks_of(tile_list[row, col + u], take)
                    apply(lax.rsqrt(distances(g, at, kind)), kind, g, times, at)
                return 0

            lax.fori_loop(0, (count + (BATCH - 1)) // BATCH, body, 0)

        @pl.when(safe)
        def _():
            many_tiles("wide", 0, count_wide)
            many_tiles("narrow", WIDE_ROWS, count_thin)

        @pl.when(jnp.logical_not(safe))
        def _():
            def wide_one(t, _):
                exact(tile_list[t >> 7, t & 127])
                return 0

            def thin_one(t, _):
                exact(tile_list[WIDE_ROWS + (t >> 8), (t & 255) >> 1] + 128 * (t & 1))
                return 0

            lax.fori_loop(0, count_wide, wide_one, 0)
            lax.fori_loop(0, 2 * count_thin, thin_one, 0)

        return r + 1, longest

    zeros_v[...] = jnp.zeros_like(zeros_v)
    upto = (lax.broadcasted_iota(jnp.int32, (128, 128), 1) <= pick).astype(jnp.float32).astype(jnp.bfloat16)
    lax.while_loop(lambda state: state[0] * SPAN < state[1], one_round, (jnp.int32(0), jnp.int32(1)))

    ones8 = jnp.ones((8, 256), jnp.bfloat16)

    def collect(f, _):
        value = rows_s[pl.ds(f * CPF, CPF)].reshape(AUX, 128)
        high = value.astype(jnp.bfloat16)
        low = (value - high.astype(jnp.float32)).astype(jnp.bfloat16)
        row = lax.dot_general(ones8, jnp.concatenate([high, low], axis=1), contract, preferred_element_type=jnp.float32)
        for h in range(2):
            row_sums[h, pl.ds(f, 1), :] = row[0:1, 128 * h:128 * h + 128]
        return 0

    lax.fori_loop(0, NF, collect, 0, unroll=16)
    rows_out = jnp.concatenate([row_sums[0], row_sums[1]], axis=1)
    outf_own[...] = rows_out[0:16]
    outf_near[...] = rows_out[16:32]
    outf_far[...] = rows_out[32:64]
    cols = []
    for h in range(2):
        flat_s = cols_s.reshape(NG * 16, 128)
        half = flat_s[pl.ds(8 * h, NG, stride=16), :]
        for r in range(1, 8):
            half = half + flat_s[pl.ds(8 * h + r, NG, stride=16), :]
        cols.append(half)
    cols = jnp.concatenate(cols, axis=1)
    for k in range(2):
        part = pl.ds(16 * k, 16)
        out_own[part, :] = cols[64 * k:64 * k + 16]
        out_near[part, :] = cols[64 * k + 16:64 * k + 32]
        out_far[part, :] = cols[64 * k + 32:64 * k + 48]
        out_far[pl.ds(32 + 16 * k, 16), :] = cols[64 * k + 48:64 * k + 64]


def rectangle(packets):
    vmem = pl.BlockSpec(memory_space=pltpu.VMEM)
    shape = lambda rows: jax.ShapeDtypeStruct((rows, AUX), jnp.float32)
    return pl.pallas_call(
        pair_kernel,
        out_shape=(shape(64), shape(32), shape(32), shape(32), shape(16), shape(16)),
        in_specs=[pl.BlockSpec(memory_space=pl.ANY)] * 11,
        out_specs=(vmem,) * 6,
        scratch_shapes=[
            pltpu.VMEM((DUMMY + 1, 2 * CHUNK, 128), jnp.bfloat16),
            pltpu.VMEM((DUMMY + 1, CHUNK, 128), jnp.float32),
            pltpu.VMEM((DUMMY + 1, CHUNK, 128), jnp.float32),
            pltpu.VMEM((NG, 16, 128), jnp.float32),
            pltpu.VMEM((NG, 16, 128), jnp.float32),
            pltpu.VMEM((NG, 16, AUX), jnp.bfloat16),
            pltpu.VMEM((2, DEPTH * 16, 128), jnp.float32),
            pltpu.VMEM((8, AUX), jnp.float32),
            pltpu.VMEM((NF, 128), jnp.float32),
            pltpu.VMEM((NF, 128), jnp.float32),
            pltpu.VMEM((8, 128), jnp.float32),
            pltpu.VMEM((2, SPAN, 128), jnp.float32),
            pltpu.VMEM((2, 128, 128), jnp.float32),
            pltpu.VMEM((SPAN // WIDE + 2, WIDE, 128), jnp.int32),
            pltpu.VMEM((LIST_ROWS + 8, 128), jnp.int32),
            pltpu.VMEM((2, NF, 128), jnp.float32),
            pltpu.SMEM((SPAN // WIDE + 2, WIDE, 128), jnp.int32),
            pltpu.SMEM((LIST_ROWS + 8, 128), jnp.int32),
            pltpu.SemaphoreType.DMA((2,)),
        ]
        + [pltpu.VMEM((ROWS, AUX), jnp.float32)] * 11
        + [
            pltpu.SemaphoreType.DMA((11,)),
        ],
        compiler_params=pltpu.CompilerParams(vmem_limit_bytes=56 * 2**20),
    )(*packets)


def index_of(z, x, c):
    return (z * 4 + x) * 2 + c


def partners(move):
    return [
        (index_of(z, x, c), index_of(*move(z, x, c)))
        for z in range(4) for x in range(4) for c in range(2)
    ]


X_NEAR = partners(lambda z, x, c: (z, x ^ 1, c))
X_FAR = partners(lambda z, x, c: (z, 3 - x, c))
Z_NEAR = partners(lambda z, x, c: (z ^ 1, x, c))
Z_FAR = partners(lambda z, x, c: (3 - z, x, c))
X_LAST = partners(lambda z, x, c: (z, x ^ 2, c))
Z_LAST = partners(lambda z, x, c: (z ^ 2, x, c))
CORE = partners(lambda z, x, c: (z, x, c ^ 1))


def swap(array, pairs):
    return lax.ppermute(array, "frag", pairs)


def local(coeffs, centres, frag_sizes, pairs):
    mask = (jnp.arange(AUX, dtype=jnp.int32)[None, :] < frag_sizes[:, None]).astype(jnp.float32)
    vmem = pl.BlockSpec(memory_space=pltpu.VMEM)
    packet = pl.pallas_call(
        pack_kernel,
        out_shape=jax.ShapeDtypeStruct((ROWS, AUX), jnp.float32),
        in_specs=[vmem] * 4,
        out_specs=vmem,
    )(coeffs, centres, frag_sizes.reshape(1, FRAG_DEV), pairs.T)

    x_near = swap(packet, X_NEAR)
    x_far = swap(packet, X_FAR)
    x_last = swap(packet, X_LAST)
    z_near = swap(packet, Z_NEAR)
    z_far = swap(packet, Z_FAR)
    z_last = swap(packet, Z_LAST)
    own_c = swap(packet, CORE)
    near_c = swap(x_near, CORE)
    far_c = swap(x_far, CORE)
    last_c = swap(x_last, CORE)

    g_far, g_near, g_own, f_far, f_near, f_own = rectangle(
        (packet, z_near, z_far, z_last, x_near, x_far, x_last, own_c, near_c, far_c, last_c),
    )
    far_back = swap(g_far, X_FAR)
    f_back = swap(f_far, Z_FAR)
    near_back = swap(g_near + far_back[32:], X_NEAR)
    f_last = swap(f_near + f_back[16:], Z_NEAR)
    both = g_own + far_back[:32] + near_back
    total = both[:16] + f_own + f_back[:16] + f_last + swap(both[16:], CORE)
    return total * mask


def solution(mesh):
    return jax.shard_map(
        local,
        mesh=mesh,
        in_specs=(
            P(("cplx", "frag"), None),
            P(("cplx", "frag"), None, None),
            P(("cplx", "frag")),
            P(("cplx", "frag"), None),
        ),
        out_specs=P(("cplx", "frag"), None),
        check_vma=False,
    )
```

```python
import functools

import jax
import jax.numpy as jnp
from jax import lax
from jax.experimental import pallas as pl
from jax.experimental.pallas import tpu as pltpu
from jax.sharding import PartitionSpec as P

FRAG_DEV = 16
AUX = 256
ROWS = 96
NF = 64
NG = 128
CHUNK = 32
CPF = AUX // CHUNK
WIDE = 4
NARROW = 8
SPAN = 96
WIDE_ROWS = 24
THIN_ROWS = 16
LIST_ROWS = WIDE_ROWS + THIN_ROWS
DUMMY = NF * CPF
DEPTH = 48
BATCH = 16
SHIFT = 3
WIDTH_FLOOR = 1.0 / 32.0


def pieces(value):
    first = value.astype(jnp.bfloat16).astype(jnp.float32)
    rest = value - first
    second = rest.astype(jnp.bfloat16).astype(jnp.float32)
    return first, second, rest - second


def pack_kernel(coeffs, centres, sizes, pairs, out):
    for k in range(4):
        out[pl.ds(16 * k, 16), :] = centres[:, k, :]
    row = sizes[...].astype(jnp.float32)
    square = (FRAG_DEV, FRAG_DEV)
    eye = lax.broadcasted_iota(jnp.int32, square, 0) == lax.broadcasted_iota(jnp.int32, square, 1)
    column = jnp.sum(jnp.where(eye, row, 0.0), axis=1, keepdims=True)
    lane = lax.broadcasted_iota(jnp.int32, (FRAG_DEV, AUX), 1).astype(jnp.float32)
    out[pl.ds(64, 16), :] = coeffs[...] * (lane < column).astype(jnp.float32)
    out[pl.ds(88, 8), :] = jnp.zeros((8, AUX), jnp.float32)
    out[pl.ds(88, 1), 0:FRAG_DEV] = row
    for r in range(8):
        out[pl.ds(80 + r, 1), :] = pairs[r // 4:r // 4 + 1, AUX * (r % 4):AUX * (r % 4) + AUX].astype(jnp.float32)


def pair_kernel(*refs):
    sources, refs = refs[:11], refs[11:]
    out_far, out_near, out_own, outf_far, outf_near, outf_own = refs[:6]
    (lhs, rows_c, rows_s, cols_s, cols_c, rhs, build, slots, counts, chunks, zeros_v, places, ends,
     table_v, tiles_v, row_sums, table, tile_list, sem) = refs[6:25]
    packets, arrived = refs[25:36], refs[36]
    loads = [pltpu.make_async_copy(a, b, arrived.at[k]) for k, (a, b) in enumerate(zip(sources, packets))]
    for load in loads:
        load.start()
    f_blocks = [packets[0], packets[1], packets[2], packets[3]]
    g_blocks = [packets[0]] + list(packets[4:])
    me = lax.axis_index("frag")
    plane, column = lax.div(me, 8), lax.rem(me, 8)
    zs = [plane, plane ^ 1, 3 - plane, (3 - plane) ^ 1]
    f_devs = [8 * at + column for at in zs]
    line, core = lax.div(column, 2), lax.rem(column, 2)
    xs = [line, line ^ 1, 3 - line, (3 - line) ^ 1]
    g_devs = [8 * plane + 2 * at + c for c in (core, 1 - core) for at in xs]

    def put_rows(r, value):
        for h in range(2):
            build[h, pl.ds(r * 16, 16), :] = value[:, 128 * h:128 * h + 128]

    def take_rows(h, at, count):
        return build.at[h][pl.ds(at, count, stride=16), :]

    pick = lax.broadcasted_iota(jnp.int32, (128, 128), 0)

    def spread(rows, lo, hi, scale):
        sel = jnp.where((pick >= lo) & (pick <= hi), scale, 0.0)
        return jnp.dot(rows, sel.astype(jnp.bfloat16), preferred_element_type=jnp.float32)

    lowest = None
    for i, blk in enumerate(f_blocks):
        loads[i].wait()
        x, y, z, w, c = (blk[pl.ds(16 * k, 16), :] for k in range(5))
        lowest = w if lowest is None else jnp.minimum(lowest, w)
        s = x * x + y * y + z * z + w
        one = jnp.ones_like(x)
        zero = jnp.zeros_like(x)
        px, py, pz = pieces(-2.0 * x), pieces(-2.0 * y), pieces(-2.0 * z)
        ps, pw, pc = pieces(s), pieces(w), pieces(c)
        for k in range(3):
            delta = one if k == 0 else zero
            extra = pc if k == 0 else (pw if k == 1 else (zero, zero, zero))
            rows = [px[k], py[k], pz[k], delta, ps[k], *extra,
                    px[k], py[k], pz[k], delta, px[k], py[k], pz[k], delta]
            for r, value in enumerate(rows):
                put_rows(16 * k + r, value)

        def one_row(lf, _, i=i):
            for h in range(2):
                feats = take_rows(h, lf, DEPTH).T
                feats = jnp.concatenate([feats, jnp.zeros((128, 128 - DEPTH), jnp.float32)], axis=1)
                feats = feats.astype(jnp.bfloat16)
                at = pl.ds((i * 16 + lf) * CPF + 4 * h, 4)
                lhs[at, 0:CHUNK, :] = feats.reshape(4, CHUNK, 128)
                rows_c[at] = spread(feats, 5, 7, 1.0).reshape(4, CHUNK, 128)
                rows_s[at] = jnp.zeros((4, CHUNK, 128), jnp.float32)
            return 0

        lax.fori_loop(0, 16, one_row, 0, unroll=16)
    spare_lane = lax.broadcasted_iota(jnp.int32, (CHUNK, 128), 1)
    lhs[DUMMY, 0:CHUNK, :] = (spare_lane == 4).astype(jnp.float32).astype(jnp.bfloat16)

    rows_c[DUMMY] = jnp.zeros((CHUNK, 128), jnp.float32)
    rows_s[DUMMY] = jnp.zeros((CHUNK, 128), jnp.float32)

    for load in loads[4:]:
        load.wait()
    for j, blk in enumerate(g_blocks):
        x, y, z, w, c = (blk[pl.ds(16 * k, 16), :] for k in range(5))
        lowest = jnp.minimum(lowest, w)
        s = x * x + y * y + z * z + w
        one = jnp.ones_like(x)
        zero = jnp.zeros_like(x)
        px, py, pz, ps = pieces(x), pieces(y), pieces(z), pieces(s)
        rows = [px[0], py[0], pz[0], ps[0], one, zero, zero, zero,
                px[1], py[1], pz[1], ps[1], px[2], py[2], pz[2], ps[2]]
        for r, value in enumerate(rows):
            put_rows(r, value)

        def one_column(lg, _, j=j, blk=blk):
            cols_s[j * 16 + lg] = jnp.zeros((16, 128), jnp.float32)
            coef = blk[pl.ds(64 + lg, 1), :]
            for h in range(2):
                cols_c[j * 16 + lg, h:h + 1, :] = coef[:, 128 * h:128 * h + 128]
            rhs[j * 16 + lg] = jnp.concatenate([take_rows(h, lg, 16) for h in range(2)], axis=1).astype(jnp.bfloat16)
            return 0

        lax.fori_loop(0, 16, one_column, 0, unroll=16)

    lane = lax.broadcasted_iota(jnp.int32, (8, AUX), 1)
    back = jnp.zeros((8, AUX), jnp.float32)
    for j, blk in enumerate(g_blocks):
        shift = lax.rem(32 * j - 32 * column + 256, 256)
        turned = pltpu.roll(blk[pl.ds(80, 8), :], shift, 1)
        back = jnp.where(lane // 32 == j, turned, back)
    slots[...] = back
    g_lane = lax.broadcasted_iota(jnp.int32, (16, AUX), 0).astype(jnp.float32)
    g_ids = jnp.concatenate([g_lane + (16 * g_devs[j]).astype(jnp.float32) for j in range(8)], axis=0)
    for i, blk in enumerate(f_blocks):
        f_ids = g_lane + (16 * f_devs[i]).astype(jnp.float32)
        f_plane = zs[i]

        def table_of(row_f, row_g):
            odd = (row_f + row_g) - 2.0 * jnp.floor((row_f + row_g) * 0.5)
            less = (row_f < row_g).astype(jnp.float32)
            use = (odd == less) & (row_f != row_g)
            row_f = jnp.where(use, row_f, -1.0)
            left = (row_f == f_ids).astype(jnp.float32).astype(jnp.bfloat16)
            right = (row_g == g_ids).astype(jnp.float32).astype(jnp.bfloat16)
            return lax.dot_general(left, right, (((1,), (1,)), ((), ())), preferred_element_type=jnp.float32)

        there = table_of(blk[pl.ds(80 + plane, 1), :], blk[pl.ds(84 + plane, 1), :])
        back_i = table_of(slots[pl.ds(4 + f_plane, 1), :], slots[pl.ds(f_plane, 1), :])
        counts[pl.ds(16 * i, 16), :] = there + back_i
        sizes = blk[pl.ds(88, 1), :]
        eye = lax.broadcasted_iota(jnp.int32, (16, AUX), 0) == lax.broadcasted_iota(jnp.int32, (16, AUX), 1)
        size_col = jnp.sum(jnp.where(eye, sizes, 0.0), axis=1, keepdims=True)
        many = jnp.floor((size_col + (CHUNK - 1)) * (1.0 / CHUNK))
        chunks[pl.ds(16 * i, 16), :] = jnp.broadcast_to(many, (16, 128))

    most = jnp.max(counts[...]).astype(jnp.int32)
    safe = jnp.min(lowest) >= WIDTH_FLOOR
    row8 = lax.broadcasted_iota(jnp.int32, (8, 128), 0)

    lane8 = lax.broadcasted_iota(jnp.int32, (8, 128), 1)
    sizes = jnp.zeros((8, 128), jnp.float32)
    for j, blk in enumerate(g_blocks):
        part = blk[pl.ds(88, 8), 0:128]
        part = part if j == 0 else pltpu.roll(part, 16 * j, 1)
        sizes = jnp.where(lane8 // 16 == j, part, sizes)
    slots[:, 0:128] = sizes
    is_wide = jnp.where(jnp.broadcast_to(slots[pl.ds(0, 1), 0:128], (8, 128)) > 128.0, 1.0, 0.0)
    per_tile = jnp.where(is_wide > 0.0, float(WIDE), float(NARROW))
    contract = (((1,), (1,)), ((), ()))

    blank = jnp.zeros((128 - DEPTH, 128), jnp.bfloat16)
    none = jnp.zeros((128, 128), jnp.bfloat16)

    def chunks_of(code, take):
        g, q = code & 127, code >> 7
        views = [table.at[q + v, :, pl.ds(g, 1)] for v in range(take // WIDE)]
        at = [views[u // WIDE][u % WIDE, 0] for u in range(take)]
        times = at[0] >> 10
        return g, times, [e & 1023 if u % WIDE == 0 else e for u, e in enumerate(at)]

    def distances(g, at, kind):
        block = rhs[g]
        left = jnp.concatenate([lhs[e, 0:CHUNK, :] for e in at[:4]], axis=0)
        if kind == "narrow":
            left = jnp.concatenate([left, jnp.concatenate([lhs[e, 0:CHUNK, :] for e in at[4:]], axis=0)], axis=1)
            thin = block[:, :128]
            right = jnp.concatenate([thin, thin, thin, blank], axis=0)
            right = jnp.concatenate([jnp.concatenate([right, none], axis=1), jnp.concatenate([none, right], axis=1)], axis=0)
        else:
            right = jnp.concatenate([block, block, block, jnp.concatenate([blank, blank], axis=1)], axis=0)
        return jnp.dot(left, right, preferred_element_type=jnp.float32)

    def gather(at):
        return jnp.concatenate([rows_c[e] for e in at], axis=0)

    def fold(value):
        return jnp.sum(value.reshape(-1, 8, 128), axis=0)

    def apply(kern, kind, g, times, at):
        times = times.astype(jnp.float32)
        k0, k1 = kern[:, :128], kern[:, 128:]
        weight = cols_c[g, 0:1, :] * times
        if kind == "narrow":
            second = fold(k0 * gather(at[:4]) + k1 * gather(at[4:]))
            cols_s[g, 0:8, :] = cols_s[g, 0:8, :] + second * times
            first = [k[u * CHUNK:(u + 1) * CHUNK] * weight for k in (k0, k1) for u in range(4)]
        else:
            coef = gather(at)
            cols_s[g, 0:8, :] = cols_s[g, 0:8, :] + fold(k0 * coef) * times
            cols_s[g, 8:16, :] = cols_s[g, 8:16, :] + fold(k1 * coef) * times
            both = k0 * weight + k1 * (cols_c[g, 1:2, :] * times)
            first = [both[u * CHUNK:(u + 1) * CHUNK] for u in range(4)]
        sums = [rows_s[e] for e in at]
        for e, value, more in zip(at, sums, first):
            rows_s[e] = value + more

    def exact(code):
        g, times, at = chunks_of(code, WIDE)
        left = jnp.concatenate([lhs[e, 0:CHUNK, :] for e in at], axis=0)
        part = rhs[g].astype(jnp.float32)
        wide = spread(left, 21, 23, 1.0)
        dist = jnp.concatenate([wide, wide], axis=1) + width_row(g)
        for k in range(3):
            mine = jnp.where(((pick % 16 == k) & (pick < DEPTH)), -0.5, 0.0).astype(jnp.bfloat16)
            mine = jnp.dot(left, mine, preferred_element_type=jnp.float32)
            other = part[k:k + 1] + part[8 + k:9 + k] + part[12 + k:13 + k]
            gap = jnp.concatenate([mine, mine], axis=1) - other
            dist = dist + gap * gap
        apply(lax.rsqrt(dist), "wide", g, times, at)

    def width_row(g):
        row = jnp.zeros((1, AUX), jnp.float32)
        for k, blk in enumerate(g_blocks):
            row = jnp.where(g // 16 == k, blk[pl.ds(48 + g % 16, 1), :], row)
        return row

    def one_round(state):
        r, _ = state
        groups = SPAN // 8
        at = [(row8 + 8 * t + SPAN * r).astype(jnp.float32) for t in range(groups)]

        def one_class(m, state):
            vals, times, total = state
            times = tuple(jnp.where(a >= total, m.astype(jnp.float32), v) for a, v in zip(at, times))

            def scan(f, state):
                vals, total = state
                many = jnp.broadcast_to(chunks[pl.ds(f, 1), :], (8, 128))
                listed = jnp.broadcast_to(counts[pl.ds(f, 1), :], (8, 128))
                mark = (many + f.astype(jnp.float32) * 16.0) * 4096.0 + total
                vals = tuple(jnp.where(a >= total, mark, v) for a, v in zip(at, vals))
                return vals, total + jnp.where(listed == m.astype(jnp.float32), many, 0.0)

            vals, total = lax.fori_loop(0, NF, scan, (vals, total), unroll=16)
            vals = tuple(jnp.where(a >= total, -1.0, v) for a, v in zip(at, vals))
            total = jnp.floor((total + per_tile - 1.0) / per_tile) * per_tile
            return vals, times, total

        flat = zeros_v[...]
        none = (flat,) * groups
        vals, times, total = lax.fori_loop(1, most + 1, one_class, (none, none, flat))
        for t in range(groups):
            code = jnp.floor(vals[t] * (1.0 / 4096.0))
            offset = at[t] - (vals[t] - 4096.0 * code)
            frag = jnp.floor(code * (1.0 / 16.0))
            entry = jnp.where((vals[t] >= 0.0) & (at[t] < total), frag * CPF + offset, float(DUMMY))
            places[0, pl.ds(8 * t, 8), :] = entry
            places[1, pl.ds(8 * t, 8), :] = times[t]
        groups4 = SPAN // WIDE
        for u in range(WIDE):
            value = places.at[0][pl.ds(u, groups4, stride=WIDE), :]
            if u == 0:
                value = value + 1024.0 * places.at[1][pl.ds(u, groups4, stride=WIDE), :]
            table_v[pl.ds(0, groups4), u, :] = value.astype(jnp.int32)
        table_v[pl.ds(groups4, 2)] = jnp.full((2, WIDE, 128), DUMMY, jnp.int32)
        left_over = jnp.clip(total - (SPAN * r).astype(jnp.float32), 0.0, float(SPAN))
        tiles = left_over / per_tile
        tiles_wide = tiles * is_wide
        tiles_thin = tiles - tiles_wide
        for k, tiles in enumerate((tiles_wide, tiles_thin)):
            ends[k] = lax.dot_general(upto, jnp.concatenate([tiles] * 16, axis=0).astype(jnp.bfloat16), contract, preferred_element_type=jnp.float32)
        number = [(lane8 + 128 * row8 + 1024 * k).astype(jnp.float32) for k in range(WIDE_ROWS // 8)]
        kinds = [(0, k) for k in range(WIDE_ROWS // 8)] + [(1, k) for k in range(THIN_ROWS // 8)]

        def seek(c, state):
            out = []
            column = (c + 1).astype(jnp.float32)
            edges = [jnp.broadcast_to(ends.at[n][pl.ds(c, 1), :], (8, 128)) for n in range(2)]
            for (thin, k), (where, begin) in zip(kinds, state):
                end = edges[thin]
                hit = number[k] >= end
                out.append((jnp.where(hit, column, where), jnp.where(hit, end, begin)))
            return tuple(out)

        found = lax.fori_loop(0, NG, seek, ((flat, flat),) * len(kinds), unroll=16)
        for (thin, k), (where, begin) in zip(kinds, found):
            place = (number[k] - begin) * (128.0 * (1 + thin)) + where
            place = jnp.where(where < float(NG), place, float(groups4 * 128))
            tiles_v[pl.ds(thin * WIDE_ROWS + 8 * k, 8), :] = place.astype(jnp.int32)
        info = jnp.where(row8 == 0, jnp.sum(tiles_wide, axis=1, keepdims=True), jnp.sum(tiles_thin, axis=1, keepdims=True))
        tiles_v[pl.ds(LIST_ROWS, 8), :] = info.astype(jnp.int32)
        longest = jnp.max(total).astype(jnp.int32)
        copies = [pltpu.make_async_copy(table_v, table, sem.at[0]), pltpu.make_async_copy(tiles_v, tile_list, sem.at[1])]
        for copy in copies:
            copy.start()
        for copy in copies:
            copy.wait()
        count_wide, count_thin = tile_list[LIST_ROWS, 0], tile_list[LIST_ROWS + 1, 0]

        def many_tiles(kind, first_row, count):
            take = NARROW if kind == "narrow" else WIDE

            def body(b, _):
                row, col = first_row + lax.shift_right_logical(b, SHIFT), (b & (128 // BATCH - 1)) * BATCH
                for u in range(BATCH):
                    g, times, at = chunks_of(tile_list[row, col + u], take)
                    apply(lax.rsqrt(distances(g, at, kind)), kind, g, times, at)
                return 0

            lax.fori_loop(0, (count + (BATCH - 1)) // BATCH, body, 0)

        @pl.when(safe)
        def _():
            many_tiles("wide", 0, count_wide)
            many_tiles("narrow", WIDE_ROWS, count_thin)

        @pl.when(jnp.logical_not(safe))
        def _():
            def wide_one(t, _):
                exact(tile_list[t >> 7, t & 127])
                return 0

            def thin_one(t, _):
                exact(tile_list[WIDE_ROWS + (t >> 8), (t & 255) >> 1] + 128 * (t & 1))
                return 0

            lax.fori_loop(0, count_wide, wide_one, 0)
            lax.fori_loop(0, 2 * count_thin, thin_one, 0)

        return r + 1, longest

    zeros_v[...] = jnp.zeros_like(zeros_v)
    upto = (lax.broadcasted_iota(jnp.int32, (128, 128), 1) <= pick).astype(jnp.float32).astype(jnp.bfloat16)
    lax.while_loop(lambda state: state[0] * SPAN < state[1], one_round, (jnp.int32(0), jnp.int32(1)))

    ones8 = jnp.ones((8, 256), jnp.bfloat16)

    def collect(f, _):
        value = rows_s[pl.ds(f * CPF, CPF)].reshape(AUX, 128)
        high = value.astype(jnp.bfloat16)
        low = (value - high.astype(jnp.float32)).astype(jnp.bfloat16)
        row = lax.dot_general(ones8, jnp.concatenate([high, low], axis=1), contract, preferred_element_type=jnp.float32)
        for h in range(2):
            row_sums[h, pl.ds(f, 1), :] = row[0:1, 128 * h:128 * h + 128]
        return 0

    lax.fori_loop(0, NF, collect, 0, unroll=16)
    rows_out = jnp.concatenate([row_sums[0], row_sums[1]], axis=1)
    outf_own[...] = rows_out[0:16]
    outf_near[...] = rows_out[16:32]
    outf_far[...] = rows_out[32:64]
    cols = []
    for h in range(2):
        flat_s = cols_s.reshape(NG * 16, 128)
        half = flat_s[pl.ds(8 * h, NG, stride=16), :]
        for r in range(1, 8):
            half = half + flat_s[pl.ds(8 * h + r, NG, stride=16), :]
        cols.append(half)
    cols = jnp.concatenate(cols, axis=1)
    for k in range(2):
        part = pl.ds(16 * k, 16)
        out_own[part, :] = cols[64 * k:64 * k + 16]
        out_near[part, :] = cols[64 * k + 16:64 * k + 32]
        out_far[part, :] = cols[64 * k + 32:64 * k + 48]
        out_far[pl.ds(32 + 16 * k, 16), :] = cols[64 * k + 48:64 * k + 64]


def rectangle(packets):
    vmem = pl.BlockSpec(memory_space=pltpu.VMEM)
    shape = lambda rows: jax.ShapeDtypeStruct((rows, AUX), jnp.float32)
    return pl.pallas_call(
        pair_kernel,
        out_shape=(shape(64), shape(32), shape(32), shape(32), shape(16), shape(16)),
        in_specs=[pl.BlockSpec(memory_space=pl.ANY)] * 11,
        out_specs=(vmem,) * 6,
        scratch_shapes=[
            pltpu.VMEM((DUMMY + 1, 2 * CHUNK, 128), jnp.bfloat16),
            pltpu.VMEM((DUMMY + 1, CHUNK, 128), jnp.float32),
            pltpu.VMEM((DUMMY + 1, CHUNK, 128), jnp.float32),
            pltpu.VMEM((NG, 16, 128), jnp.float32),
            pltpu.VMEM((NG, 16, 128), jnp.float32),
            pltpu.VMEM((NG, 16, AUX), jnp.bfloat16),
            pltpu.VMEM((2, DEPTH * 16, 128), jnp.float32),
            pltpu.VMEM((8, AUX), jnp.float32),
            pltpu.VMEM((NF, 128), jnp.float32),
            pltpu.VMEM((NF, 128), jnp.float32),
            pltpu.VMEM((8, 128), jnp.float32),
            pltpu.VMEM((2, SPAN, 128), jnp.float32),
            pltpu.VMEM((2, 128, 128), jnp.float32),
            pltpu.VMEM((SPAN // WIDE + 2, WIDE, 128), jnp.int32),
            pltpu.VMEM((LIST_ROWS + 8, 128), jnp.int32),
            pltpu.VMEM((2, NF, 128), jnp.float32),
            pltpu.SMEM((SPAN // WIDE + 2, WIDE, 128), jnp.int32),
            pltpu.SMEM((LIST_ROWS + 8, 128), jnp.int32),
            pltpu.SemaphoreType.DMA((2,)),
        ]
        + [pltpu.VMEM((ROWS, AUX), jnp.float32)] * 11
        + [
            pltpu.SemaphoreType.DMA((11,)),
        ],
        compiler_params=pltpu.CompilerParams(vmem_limit_bytes=56 * 2**20),
    )(*packets)


def index_of(z, x, c):
    return (z * 4 + x) * 2 + c


def partners(move):
    return [
        (index_of(z, x, c), index_of(*move(z, x, c)))
        for z in range(4) for x in range(4) for c in range(2)
    ]


X_NEAR = partners(lambda z, x, c: (z, x ^ 1, c))
X_FAR = partners(lambda z, x, c: (z, 3 - x, c))
Z_NEAR = partners(lambda z, x, c: (z ^ 1, x, c))
Z_FAR = partners(lambda z, x, c: (3 - z, x, c))
X_LAST = partners(lambda z, x, c: (z, x ^ 2, c))
Z_LAST = partners(lambda z, x, c: (z ^ 2, x, c))
CORE = partners(lambda z, x, c: (z, x, c ^ 1))


def swap(array, pairs):
    return lax.ppermute(array, "frag", pairs)


def local(coeffs, centres, frag_sizes, pairs):
    mask = (jnp.arange(AUX, dtype=jnp.int32)[None, :] < frag_sizes[:, None]).astype(jnp.float32)
    vmem = pl.BlockSpec(memory_space=pltpu.VMEM)
    packet = pl.pallas_call(
        pack_kernel,
        out_shape=jax.ShapeDtypeStruct((ROWS, AUX), jnp.float32),
        in_specs=[vmem] * 4,
        out_specs=vmem,
    )(coeffs, centres, frag_sizes.reshape(1, FRAG_DEV), pairs.T)

    x_near = swap(packet, X_NEAR)
    x_far = swap(packet, X_FAR)
    x_last = swap(packet, X_LAST)
    z_near = swap(packet, Z_NEAR)
    z_far = swap(packet, Z_FAR)
    z_last = swap(packet, Z_LAST)
    own_c = swap(packet, CORE)
    near_c = swap(x_near, CORE)
    far_c = swap(x_far, CORE)
    last_c = swap(x_last, CORE)

    g_far, g_near, g_own, f_far, f_near, f_own = rectangle(
        (packet, z_near, z_far, z_last, x_near, x_far, x_last, own_c, near_c, far_c, last_c),
    )
    far_back = swap(g_far, X_FAR)
    f_back = swap(f_far, Z_FAR)
    near_back = swap(g_near + far_back[32:], X_NEAR)
    f_last = swap(f_near + f_back[16:], Z_NEAR)
    both = g_own + far_back[:32] + near_back
    total = both[:16] + f_own + f_back[:16] + f_last + swap(both[16:], CORE)
    return total * mask


def solution(mesh):
    return jax.shard_map(
        local,
        mesh=mesh,
        in_specs=(
            P(("cplx", "frag"), None),
            P(("cplx", "frag"), None, None),
            P(("cplx", "frag")),
            P(("cplx", "frag"), None),
        ),
        out_specs=P(("cplx", "frag"), None),
        check_vma=False,
    )
```
